32 devices in a mesh: ctx: 8 (over z, y), wt: 4 (over x, core).
Axes of the slice: x: 2, y: 2, z: 4, core: 2. Of those that a mesh axis runs over, the one named last changes fastest.
Arguments:
- residual_in: bfloat16 [4, 3072, 768], P('wt', 'ctx')
- cotangent: bfloat16 [4, 3072, 768], P('wt', 'ctx'), may hold values from -6 to 6
- block_order: int32 [8], replicated, may hold values from 0 to 7, each once
- doc_starts: int32 [4, 3], P('wt'), may hold values from 0 to 3071, as said below
- gain_attn: bfloat16 [768], P('wt'), may hold values from 0.5 to 1.5
- w_query: bfloat16 [768, 768], P('wt'), may hold values from -0.21875 to 0.21875
- w_key: bfloat16 [768, 768], P('wt'), may hold values from -0.21875 to 0.21875
- w_value: bfloat16 [768, 768], P('wt'), may hold values from -0.21875 to 0.21875
- mix_logit: bfloat16 [12, 12], P('wt'), may hold values from -3.5 to 3.5
- mix_weight: bfloat16 [12, 12], P('wt'), may hold values from -1.75 to 1.75
- w_output: bfloat16 [768, 768], P('wt'), may hold values from -1.5 to 1.5
- gain_ffn: bfloat16 [768], P('wt'), may hold values from 0.5 to 1.5
- w_in: bfloat16 [768, 3072], P('wt'), may hold values from -0.21875 to 0.21875
- w_out: bfloat16 [3072, 768], P('wt'), may hold values from -0.109375 to 0.109375
Outputs:
- output: bfloat16 [4, 3072, 768], P('wt', 'ctx')
- input_grad: bfloat16 [4, 3072, 768], P('wt', 'ctx')
- rms_values: float32 [3], replicated
- grad_gain_attn: float32 [768], P('wt')
- grad_w_query: float32 [768, 768], P('wt')
- grad_w_key: float32 [768, 768], P('wt')
- grad_w_value: float32 [768, 768], P('wt')
- grad_mix_logit: float32 [12, 12], P('wt')
- grad_mix_weight: float32 [12, 12], P('wt')
- grad_w_output: float32 [768, 768], P('wt')
- grad_gain_ffn: float32 [768], P('wt')
- grad_w_in: float32 [768, 3072], P('wt')
- grad_w_out: float32 [3072, 768], P('wt')
The draws below stay inside these ranges and needn't reach their ends.
Inputs may be any that keep to these rules, and one draw needn't show every extreme that they name: `block_order`: each number once. `doc_starts`: each row rises: 0, then a start below 384, then one above 2688.
All inputs are finite; a program needn't handle non-finite values.
Results may differ from the reference program's by a relative error of at most 0.02.
Values may be sent and summed in bfloat16 or wider, within the bound.
No kernel may reach another device: no remote copies, remote signals or barrier semaphores. Data moves between devices by JAX's collectives and lax.ppermute only.
A program may use at most 256 MiB of HBM per device.

```python
import math
import jax
import jax.numpy as jnp
from jax import lax

D = 768
HEADS = 12
HSIZE = 64
FF = 3072
TOK_DEV = 384
SEQS = 4
SEQLEN = 3072
BLOCKS = 8


def draw_residual_in(key, part):
    key_base = jax.random.fold_in(jax.random.fold_in(key, 11), 0)
    row_index = jnp.arange(SEQLEN, dtype=jnp.float32)
    rising = (0.5 + row_index / SEQLEN)[None, :, None]
    values = jax.random.normal(key_base, (SEQS, SEQLEN, D), jnp.float32) * rising
    return values.astype(jnp.bfloat16)


def draw_doc_starts(key, part):
    key_first, key_second = jax.random.split(jax.random.fold_in(key, 23))
    first_start = jax.random.randint(key_first, (SEQS,), 1, TOK_DEV)
    second_start = jax.random.randint(key_second, (SEQS,), SEQLEN - TOK_DEV + 1, SEQLEN)
    return jnp.stack([jnp.zeros((SEQS,), jnp.int32), first_start, second_start], axis=1).astype(jnp.int32)


def shard_levels(stream_key, dims, shards, least, largest):
    level = 1.0
    for position, blocks in shards:
        steps = jax.random.uniform(jax.random.fold_in(jax.random.fold_in(stream_key, 6), position), (blocks,), jnp.float32, least / len(shards), largest / len(shards))
        level = level * jnp.repeat(jnp.exp(steps), dims[position] // blocks).reshape((-1,) + (1,) * (len(dims) - 1 - position))
    return level


def scatter_about(own_key, shape, scale, reach, cuts=(), kind=jnp.bfloat16):
    level = shard_levels(own_key, shape, cuts, -0.22, 0.18) if cuts else 1.0
    drawn = jax.random.normal(own_key, shape, jnp.float32) * scale * level
    return jnp.minimum(jnp.maximum(drawn, -reach), reach).astype(kind)


def setup_inputs(seed: int = 0) -> dict:
    streams_of = jax.random.split(jax.random.key(seed), 15)
    residual_in = draw_residual_in(jax.random.fold_in(streams_of[14], 71), 0)
    cotangent = scatter_about(streams_of[1], (SEQS, SEQLEN, D), 1.0, 6.0, ((0, 4), (1, 8)))
    block_order = jax.random.permutation(streams_of[2], BLOCKS).astype(jnp.int32)
    doc_starts = draw_doc_starts(jax.random.fold_in(streams_of[14], 71), 0)
    gain_attn = jnp.clip(1.0 + 0.1 * jax.random.normal(streams_of[4], (D,), jnp.float32), 0.5, 1.5).astype(jnp.bfloat16)
    w_query = scatter_about(streams_of[5], (D, D), D ** -0.5, 0.21875, ((0, 4),))
    w_key = scatter_about(streams_of[6], (D, D), D ** -0.5, 0.21875, ((0, 4),))
    w_value = scatter_about(streams_of[7], (D, D), D ** -0.5, 0.21875, ((0, 4),))
    mix_logit = scatter_about(streams_of[8], (HEADS, HEADS), (HEADS // 4) ** -0.5, 3.5, ((0, 4),))
    mix_weight = scatter_about(streams_of[9], (HEADS, HEADS), HEADS ** -0.5, 1.75, ((0, 4),))
    w_output = scatter_about(streams_of[10], (D, D), 16 ** -0.5, 1.5, ((0, 4),))
    gain_ffn = jnp.clip(1.0 + 0.1 * jax.random.normal(streams_of[11], (D,), jnp.float32), 0.5, 1.5).astype(jnp.bfloat16)
    w_in = scatter_about(streams_of[12], (D, FF), D ** -0.5, 0.21875, ((0, 4),))
    w_out = scatter_about(streams_of[13], (FF, D), FF ** -0.5, 0.109375, ((0, 4),))
    return {"residual_in": residual_in, "cotangent": cotangent, "block_order": block_order, "doc_starts": doc_starts, "gain_attn": gain_attn, "w_query": w_query, "w_key": w_key, "w_value": w_value, "mix_logit": mix_logit, "mix_weight": mix_weight, "w_output": w_output, "gain_ffn": gain_ffn, "w_in": w_in, "w_out": w_out}


NEG = -1e+30
EPS = 1e-06
HIGH = lax.Precision.HIGHEST

@jax.custom_vjp
def low(v):
    return lax.optimization_barrier(v.astype(jnp.bfloat16)).astype(jnp.float32)

@jax.custom_vjp
def low_back(v):
    return v

def low_keep(v):
    return (low(v), None)

def low_pass(kept, grad):
    return (grad,)

def back_keep(v):
    return (v, None)

def back_low(kept, grad):
    return (low(grad),)
low.defvjp(low_keep, low_pass)
low_back.defvjp(back_keep, back_low)

def matmul(left, right):
    return jnp.dot(left, right, precision=HIGH, preferred_element_type=jnp.float32)

def rms_norm(values, gain):
    return values * lax.rsqrt(lax.optimization_barrier(jnp.mean(values * values, axis=-1, keepdims=True)) + EPS) * gain

def attend(query_block, query_pos, query_doc, key_heads, value_heads, key_pos, key_doc, logit_mix, weight_mix):
    scores = low_back(jnp.einsum('qhd,khd->hqk', query_block, key_heads, precision=HIGH) * HSIZE ** (-0.5))
    logits = jnp.einsum('hqk,hg->gqk', scores, logit_mix, precision=HIGH)
    visible = (key_pos[None, :] <= query_pos[:, None]) & (key_doc[None, :] == query_doc[:, None])
    logits = jnp.where(visible[None], logits, NEG)
    row_top = lax.optimization_barrier(jnp.max(logits, axis=-1, keepdims=True))
    shifted = jnp.exp(logits - row_top)
    probability = shifted / lax.optimization_barrier(jnp.sum(shifted, axis=-1, keepdims=True))
    mixed_w = low(jnp.einsum('gqk,gh->hqk', probability, weight_mix, precision=HIGH))
    return jnp.einsum('hqk,khd->qhd', mixed_w, value_heads, precision=HIGH)

def one_sequence(sequence_item, positions, params):
    inputs, doc_ids = sequence_item
    gain_one, query_mat, key_mat, value_mat, logit_mix, weight_mix, output_mat, gain_two, inner_mat, outer_mat = params
    normed = low(rms_norm(inputs, gain_one))
    queries = low(low_back(matmul(normed, query_mat)))
    keys = low(low_back(matmul(normed, key_mat)))
    values = low(low_back(matmul(normed, value_mat)))
    block_rows = math.gcd(SEQLEN, 256)
    block_count = SEQLEN // block_rows
    key_heads = keys.reshape(SEQLEN, HEADS, HSIZE)
    value_heads = values.reshape(SEQLEN, HEADS, HSIZE)
    attend_saved = jax.checkpoint(attend)

    def one_block(piece):
        return attend_saved(piece[0], piece[1], piece[2], key_heads, value_heads, positions, doc_ids, logit_mix, weight_mix)
    attended = lax.map(one_block, (queries.reshape(block_count, block_rows, HEADS, HSIZE), positions.reshape(block_count, block_rows), doc_ids.reshape(block_count, block_rows)))
    attended = low(low_back(attended.reshape(SEQLEN, D)))
    branch = low_back(matmul(attended, output_mat))
    middle = inputs + branch
    normed_two = low(rms_norm(middle, gain_two))
    hidden = low_back(matmul(normed_two, inner_mat))
    active = low(jax.nn.gelu(hidden, approximate=True))
    feed = low_back(matmul(active, outer_mat))
    return (middle + feed, jnp.sum(branch * branch), jnp.sum(feed * feed))

def reference(residual_in, cotangent, block_order, doc_starts, gain_attn, w_query, w_key, w_value, mix_logit, mix_weight, w_output, gain_ffn, w_in, w_out):
    row_index = jnp.arange(SEQLEN, dtype=jnp.int32)
    positions = (block_order[row_index // TOK_DEV] * TOK_DEV + row_index % TOK_DEV).astype(jnp.int32)
    doc_ids = (positions[None, :] >= doc_starts[:, 1:2]).astype(jnp.int32) + (positions[None, :] >= doc_starts[:, 2:3]).astype(jnp.int32)
    weights_in = tuple((member.astype(jnp.float32) for member in (gain_attn, w_query, w_key, w_value, mix_logit, mix_weight, w_output, gain_ffn, w_in, w_out)))

    def layer(inputs, *params):
        outputs, attn_sq, ffn_sq = lax.map(lambda sequence_item: one_sequence(sequence_item, positions, params), (inputs, doc_ids))
        return (outputs, (jnp.sum(attn_sq), jnp.sum(ffn_sq)))
    outputs, pullback, sums = jax.vjp(layer, residual_in.astype(jnp.float32), *weights_in, has_aux=True)
    grads = pullback(cotangent.astype(jnp.float32))
    entries = float(SEQS * SEQLEN * D)
    rms_values = jnp.sqrt(jnp.stack([jnp.sum(outputs * outputs), sums[0], sums[1]]) / entries)
    return (outputs.astype(jnp.bfloat16), grads[0].astype(jnp.bfloat16), rms_values, grads[1], grads[2], grads[3], grads[4], grads[5], grads[6], grads[7], grads[8], grads[9], grads[10])
```

```python
import functools
import math

import jax
import jax.numpy as jnp
from jax import lax
from jax.experimental import pallas as pl
from jax.experimental.pallas import tpu as pltpu
from jax.sharding import PartitionSpec as P

NEG = -1e30
EPS = 1e-06
LOG2E = 1.4426950408889634
LN2 = 0.6931471805599453
F32 = jnp.float32
BF16 = jnp.bfloat16
NT = (((1,), (1,)), ((), ()))
VMEM_BYTES = 60 * 1024 * 1024


def dot(left, right):
    return jnp.dot(left, right, preferred_element_type=F32)


def dot_nt(left, right):
    return lax.dot_general(left, right, NT, preferred_element_type=F32)


def rms_norm(values, gain):
    return values * lax.rsqrt(jnp.mean(values * values, axis=-1, keepdims=True) + EPS) * gain


def gelu_tanh(values):
    return jax.nn.gelu(values, approximate=True)


def params(flops, moved, dims=1):
    return dict(
        compiler_params=pltpu.CompilerParams(
            dimension_semantics=("arbitrary",) * dims, vmem_limit_bytes=VMEM_BYTES
        ),
        cost_estimate=pl.CostEstimate(flops=flops, bytes_accessed=moved, transcendentals=0),
    )


HEAD = 5


def project_kernel(sc, x_ref, gain_ref, wk_ref, wv_ref, k_ref, v_ref, kt_ref, vt_ref, nt_ref):
    x = x_ref[0].astype(F32)
    normed = rms_norm(x, gain_ref[...]).astype(BF16)
    nt_ref[0] = normed.T
    k = dot(normed, wk_ref[...]).astype(BF16)
    k_ref[0] = k
    kt_ref[0] = k.T
    v = dot(normed, wv_ref[...]).astype(BF16)
    v_ref[0] = v
    vt_ref[0] = v.T


def project(scalars, x_rel, gain, wk, wv):
    count, rows, width = x_rel.shape
    place = lambda j, sc: (sc[HEAD + 2 * count + j], 0, 0)
    fixed = lambda j, sc: (0, 0)
    tall = jax.ShapeDtypeStruct((count, rows, width), BF16)
    wide = jax.ShapeDtypeStruct((count, width, rows), BF16)
    return pl.pallas_call(
        project_kernel,
        grid_spec=pltpu.PrefetchScalarGridSpec(
            num_scalar_prefetch=1,
            grid=(count,),
            in_specs=[
                pl.BlockSpec((1, rows, width), lambda j, sc: (j, 0, 0)),
                pl.BlockSpec((1, width), fixed),
                pl.BlockSpec((width, width), fixed),
                pl.BlockSpec((width, width), fixed),
            ],
            out_specs=[
                pl.BlockSpec((1, rows, width), place),
                pl.BlockSpec((1, rows, width), place),
                pl.BlockSpec((1, width, rows), place),
                pl.BlockSpec((1, width, rows), place),
                pl.BlockSpec((1, width, rows), place),
            ],
        ),
        out_shape=[tall, tall, wide, wide, wide],
        **params(4 * count * rows * width * width, 12 * count * rows * width),
    )(scalars, x_rel, gain, wk, wv)


def bias_of(sc, key_place, query_place, rows, half):
    key_pos = key_place + lax.broadcasted_iota(jnp.int32, (rows, 2 * half), 0)
    lane = lax.broadcasted_iota(jnp.int32, (rows, 2 * half), 1)
    query_pos = query_place + jnp.where(lane >= half, lane - half, lane)
    key_doc = (key_pos >= sc[3]).astype(jnp.int32) + (key_pos >= sc[4]).astype(jnp.int32)
    query_doc = (query_pos >= sc[3]).astype(jnp.int32) + (query_pos >= sc[4]).astype(jnp.int32)
    return jnp.where((key_pos <= query_pos) & (key_doc == query_doc), 0.0, NEG)


def fold(target, lead, source, mix_ref, heads, half):
    values = source.astype(F32)
    for g in range(heads):
        piece = (values * mix_ref[g : g + 1, :]).astype(BF16)
        if lead is None:
            target[g * half : (g + 1) * half, :] = piece
        else:
            target[lead, g * half : (g + 1) * half, :] = piece


def attend_kernel(
    count, heads, group, sc, q_ref, k_ref, vt_ref, mix_ref, back_ref,
    att_ref, t_ref, lse_ref, folded, total, top, norm, bias_s,
):
    half, width = q_ref.shape[1], q_ref.shape[2]
    rows = k_ref.shape[1]
    step = pl.program_id(0)
    own = sc[0]
    first_half = step <= own
    tile = jnp.where(first_half, step, step - own - 1)
    query_place = jnp.where(first_half, own * rows, (count - 1 - own) * rows + half)

    @pl.when((step == 0) | (step == own + 1))
    def start():
        fold(folded, None, q_ref[0], mix_ref, heads, half)
        top[...] = jnp.full(top.shape, NEG, F32)
        norm[...] = jnp.zeros(norm.shape, F32)
        total[...] = jnp.zeros(total.shape, F32)

    bias_s[...] = bias_of(sc, tile * rows, query_place, rows, half)
    span = group * half
    for c in range(heads // group):
        cols = slice(c * span, (c + 1) * span)
        logits = dot_nt(k_ref[0], folded[cols, :])
        logits = logits + jnp.concatenate([bias_s[...]] * (group // 2), axis=1)
        before = top[:, cols]
        after = jnp.maximum(before, jnp.max(logits, axis=0, keepdims=True))
        shrink = jnp.exp2(before - after)
        weights = jnp.exp2(logits - after)
        top[:, cols] = after
        norm[:, cols] = norm[:, cols] * shrink + jnp.sum(weights, axis=0, keepdims=True)
        total[:, cols] = total[:, cols] * shrink + dot(vt_ref[0], weights.astype(BF16))

    @pl.when((step == own) | (step == count))
    def finish():
        lse_ref[0] = top[...] + jnp.log2(norm[...])
        inverse = 1.0 / norm[...]
        attended = jnp.zeros((width, half), F32)
        for p in range(heads // 2):
            cols = slice(2 * p * half, (2 * p + 2) * half)
            scaled = total[:, cols] * inverse[:, cols]
            t_ref[0, :, cols] = scaled.astype(BF16)
            attended += back_ref[:, 2 * p : 2 * p + 1] * scaled[:, :half]
            attended += back_ref[:, 2 * p + 1 : 2 * p + 2] * scaled[:, half:]
        att_ref[0] = attended.T.astype(BF16)


def attend(scalars, q, k, vt, mix_rows, weight_cols, heads):
    count, rows, width = k.shape
    half = q.shape[1]
    span = heads * half
    which = lambda s, sc: (jnp.where(s <= sc[0], 0, 1), 0, 0)
    tile = lambda s, sc: (sc[HEAD + jnp.where(s <= sc[0], s, s - sc[0] - 1)], 0, 0)
    fixed = lambda s, sc: (0, 0)
    group = math.gcd(heads, 4)
    return pl.pallas_call(
        functools.partial(attend_kernel, count, heads, group),
        grid_spec=pltpu.PrefetchScalarGridSpec(
            num_scalar_prefetch=1,
            grid=(count + 1,),
            in_specs=[
                pl.BlockSpec((1, half, width), which),
                pl.BlockSpec((1, rows, width), tile),
                pl.BlockSpec((1, width, rows), tile),
                pl.BlockSpec((heads, width), fixed),
                pl.BlockSpec((width, heads), fixed),
            ],
            out_specs=[
                pl.BlockSpec((1, half, width), which),
                pl.BlockSpec((1, width, span), which),
                pl.BlockSpec((1, 1, span), which),
            ],
            scratch_shapes=[
                pltpu.VMEM((span, width), BF16),
                pltpu.VMEM((width, span), F32),
                pltpu.VMEM((1, span), F32),
                pltpu.VMEM((1, span), F32),
                pltpu.VMEM((rows, 2 * half), F32),
            ],
        ),
        out_shape=[
            jax.ShapeDtypeStruct((2, half, width), BF16),
            jax.ShapeDtypeStruct((2, width, span), BF16),
            jax.ShapeDtypeStruct((2, 1, span), F32),
        ],
        **params(4 * (count + 1) * rows * span * width, 6 * count * rows * width),
    )(scalars, q, k, vt, mix_rows, weight_cols)


def pair_rows(left, right, heads):
    product = left * right
    size = product.shape[0] // heads
    return jnp.concatenate(
        [
            jnp.sum(product[h * size : (h + 1) * size, :], axis=0, keepdims=True)
            for h in range(heads)
        ],
        axis=0,
    )


def delta_kernel(heads, grad_ref, t_ref, spread_ref, r_ref, delta_ref):
    half = grad_ref.shape[1]
    grad_t = grad_ref[0].astype(F32).T
    twice = jnp.concatenate([grad_t, grad_t], axis=1)
    for p in range(heads // 2):
        cols = slice(2 * p * half, (2 * p + 2) * half)
        found = pair_rows(twice, t_ref[0, :, cols].astype(F32), heads)
        r_ref[0, :, cols] = found
        delta_ref[0, :, cols] = jnp.sum(found * spread_ref[:, cols], axis=0, keepdims=True)


def deltas(grad_att, t, spread, heads):
    _, half, width = grad_att.shape
    span = heads * half
    return pl.pallas_call(
        functools.partial(delta_kernel, heads),
        grid=(2,),
        in_specs=[
            pl.BlockSpec((1, half, width), lambda s: (s, 0, 0)),
            pl.BlockSpec((1, width, span), lambda s: (s, 0, 0)),
            pl.BlockSpec((heads, span), lambda s: (0, 0)),
        ],
        out_specs=[
            pl.BlockSpec((1, heads, span), lambda s: (s, 0, 0)),
            pl.BlockSpec((1, 1, span), lambda s: (s, 0, 0)),
        ],
        out_shape=[
            jax.ShapeDtypeStruct((2, heads, span), F32),
            jax.ShapeDtypeStruct((2, 1, span), F32),
        ],
        **params(4 * width * span, 4 * width * span),
    )(grad_att, t, spread)


def back_place(step, own, count):
    low = jnp.minimum(own, count - 1 - own)
    both = step < 2 * (low + 1)
    tile = jnp.where(both, step // 2, step - low - 1)
    part = jnp.where(both, step % 2, jnp.where(own > count - 1 - own, 0, 1))
    return low, both, tile, part


def back_kernel(
    count, heads, group, scale, sc, q_ref, ga_ref, k_ref, v_ref, kt_ref, lse_ref, delta_ref,
    mix_ref, weight_ref, mixc_ref, dk_ref, dv_ref, dq_ref, r_ref,
    fq, fa, total, dk_s, dv_s, bias_s,
):
    half, width = q_ref.shape[1], q_ref.shape[2]
    rows = k_ref.shape[1]
    step = pl.program_id(0)
    own = sc[0]
    low, both, tile, part = back_place(step, own, count)
    query_place = jnp.where(part == 0, own * rows, (count - 1 - own) * rows + half)

    @pl.when(step == 0)
    def start():
        for n in range(2):
            fold(fq, n, q_ref[n], mix_ref, heads, half)
            fold(fa, n, ga_ref[n], weight_ref, heads, half)
        total[...] = jnp.zeros(total.shape, F32)

    @pl.when(jnp.logical_not(both) | (part == 0))
    def clear():
        dk_s[...] = jnp.zeros(dk_s.shape, F32)
        dv_s[...] = jnp.zeros(dv_s.shape, F32)

    bias_s[...] = bias_of(sc, tile * rows, query_place, rows, half)
    span = group * half
    for c in range(heads // group):
        cols = slice(c * span, (c + 1) * span)
        fq_c, fa_c = fq[part, cols, :], fa[part, cols, :]
        logits = dot_nt(k_ref[0], fq_c)
        grad_prob = dot_nt(v_ref[0], fa_c)
        logits = logits + jnp.concatenate([bias_s[...]] * (group // 2), axis=1)
        prob = jnp.exp2(logits - lse_ref[part, :, cols])
        grad_logits = (prob * (grad_prob - delta_ref[part, :, cols])).astype(BF16)
        dv_s[...] += dot(prob.astype(BF16), fa_c)
        dk_s[...] += dot(grad_logits, fq_c)
        total[part, :, cols] += dot(kt_ref[0], grad_logits)

    @pl.when(jnp.logical_not(both) | (part == 1))
    def leave():
        dk_ref[0] = (dk_s[...] * LN2).astype(BF16)
        dv_ref[0] = dv_s[...].astype(BF16)

    @pl.when(step == count)
    def finish():
        for n in range(2):
            q_t = q_ref[n].astype(F32).T
            twice = jnp.concatenate([q_t, q_t], axis=1)
            grad = jnp.zeros((width, half), F32)
            for p in range(heads // 2):
                cols = slice(2 * p * half, (2 * p + 2) * half)
                piece = total[n, :, cols]
                r_ref[n, :, cols] = pair_rows(twice, piece, heads)
                grad += mixc_ref[:, 2 * p : 2 * p + 1] * piece[:, :half]
                grad += mixc_ref[:, 2 * p + 1 : 2 * p + 2] * piece[:, half:]
            dq_ref[n] = (grad.T * scale).astype(BF16)


def back(scalars, q, grad_att, k, v, kt, lse, delta, mix_rows, weight_rows, mix_cols, heads, scale):
    count, rows, width = k.shape
    half = q.shape[1]
    span = heads * half
    tile = lambda s, sc: (sc[HEAD + back_place(s, sc[0], count)[2]], 0, 0)
    whole = lambda s, sc: (0, 0, 0)
    fixed = lambda s, sc: (0, 0)
    group = math.gcd(heads, 4)
    once = pl.Buffered(1)
    return pl.pallas_call(
        functools.partial(back_kernel, count, heads, group, scale),
        grid_spec=pltpu.PrefetchScalarGridSpec(
            num_scalar_prefetch=1,
            grid=(count + 1,),
            in_specs=[
                pl.BlockSpec((2, half, width), whole, pipeline_mode=once),
                pl.BlockSpec((2, half, width), whole, pipeline_mode=once),
                pl.BlockSpec((1, rows, width), tile),
                pl.BlockSpec((1, rows, width), tile),
                pl.BlockSpec((1, width, rows), tile),
                pl.BlockSpec((2, 1, span), whole, pipeline_mode=once),
                pl.BlockSpec((2, 1, span), whole, pipeline_mode=once),
                pl.BlockSpec((heads, width), fixed),
                pl.BlockSpec((heads, width), fixed),
                pl.BlockSpec((width, heads), fixed),
            ],
            out_specs=[
                pl.BlockSpec((1, rows, width), tile),
                pl.BlockSpec((1, rows, width), tile),
                pl.BlockSpec((2, half, width), whole),
                pl.BlockSpec((2, heads, span), whole),
            ],
            scratch_shapes=[
                pltpu.VMEM((2, span, width), BF16),
                pltpu.VMEM((2, span, width), BF16),
                pltpu.VMEM((2, width, span), F32),
                pltpu.VMEM((rows, width), F32),
                pltpu.VMEM((rows, width), F32),
                pltpu.VMEM((rows, 2 * half), F32),
            ],
        ),
        out_shape=[
            jax.ShapeDtypeStruct((count, rows, width), BF16),
            jax.ShapeDtypeStruct((count, rows, width), BF16),
            jax.ShapeDtypeStruct((2, half, width), BF16),
            jax.ShapeDtypeStruct((2, heads, span), F32),
        ],
        **params(10 * (count + 1) * rows * span * width, 10 * count * rows * width),
    )(scalars, q, grad_att, k, v, kt, lse, delta, mix_rows, weight_rows, mix_cols)


def input_kernel(
    count, sc, dk_ref, dv_ref, x_ref, nt_ref, wk_ref, wv_ref, gain_ref, gq_ref, gm_ref,
    part_ref, dwk_ref, dwv_ref, gain_out, grad_s,
):
    rows = x_ref.shape[1]
    half = rows // 2
    j = pl.program_id(0)
    device = sc[HEAD + 2 * count + j]
    own = sc[0]
    valid = sc[HEAD + count + device] <= jnp.maximum(own, count - 1 - own)

    @pl.when(j == 0)
    def start():
        dwk_ref[...] = jnp.zeros(dwk_ref.shape, F32)
        dwv_ref[...] = jnp.zeros(dwv_ref.shape, F32)
        gain_out[...] = jnp.zeros(gain_out.shape, F32)

    @pl.when(valid)
    def seen():
        dk, dv = dk_ref[0], dv_ref[0]
        grad_s[...] = dot_nt(dk, wk_ref[...]) + dot_nt(dv, wv_ref[...])
        dwk_ref[...] += dot(nt_ref[0], dk)
        dwv_ref[...] += dot(nt_ref[0], dv)

    @pl.when(jnp.logical_not(valid))
    def unseen():
        grad_s[...] = jnp.zeros(grad_s.shape, F32)

    @pl.when(device == sc[1])
    def at_own():
        grad_s[:half, :] += gq_ref[0]

    @pl.when(device == sc[2])
    def at_partner():
        grad_s[half:, :] += gq_ref[1]

    x = x_ref[0].astype(F32)
    grad = grad_s[...]
    inverse = lax.rsqrt(jnp.mean(x * x, axis=-1, keepdims=True) + EPS)
    bare = x * inverse
    gained = grad * gain_ref[...]
    gain_out[...] += jnp.sum(grad * bare, axis=0, keepdims=True)
    back_x = inverse * (gained - bare * jnp.mean(gained * bare, axis=-1, keepdims=True))
    part_ref[0] = back_x.astype(BF16)

    @pl.when(device == sc[1])
    def own_rows():
        part_ref[0, :half, :] = (back_x[:half] + gm_ref[0]).astype(BF16)

    @pl.when(device == sc[2])
    def partner_rows():
        part_ref[0, half:, :] = (back_x[half:] + gm_ref[1]).astype(BF16)


def input_parts(scalars, dk, dv, x_rel, nt, wk, wv, gain, gq, gm):
    count, rows, width = x_rel.shape
    place = lambda j, sc: (sc[HEAD + 2 * count + j], 0, 0)
    fixed = lambda j, sc: (0, 0)
    whole = lambda j, sc: (0, 0, 0)
    return pl.pallas_call(
        functools.partial(input_kernel, count),
        grid_spec=pltpu.PrefetchScalarGridSpec(
            num_scalar_prefetch=1,
            grid=(count,),
            in_specs=[
                pl.BlockSpec((1, rows, width), place),
                pl.BlockSpec((1, rows, width), place),
                pl.BlockSpec((1, rows, width), lambda j, sc: (j, 0, 0)),
                pl.BlockSpec((1, width, rows), place),
                pl.BlockSpec((width, width), fixed),
                pl.BlockSpec((width, width), fixed),
                pl.BlockSpec((1, width), fixed),
                pl.BlockSpec((2, rows // 2, width), whole),
                pl.BlockSpec((2, rows // 2, width), whole),
            ],
            out_specs=[
                pl.BlockSpec((1, rows, width), place),
                pl.BlockSpec((width, width), fixed),
                pl.BlockSpec((width, width), fixed),
                pl.BlockSpec((1, width), fixed),
            ],
            scratch_shapes=[pltpu.VMEM((rows, width), F32)],
        ),
        out_shape=[
            jax.ShapeDtypeStruct((count, rows, width), BF16),
            jax.ShapeDtypeStruct((width, width), F32),
            jax.ShapeDtypeStruct((width, width), F32),
            jax.ShapeDtypeStruct((1, width), F32),
        ],
        **params(8 * count * rows * width * width, 10 * count * rows * width),
    )(scalars, dk, dv, x_rel, nt, wk, wv, gain, gq, gm)


def swaps(size, distance):
    return [(i, i ^ distance) for i in range(size)]


def gather_wt(value):
    size = lax.axis_size("wt")
    me = lax.axis_index("wt")
    pieces = [value]
    distance = size // 2
    while distance:
        pieces = pieces + [lax.ppermute(p, "wt", swaps(size, distance)) for p in pieces]
        distance //= 2
    bits = size.bit_length() - 1
    place = [int(format(n, "0%db" % bits)[::-1], 2) for n in range(size)]
    stacked = jnp.stack([pieces[place.index(n)] for n in range(size)])
    return jnp.concatenate(
        [lax.dynamic_index_in_dim(stacked, me ^ r, 0, keepdims=False) for r in range(size)], axis=0
    )


def ring(count):
    return [(i, (i + 2) % count) for i in range(count)]


def gather_ctx(value):
    count = lax.axis_size("ctx")
    pieces = []
    moving = value
    for k in range(count // 2):
        if k:
            moving = lax.ppermute(moving, "ctx", ring(count))
        pieces += [moving, lax.ppermute(moving, "ctx", swaps(count, 1))]
    return pieces


def relative_devices(count, me):
    outer, inner = me // 2, me % 2
    places = []
    for k in range(count // 2):
        base = 2 * jnp.mod(outer - k, count // 2)
        places += [base + inner, base + 1 - inner]
    return jnp.stack(places)


def scatter_ctx(parts):
    count = lax.axis_size("ctx")
    me = lax.axis_index("ctx")
    outer, inner = me // 2, me % 2
    total = None
    for k in range(1, count // 2 + 1):
        base = 2 * jnp.mod(outer - k, count // 2)
        kept = lax.dynamic_index_in_dim(parts, base + inner, 0, keepdims=False)
        sent = lax.dynamic_index_in_dim(parts, base + 1 - inner, 0, keepdims=False)
        found = kept.astype(F32) + lax.ppermute(sent, "ctx", swaps(count, 1)).astype(F32)
        if total is not None:
            found = found + lax.ppermute(total.astype(BF16), "ctx", ring(count)).astype(F32)
        total = found
    return total


def shards(
    residual_in,
    cotangent,
    block_order,
    doc_starts,
    gain_attn,
    w_query,
    w_key,
    w_value,
    mix_logit,
    mix_weight,
    w_output,
    gain_ffn,
    w_in,
    w_out,
):
    rows, width = residual_in.shape[1:]
    half = rows // 2
    heads = mix_logit.shape[1]
    size = width // heads
    scale = size ** (-0.5)
    count = lax.axis_size("ctx")
    me = lax.axis_index("ctx")
    wt_count = lax.axis_size("wt")
    starts = doc_starts[0]

    small = jnp.concatenate(
        [
            gain_attn.reshape(1, -1),
            gain_ffn.reshape(1, -1),
            mix_logit.reshape(1, -1),
            mix_weight.reshape(1, -1),
        ],
        axis=1,
    )
    small = lax.all_gather(small, "wt", axis=0, tiled=True).astype(F32)
    n_gain = gain_attn.shape[0]
    n_mix = mix_logit.size
    gain_one = small[:, :n_gain].reshape(1, width)
    gain_two = small[:, n_gain : 2 * n_gain].reshape(1, width)
    logit_mix = small[:, 2 * n_gain : 2 * n_gain + n_mix].reshape(heads, heads)
    weight_mix = small[:, 2 * n_gain + n_mix :].reshape(heads, heads)

    x_own = residual_in[0]
    x_rel = jnp.stack(gather_ctx(x_own))
    qkv_mat = gather_wt(jnp.concatenate([w_query, w_key, w_value], axis=1))
    query_mat, key_mat, value_mat = (qkv_mat[:, n * width : (n + 1) * width] for n in range(3))
    output_mat = lax.all_gather(w_output, "wt", axis=0, tiled=True)
    inner_mat = lax.all_gather(w_in, "wt", axis=0, tiled=True)
    outer_mat = lax.all_gather(w_out, "wt", axis=0, tiled=True)

    order = block_order.astype(jnp.int32)
    devices = jnp.arange(count, dtype=jnp.int32)
    by_block = jnp.sum(jnp.where(order[None, :] == devices[:, None], devices[None, :], 0), axis=1)
    own = order[me]
    partner = by_block[count - 1 - own]
    relative = relative_devices(count, me).astype(jnp.int32)
    partner_place = jnp.sum(jnp.where(relative == partner, devices, 0))
    scalars = jnp.concatenate(
        [jnp.stack([own, me.astype(jnp.int32), partner, starts[1], starts[2]]), by_block, order, relative]
    ).astype(jnp.int32)

    mix_by_g = jnp.repeat(logit_mix.T, size, axis=1)
    weight_by_g = jnp.repeat(weight_mix, size, axis=1)
    mix_rows = mix_by_g * (scale * LOG2E)
    spread = jnp.repeat(weight_mix.T, half, axis=1)

    k, v, kt, vt, nt = project(scalars, x_rel, gain_one, key_mat, value_mat)
    x_two = lax.dynamic_index_in_dim(x_rel, partner_place, 0, keepdims=False)[half:]
    x_low = jnp.concatenate([x_own[:half], x_two], axis=0)
    inputs = x_low.astype(F32)
    normed_low = rms_norm(inputs, gain_one).astype(BF16)
    q = dot(normed_low, query_mat).astype(BF16).reshape(2, half, width)

    def exchange(second):
        every = lax.all_gather(second, "ctx", axis=0)
        return lax.dynamic_index_in_dim(every, partner, 0, keepdims=False)

    dy_low = jnp.concatenate([cotangent[0, :half], exchange(cotangent[0, half:])], axis=0)

    attended, t, lse = attend(scalars, q, k, vt, mix_rows, weight_by_g.T, heads)
    attended_low = attended.reshape(rows, width)

    branch = dot(attended_low, output_mat)
    middle = inputs + branch
    normed_two, norm_two_back = jax.vjp(rms_norm, middle, gain_two)
    normed_two_low = normed_two.astype(BF16)
    hidden = dot(normed_two_low, inner_mat)
    active, gelu_back = jax.vjp(gelu_tanh, hidden)
    active_low = active.astype(BF16)
    feed = dot(active_low, outer_mat)
    output = middle + feed
    squares = jnp.stack([jnp.sum(output * output), jnp.sum(branch * branch), jnp.sum(feed * feed)])
    out_low = output.astype(BF16)
    output_own = jnp.concatenate([out_low[:half], exchange(out_low[half:])], axis=0)

    grad_outer = jnp.einsum("ti,to->io", active_low, dy_low, preferred_element_type=F32)
    grad_active = dot_nt(dy_low, outer_mat)
    grad_hidden_low = gelu_back(grad_active)[0].astype(BF16)
    grad_inner = jnp.einsum("ti,tf->if", normed_two_low, grad_hidden_low, preferred_element_type=F32)
    grad_normed_two = dot_nt(grad_hidden_low, inner_mat)
    grad_mid_norm, grad_gain_two = norm_two_back(grad_normed_two)
    grad_middle = dy_low.astype(F32) + grad_mid_norm
    grad_branch_low = grad_middle.astype(BF16)
    grad_output_mat = jnp.einsum(
        "ti,to->io", attended_low, grad_branch_low, preferred_element_type=F32
    )
    grad_att = dot_nt(grad_branch_low, output_mat).astype(BF16).reshape(2, half, width)

    def reduce(values):
        share = lax.psum_scatter(values.astype(BF16), "wt", scatter_dimension=0, tiled=True)
        return lax.psum(share, "ctx")

    grad_outer_own = reduce(grad_outer)
    grad_inner_own = reduce(grad_inner)
    grad_output_own = reduce(grad_output_mat)

    r_weight, delta = deltas(grad_att, t, spread, heads)
    dk, dv, dq, r_logit = back(
        scalars, q, grad_att, k, v, kt, lse, delta, mix_rows, weight_by_g, mix_by_g.T, heads, scale
    )
    dq_low = dq.reshape(rows, width)
    gq = dot_nt(dq_low, query_mat).reshape(2, half, width)
    grad_query_mat = jnp.einsum("ti,to->io", normed_low, dq_low, preferred_element_type=F32)
    parts, grad_key_mat, grad_value_mat, grad_gain_one = input_parts(
        scalars, dk, dv, x_rel, nt, key_mat, value_mat, gain_one, gq,
        grad_middle.reshape(2, half, width),
    )
    input_grad = scatter_ctx(parts).astype(BF16)
    qkv_own = reduce(jnp.concatenate([grad_query_mat, grad_key_mat, grad_value_mat], axis=1))

    by_heads = lambda found: jnp.sum(found.reshape(2, heads, heads, half), axis=(0, 3))
    grad_mix_weight = by_heads(r_weight).T
    grad_mix_logit = by_heads(r_logit) * scale
    shared = jnp.concatenate(
        [
            squares,
            grad_gain_one.reshape(-1),
            grad_gain_two.reshape(-1),
            grad_mix_logit.reshape(-1),
            grad_mix_weight.reshape(-1),
        ]
    )
    shared = lax.psum(shared, ("ctx", "wt"))
    entries = float(rows * width) * (count * wt_count)
    rms_values = jnp.sqrt(shared[:3] / entries)
    wt_me = lax.axis_index("wt")

    def own_rows(first, full):
        piece = shared[first : first + math.prod(full)].reshape(full)
        per = full[0] // wt_count
        return lax.dynamic_slice_in_dim(piece, wt_me * per, per, 0)

    grad_gain_one_own = own_rows(3, (width,))
    grad_gain_two_own = own_rows(3 + width, (width,))
    grad_mix_logit_own = own_rows(3 + 2 * width, (heads, heads))
    grad_mix_weight_own = own_rows(3 + 2 * width + heads * heads, (heads, heads))

    return (
        output_own[None],
        input_grad[None],
        rms_values,
        grad_gain_one_own,
        qkv_own[:, :width].astype(F32),
        qkv_own[:, width : 2 * width].astype(F32),
        qkv_own[:, 2 * width :].astype(F32),
        grad_mix_logit_own,
        grad_mix_weight_own,
        grad_output_own.astype(F32),
        grad_gain_two_own,
        grad_inner_own.astype(F32),
        grad_outer_own.astype(F32),
    )


def solution(mesh):
    tokens = P("wt", "ctx", None)
    matrix = P("wt", None)
    vector = P("wt")
    return jax.shard_map(
        shards,
        mesh=mesh,
        in_specs=(tokens, tokens, P(), matrix, vector)
        + (matrix,) * 6
        + (vector, matrix, matrix),
        out_specs=(tokens, tokens, P(), vector) + (matrix,) * 6 + (vector, matrix, matrix),
        check_vma=False,
    )
```

```python
import functools
import math

import jax
import jax.numpy as jnp
from jax import lax
from jax.experimental import pallas as pl
from jax.experimental.pallas import tpu as pltpu
from jax.sharding import PartitionSpec as P

NEG = -1e30
EPS = 1e-06
LOG2E = 1.4426950408889634
LN2 = 0.6931471805599453
F32 = jnp.float32
BF16 = jnp.bfloat16
NT = (((1,), (1,)), ((), ()))
VMEM_BYTES = 60 * 1024 * 1024


def dot(left, right):
    return jnp.dot(left, right, preferred_element_type=F32)


def dot_nt(left, right):
    return lax.dot_general(left, right, NT, preferred_element_type=F32)


def rms_norm(values, gain):
    return values * lax.rsqrt(jnp.mean(values * values, axis=-1, keepdims=True) + EPS) * gain


def gelu_tanh(values):
    return jax.nn.gelu(values, approximate=True)


def params(flops, moved, dims=1):
    return dict(
        compiler_params=pltpu.CompilerParams(
            dimension_semantics=("arbitrary",) * dims, vmem_limit_bytes=VMEM_BYTES
        ),
        cost_estimate=pl.CostEstimate(flops=flops, bytes_accessed=moved, transcendentals=0),
    )


HEAD = 6


def assemble(me, target, pieces, per, cols=slice(None)):
    for n, piece in enumerate(pieces):
        rows = pl.ds(pl.multiple_of((me ^ n) * per, per), per)
        target[rows, :] = piece[:per, cols]


def project_kernel(batch, shares, sc, *refs):
    pieces, (gain_ref, *weights) = refs[:batch], refs[batch : batch + 1 + max(1, len(shares))]
    outs = refs[-(7 if shares else 6) :]
    k_ref, v_ref, kt_ref, vt_ref, nt_ref, x_out = outs[:6]
    width = x_out.shape[2]
    mat = outs[6] if shares else weights[0]
    if shares:

        @pl.when(pl.program_id(0) == 0)
        def start():
            assemble(sc[5], mat, weights, width // len(weights))

    def one(x_ref):
        x_low = x_ref[...]
        x_out[0] = x_low
        normed = rms_norm(x_low.astype(F32), gain_ref[...]).astype(BF16)
        nt_ref[0] = normed.T
        k = dot(normed, mat[:, :width]).astype(BF16)
        k_ref[0] = k
        kt_ref[0] = k.T
        v = dot(normed, mat[:, width:]).astype(BF16)
        v_ref[0] = v
        vt_ref[0] = v.T

    for n in range(batch):
        pl.when(pl.program_id(0) == n)(functools.partial(one, pieces[n]))


def project(scalars, count, first, pieces, gain, mat, before):
    batch = len(pieces)
    rows, width = pieces[0].shape
    place = lambda j, sc: (sc[HEAD + 2 * count + first + j], 0, 0)
    fixed = lambda j, sc: (0, 0)
    tall = jax.ShapeDtypeStruct((count, rows, width), BF16)
    wide = jax.ShapeDtypeStruct((count, width, rows), BF16)
    once = pl.Buffered(1)
    before = () if before is None else tuple(before)
    shares = tuple(mat) if isinstance(mat, (list, tuple)) else ()
    weights = shares or (mat,)
    out_specs = [
        pl.BlockSpec((1, rows, width), place),
        pl.BlockSpec((1, rows, width), place),
        pl.BlockSpec((1, width, rows), place),
        pl.BlockSpec((1, width, rows), place),
        pl.BlockSpec((1, width, rows), place),
        pl.BlockSpec((1, rows, width), place),
    ]
    out_shape = [tall, tall, wide, wide, wide, tall]
    if shares:
        out_specs.append(pl.BlockSpec((width, 2 * width), fixed, pipeline_mode=once))
        out_shape.append(jax.ShapeDtypeStruct((width, 2 * width), BF16))
    return pl.pallas_call(
        functools.partial(project_kernel, batch, shares),
        grid_spec=pltpu.PrefetchScalarGridSpec(
            num_scalar_prefetch=1,
            grid=(batch,),
            in_specs=[pl.BlockSpec((rows, width), fixed, pipeline_mode=once)] * batch
            + [pl.BlockSpec((1, width), fixed)]
            + [pl.BlockSpec(w.shape, fixed, pipeline_mode=once) for w in weights]
            + [pl.BlockSpec(memory_space=pl.ANY)] * len(before),
            out_specs=out_specs,
        ),
        out_shape=out_shape,
        input_output_aliases={batch + 2 + len(weights) + n: n for n in range(len(before))},
        **params(4 * batch * rows * width * width, 14 * batch * rows * width),
    )(scalars, *pieces, gain, *weights, *before)


def query_kernel(sc, x_ref, gain_ref, *refs):
    shares, (q_ref, x_out, mat) = refs[:-3], refs[-3:]

    @pl.when(pl.program_id(0) == 0)
    def start():
        assemble(sc[5], mat, shares, mat.shape[0] // len(shares), slice(0, mat.shape[1]))

    x_out[0] = x_ref[0]
    normed = rms_norm(x_ref[0].astype(F32), gain_ref[...]).astype(BF16)
    q_ref[0] = dot(normed, mat[...]).astype(BF16)


def queries(scalars, xg, gain, shares):
    count, rows, width = xg.shape
    half = rows // 2
    fixed = lambda n, sc: (0, 0)
    once = pl.Buffered(1)
    part = jax.ShapeDtypeStruct((2, half, width), BF16)
    return pl.pallas_call(
        query_kernel,
        grid_spec=pltpu.PrefetchScalarGridSpec(
            num_scalar_prefetch=1,
            grid=(2,),
            in_specs=[
                pl.BlockSpec((1, half, width), lambda n, sc: (sc[1 + n], n, 0)),
                pl.BlockSpec((1, width), fixed),
            ]
            + [pl.BlockSpec(w.shape, fixed, pipeline_mode=once) for w in shares],
            out_specs=[
                pl.BlockSpec((1, half, width), lambda n, sc: (n, 0, 0)),
                pl.BlockSpec((1, half, width), lambda n, sc: (n, 0, 0)),
                pl.BlockSpec((width, width), fixed, pipeline_mode=once),
            ],
        ),
        out_shape=[part, part, jax.ShapeDtypeStruct((width, width), BF16)],
        **params(2 * rows * width * width, 4 * width * width),
    )(scalars, xg, gain, *shares)


def doc_of(sc, place):
    return (place >= sc[3]).astype(jnp.int32) + (place >= sc[4]).astype(jnp.int32)


def set_bias(bias_s, sc, key_place, query_place):
    rows, twice = bias_s.shape
    half = twice // 2
    key_end, query_end = key_place + rows - 1, query_place + half - 1
    clear = (
        (key_end <= query_place)
        & (doc_of(sc, key_place) == doc_of(sc, query_end))
        & (doc_of(sc, key_end) == doc_of(sc, query_place))
        & (doc_of(sc, key_end) == doc_of(sc, query_end))
    )

    @pl.when(clear)
    def seen():
        bias_s[...] = jnp.zeros(bias_s.shape, F32)

    @pl.when(jnp.logical_not(clear))
    def mixed():
        key_pos = key_place + lax.broadcasted_iota(jnp.int32, (rows, 1), 0)
        lane = lax.broadcasted_iota(jnp.int32, (1, twice), 1)
        query_pos = query_place + jnp.where(lane >= half, lane - half, lane)
        visible = (key_pos <= query_pos) & (doc_of(sc, key_pos) == doc_of(sc, query_pos))
        bias_s[...] = jnp.where(visible, 0.0, NEG)


def fold(target, lead, source, mix_ref, heads, half):
    values = source.astype(F32)
    for g in range(heads):
        piece = (values * mix_ref[g : g + 1, :]).astype(BF16)
        if lead is None:
            target[g * half : (g + 1) * half, :] = piece
        else:
            target[lead, g * half : (g + 1) * half, :] = piece


def attend_kernel(
    count, heads, group, sc, q_ref, k_ref, vt_ref, mix_ref, spread_ref,
    att_ref, t_ref, lse_ref, folded, total, top, norm, bias_s, mixed_s, ahead,
):
    half, width = q_ref.shape[1], q_ref.shape[2]
    rows = k_ref.shape[1]
    step = pl.program_id(0)
    own = sc[0]
    first_half = step <= own
    tile = jnp.where(first_half, step, step - own - 1)
    query_place = jnp.where(first_half, own * rows, (count - 1 - own) * rows + half)

    @pl.when((step == 0) | (step == own + 1))
    def start():
        fold(folded, None, q_ref[0], mix_ref, heads, half)
        top[...] = jnp.full(top.shape, NEG, F32)
        norm[...] = jnp.zeros(norm.shape, F32)
        total[...] = jnp.zeros(total.shape, F32)

    set_bias(bias_s, sc, tile * rows, query_place)
    span = group * half
    chunks = [slice(c * span, (c + 1) * span) for c in range(heads // group)]
    ahead[0] = dot_nt(k_ref[0], folded[chunks[0], :])
    for c, cols in enumerate(chunks):
        if c + 1 < len(chunks):
            ahead[(c + 1) % 2] = dot_nt(k_ref[0], folded[chunks[c + 1], :])
        logits = ahead[c % 2] + jnp.concatenate([bias_s[...]] * (group // 2), axis=1)
        before = top[:, cols]
        after = jnp.maximum(before, jnp.max(logits, axis=0, keepdims=True))
        shrink = jnp.exp2(before - after)
        weights = jnp.exp2(logits - after)
        top[:, cols] = after
        norm[:, cols] = norm[:, cols] * shrink + jnp.sum(weights, axis=0, keepdims=True)
        total[:, cols] = total[:, cols] * shrink + dot(vt_ref[0], weights.astype(BF16))

    @pl.when((step == own) | (step == count))
    def finish():
        lse_ref[0] = top[...] + jnp.log2(norm[...])
        norm[...] = 1.0 / norm[...]
        mix_all(
            total, spread_ref, mixed_s, half,
            lambda h, rows, cols: scale_out(total, norm, t_ref, rows, cols),
        )
        att_ref[0] = (mixed_s[:, :half] + mixed_s[:, half:]).T.astype(BF16)


def scale_out(total, norm, t_ref, rows, cols):
    scaled = total[rows, cols] * norm[:, cols]
    t_ref[0, rows, cols] = scaled.astype(BF16)
    return scaled


def mix_all(total, spread_ref, mixed_s, half, find):
    heads = spread_ref.shape[0]
    size = mixed_s.shape[0] // heads
    for h in range(heads):
        rows = slice(h * size, (h + 1) * size)
        found = jnp.zeros((size, 2 * half), F32)
        for p in range(spread_ref.shape[1] // (2 * half)):
            cols = slice(2 * p * half, (2 * p + 2) * half)
            found += find(h, rows, cols) * spread_ref[h : h + 1, cols]
        mixed_s[rows, :] = found


def attend(scalars, q, k, vt, mix_rows, spread, heads):
    count, rows, width = k.shape
    half = q.shape[1]
    span = heads * half
    which = lambda s, sc: (jnp.where(s <= sc[0], 0, 1), 0, 0)
    tile = lambda s, sc: (sc[HEAD + jnp.where(s <= sc[0], s, s - sc[0] - 1)], 0, 0)
    fixed = lambda s, sc: (0, 0)
    group = math.gcd(heads, 4)
    return pl.pallas_call(
        functools.partial(attend_kernel, count, heads, group),
        grid_spec=pltpu.PrefetchScalarGridSpec(
            num_scalar_prefetch=1,
            grid=(count + 1,),
            in_specs=[
                pl.BlockSpec((1, half, width), which),
                pl.BlockSpec((1, rows, width), tile),
                pl.BlockSpec((1, width, rows), tile),
                pl.BlockSpec((heads, width), fixed),
                pl.BlockSpec((heads, span), fixed),
            ],
            out_specs=[
                pl.BlockSpec((1, half, width), which),
                pl.BlockSpec((1, width, span), which),
                pl.BlockSpec((1, 1, span), which),
            ],
            scratch_shapes=[
                pltpu.VMEM((span, width), BF16),
                pltpu.VMEM((width, span), F32),
                pltpu.VMEM((1, span), F32),
                pltpu.VMEM((1, span), F32),
                pltpu.VMEM((rows, 2 * half), F32),
                pltpu.VMEM((width, 2 * half), F32),
                pltpu.VMEM((2, rows, group * half), F32),
            ],
        ),
        out_shape=[
            jax.ShapeDtypeStruct((2, half, width), BF16),
            jax.ShapeDtypeStruct((2, width, span), BF16),
            jax.ShapeDtypeStruct((2, 1, span), F32),
        ],
        **params(4 * (count + 1) * rows * span * width, 6 * count * rows * width),
    )(scalars, q, k, vt, mix_rows, spread)


def pair_rows(left, right, heads):
    product = left * right
    size = product.shape[0] // heads
    return jnp.concatenate(
        [
            jnp.sum(product[h * size : (h + 1) * size, :], axis=0, keepdims=True)
            for h in range(heads)
        ],
        axis=0,
    )


def lanes_of(found, first, half, lanes=128):
    place = lax.broadcasted_iota(jnp.int32, (found.shape[0], lanes), 1)
    total = jnp.zeros((found.shape[0], lanes), F32)
    for n in range(found.shape[1] // half):
        piece = jnp.sum(found[:, n * half : (n + 1) * half], axis=1, keepdims=True)
        total = jnp.where(place == first + n, piece, total)
    return total


def delta_kernel(heads, grad_ref, t_ref, spread_ref, r_ref, delta_ref):
    half = grad_ref.shape[1]
    grad_t = grad_ref[0].astype(F32).T
    twice = jnp.concatenate([grad_t, grad_t], axis=1)
    sums = jnp.zeros(r_ref.shape, F32)
    for p in range(heads // 2):
        cols = slice(2 * p * half, (2 * p + 2) * half)
        found = pair_rows(twice, t_ref[0, :, cols].astype(F32), heads)
        sums += lanes_of(found, 2 * p, half)
        delta_ref[0, :, cols] = jnp.sum(found * spread_ref[:, cols], axis=0, keepdims=True)

    @pl.when(pl.program_id(0) == 0)
    def first():
        r_ref[...] = sums

    @pl.when(pl.program_id(0) == 1)
    def second():
        r_ref[...] += sums


def deltas(grad_att, t, spread, heads):
    _, half, width = grad_att.shape
    span = heads * half
    return pl.pallas_call(
        functools.partial(delta_kernel, heads),
        grid=(2,),
        in_specs=[
            pl.BlockSpec((1, half, width), lambda s: (s, 0, 0)),
            pl.BlockSpec((1, width, span), lambda s: (s, 0, 0)),
            pl.BlockSpec((heads, span), lambda s: (0, 0)),
        ],
        out_specs=[
            pl.BlockSpec((heads, 128), lambda s: (0, 0)),
            pl.BlockSpec((1, 1, span), lambda s: (s, 0, 0)),
        ],
        out_shape=[
            jax.ShapeDtypeStruct((heads, 128), F32),
            jax.ShapeDtypeStruct((2, 1, span), F32),
        ],
        **params(4 * width * span, 4 * width * span),
    )(grad_att, t, spread)


def back_place(step, own, count):
    low = jnp.minimum(own, count - 1 - own)
    both = step < 2 * (low + 1)
    tile = jnp.where(both, step // 2, step - low - 1)
    part = jnp.where(both, step % 2, jnp.where(own > count - 1 - own, 0, 1))
    return low, both, tile, part


def back_kernel(
    count, heads, base, group, scale, sc, q_ref, ga_ref, k_ref, v_ref, kt_ref, lse_ref, delta_ref,
    mix_ref, weight_ref, spread_ref, dk_ref, dv_ref, dq_ref, r_ref,
    fq, fa, total, dk_s, dv_s, bias_s, mixed_s, twice_s, rows_s, ahead_l, ahead_p,
):
    half, width = q_ref.shape[1], q_ref.shape[2]
    rows = k_ref.shape[1]
    step = pl.program_id(0)
    own = sc[0]
    low, both, tile, part = back_place(step, own, count)
    query_place = jnp.where(part == 0, own * rows, (count - 1 - own) * rows + half)

    @pl.when(step == 0)
    def start():
        for n in range(2):
            q = q_ref[n].astype(F32)
            ga = ga_ref[n].astype(F32)
            for g in range(group):
                cols = slice(g * half, (g + 1) * half)
                fq[n, cols, :] = (q * mix_ref[base + g : base + g + 1, :]).astype(BF16)
                fa[n, cols, :] = (ga * weight_ref[base + g : base + g + 1, :]).astype(BF16)
        total[...] = jnp.zeros(total.shape, F32)

    @pl.when(jnp.logical_not(both) | (part == 0))
    def clear():
        dk_s[...] = jnp.zeros(dk_s.shape, F32)
        dv_s[...] = jnp.zeros(dv_s.shape, F32)

    set_bias(bias_s, sc, tile * rows, query_place)
    chunk = math.gcd(group, 4)
    chunks = [slice(c * chunk * half, (c + 1) * chunk * half) for c in range(group // chunk)]

    def look(c):
        ahead_l[c % 2] = dot_nt(k_ref[0], fq[part, chunks[c], :])
        ahead_p[c % 2] = dot_nt(v_ref[0], fa[part, chunks[c], :])

    look(0)
    for c, cols in enumerate(chunks):
        if c + 1 < len(chunks):
            look(c + 1)
        logits = ahead_l[c % 2] + jnp.concatenate([bias_s[...]] * (chunk // 2), axis=1)
        prob = jnp.exp2(logits - lse_ref[part, :, cols])
        grad_logits = (prob * (ahead_p[c % 2] - delta_ref[part, :, cols])).astype(BF16)
        dv_s[...] += dot(prob.astype(BF16), fa[part, cols, :])
        dk_s[...] += dot(grad_logits, fq[part, cols, :])
        total[part, :, cols] += dot(kt_ref[0], grad_logits)

    @pl.when(jnp.logical_not(both) | (part == 1))
    def leave():
        dk_ref[0] = (dk_s[...] * LN2).astype(BF16)
        dv_ref[0] = dv_s[...].astype(BF16)

    @pl.when(step == count)
    def finish():
        sums = jnp.zeros(r_ref.shape, F32)
        size = width // heads
        for n in range(2):
            q_t = q_ref[n].astype(F32).T
            twice_s[...] = jnp.concatenate([q_t, q_t], axis=1)

            def find(h, rows, cols):
                piece = total[n, rows, cols]
                rows_s[h : h + 1, cols] = jnp.sum(piece * twice_s[rows, :], axis=0, keepdims=True)
                return piece

            mix_all(total, spread_ref, mixed_s, half, find)
            sums += lanes_of(rows_s[...], 0, half)
            dq_ref[n] = ((mixed_s[:, :half] + mixed_s[:, half:]).T * scale).astype(BF16)
        r_ref[...] = sums * scale


def back(
    scalars, base, group, q, grad_att, k, v, kt, lse, delta, mix_rows, weight_rows, spread, heads, scale
):
    count, rows, width = k.shape
    half = q.shape[1]
    span = group * half
    tile = lambda s, sc: (sc[HEAD + back_place(s, sc[0], count)[2]], 0, 0)
    whole = lambda s, sc: (0, 0, 0)
    cut = lambda s, sc: (0, 0, base // group)
    fixed = lambda s, sc: (0, 0)
    once = pl.Buffered(1)
    return pl.pallas_call(
        functools.partial(back_kernel, count, heads, base, group, scale),
        grid_spec=pltpu.PrefetchScalarGridSpec(
            num_scalar_prefetch=1,
            grid=(count + 1,),
            in_specs=[
                pl.BlockSpec((2, half, width), whole, pipeline_mode=once),
                pl.BlockSpec((2, half, width), whole, pipeline_mode=once),
                pl.BlockSpec((1, rows, width), tile),
                pl.BlockSpec((1, rows, width), tile),
                pl.BlockSpec((1, width, rows), tile),
                pl.BlockSpec((2, 1, span), cut, pipeline_mode=once),
                pl.BlockSpec((2, 1, span), cut, pipeline_mode=once),
                pl.BlockSpec((heads, width), fixed),
                pl.BlockSpec((heads, width), fixed),
                pl.BlockSpec((heads, span), fixed),
            ],
            out_specs=[
                pl.BlockSpec((1, rows, width), tile),
                pl.BlockSpec((1, rows, width), tile),
                pl.BlockSpec((2, half, width), whole),
                pl.BlockSpec((heads, 128), fixed),
            ],
            scratch_shapes=[
                pltpu.VMEM((2, span, width), BF16),
                pltpu.VMEM((2, span, width), BF16),
                pltpu.VMEM((2, width, span), F32),
                pltpu.VMEM((rows, width), F32),
                pltpu.VMEM((rows, width), F32),
                pltpu.VMEM((rows, 2 * half), F32),
                pltpu.VMEM((width, 2 * half), F32),
                pltpu.VMEM((width, 2 * half), F32),
                pltpu.VMEM((heads, span), F32),
                pltpu.VMEM((2, rows, math.gcd(group, 4) * half), F32),
                pltpu.VMEM((2, rows, math.gcd(group, 4) * half), F32),
            ],
        ),
        out_shape=[
            jax.ShapeDtypeStruct((count, rows, width), BF16),
            jax.ShapeDtypeStruct((count, rows, width), BF16),
            jax.ShapeDtypeStruct((2, half, width), BF16),
            jax.ShapeDtypeStruct((heads, 128), F32),
        ],
        **params(10 * (count + 1) * rows * span * width, 10 * count * rows * width),
    )(scalars, q, grad_att, k, v, kt, lse, delta, mix_rows, weight_rows, spread)


def put(keep_ref, send_ref, place, rows, value):
    @pl.when(place % 2 == 0)
    def kept():
        keep_ref[place // 2, rows, :] = value

    @pl.when(place % 2 == 1)
    def sent():
        send_ref[place // 2, rows, :] = value


def norm_parts(x):
    inverse = lax.rsqrt(jnp.mean(x * x, axis=-1, keepdims=True) + EPS)
    return inverse, x * inverse


def norm_back(inverse, bare, grad, gain):
    gained = grad * gain
    return inverse * (gained - bare * jnp.mean(gained * bare, axis=-1, keepdims=True))


def ffn_kernel(wt_count, sc, att_ref, x_ref, dy_ref, gain_ref, *refs):
    n = wt_count
    halves = (len(refs) - 16) // n
    wo_shares, win_shares = refs[:n], [refs[(i + 1) * n : (i + 2) * n] for i in range(halves)]
    (
        wout_ref,
        out_ref, gm_ref, gatt_ref, keep_ref, send_ref, gain_out, sq_ref,
        middle_s, low_s, low_t, feed_s, grad_s, wo_ref, win_ref,
    ) = refs[(halves + 1) * n :]
    j = pl.program_id(0)
    last = pl.num_programs(0) - 1
    me = sc[5]
    width = x_ref.shape[1]
    per = width // wt_count
    for i in range(halves):
        for side in range(2):
            pl.when(j == 2 * i + side)(
                functools.partial(
                    assemble, me, win_ref, win_shares[i], per, slice(side * width, (side + 1) * width)
                )
            )

    @pl.when(j == 0)
    def start():
        assemble(me, wo_ref, wo_shares, per, slice(width, 2 * width))
        branch = dot(att_ref[...], wo_ref[...])
        middle = x_ref[...].astype(F32) + branch
        middle_s[...] = middle
        _, bare = norm_parts(middle)
        low = (bare * gain_ref[...]).astype(BF16)
        low_s[...] = low
        low_t[...] = low.T
        feed_s[...] = jnp.zeros(feed_s.shape, F32)
        grad_s[...] = jnp.zeros(grad_s.shape, F32)
        sq_ref[...] = jnp.zeros(sq_ref.shape, F32)
        sq_ref[1:2, :] = jnp.broadcast_to(jnp.sum(branch * branch).reshape(1, 1), (1, 128))

    dy = dy_ref[...]
    hidden = dot(low_s[...], win_ref[...])
    grad_active = dot_nt(dy, wout_ref[...])
    square = hidden * hidden
    inner = jnp.tanh(hidden * (0.7978845608028654 + 0.7978845608028654 * 0.044715 * square))
    half_one = 0.5 + 0.5 * inner
    active = (hidden * half_one).astype(BF16)
    slope = half_one + (0.5 * hidden) * (1.0 - inner * inner) * (
        0.7978845608028654 + 3.0 * 0.7978845608028654 * 0.044715 * square
    )
    grad_hidden = (grad_active * slope).astype(BF16)
    feed_s[...] += dot(active, wout_ref[...])
    grad_s[...] += dot_nt(grad_hidden, win_ref[...])
    grad_out = dot(active.T, dy).astype(BF16)
    grad_in = dot(low_t[...], grad_hidden).astype(BF16)
    put(keep_ref, send_ref, j ^ me, slice(0, width), grad_out)
    for t in range(wt_count):
        rows = pl.ds(pl.multiple_of(width + j * per, per), per)
        put(keep_ref, send_ref, t ^ me, rows, grad_in[t * per : (t + 1) * per, :])

    @pl.when(j == last)
    def finish():
        middle = middle_s[...]
        feed = feed_s[...]
        output = middle + feed
        out_ref[...] = output.astype(BF16)
        sq_ref[0:1, :] = jnp.broadcast_to(jnp.sum(output * output).reshape(1, 1), (1, 128))
        sq_ref[2:3, :] = jnp.broadcast_to(jnp.sum(feed * feed).reshape(1, 1), (1, 128))
        inverse, bare = norm_parts(middle)
        grad = grad_s[...]
        gain_out[...] = jnp.sum(grad * bare, axis=0, keepdims=True)
        grad_middle = dy.astype(F32) + norm_back(inverse, bare, grad, gain_ref[...])
        gm_ref[...] = grad_middle
        low = grad_middle.astype(BF16)
        gatt_ref[...] = dot_nt(low, wo_ref[...]).astype(BF16)
        grad_o = dot(att_ref[...].T, low).astype(BF16)
        for t in range(wt_count):
            put(
                keep_ref, send_ref, t ^ me,
                slice(keep_ref.shape[1] - per, keep_ref.shape[1]),
                grad_o[t * per : (t + 1) * per, :],
            )


def ffn(scalars, wt_count, sq_rows, att, x, dy, gain, wo, wins, wout):
    rows, width = x.shape
    chunks = 2 * len(wins)
    per = width // wt_count
    total = width + per * chunks + per
    fixed = lambda j, sc: (0, 0)
    whole = lambda j, sc: (0, 0, 0)
    once = pl.Buffered(1)
    kernel = functools.partial(ffn_kernel, wt_count)
    shares = [*wo, *(share for win in wins for share in win)]
    return pl.pallas_call(
        kernel,
        grid_spec=pltpu.PrefetchScalarGridSpec(
            num_scalar_prefetch=1,
            grid=(chunks,),
            in_specs=[
                pl.BlockSpec((rows, width), fixed, pipeline_mode=once),
                pl.BlockSpec((rows, width), fixed, pipeline_mode=once),
                pl.BlockSpec((rows, width), fixed, pipeline_mode=once),
                pl.BlockSpec((1, width), fixed),
            ]
            + [pl.BlockSpec(w.shape, fixed, pipeline_mode=once) for w in shares]
            + [pl.BlockSpec((width, width), lambda j, sc: (j, 0))],
            out_specs=[
                pl.BlockSpec((rows, width), fixed),
                pl.BlockSpec((rows, width), fixed),
                pl.BlockSpec((rows, width), fixed),
                pl.BlockSpec((wt_count // 2, total, width), whole),
                pl.BlockSpec((wt_count // 2, total, width), whole),
                pl.BlockSpec((1, width), fixed),
                pl.BlockSpec((sq_rows, 128), fixed),
            ],
            scratch_shapes=[
                pltpu.VMEM((rows, width), F32),
                pltpu.VMEM((rows, width), BF16),
                pltpu.VMEM((width, rows), BF16),
                pltpu.VMEM((rows, width), F32),
                pltpu.VMEM((rows, width), F32),
                pltpu.VMEM((width, width), BF16),
                pltpu.VMEM((width, width), BF16),
            ],
        ),
        out_shape=[
            jax.ShapeDtypeStruct((rows, width), BF16),
            jax.ShapeDtypeStruct((rows, width), F32),
            jax.ShapeDtypeStruct((rows, width), BF16),
            jax.ShapeDtypeStruct((wt_count // 2, total, width), BF16),
            jax.ShapeDtypeStruct((wt_count // 2, total, width), BF16),
            jax.ShapeDtypeStruct((1, width), F32),
            jax.ShapeDtypeStruct((sq_rows, 128), F32),
        ],
        **params(10 * chunks * rows * width * width + 6 * rows * width * width, 24 * width * width),
    )(scalars, att, x, dy, gain, *shares, wout)


TAIL_ROWS = 16


def seen_by(sc, count, device):
    return sc[HEAD + count + device] <= jnp.maximum(sc[0], count - 1 - sc[0])


def weight_kernel(
    count, wt_count, sc, dk_ref, dv_ref, dq_ref, nt_ref, rl_ref, rw_ref, gain_two_ref, sq_ref,
    keep_ref, send_ref, dwq, dwk, dwv,
):
    width, rows = nt_ref.shape[1:]
    half = rows // 2
    device = pl.program_id(0)
    me_wt = sc[5]

    @pl.when(device == 0)
    def start():
        dwq[...] = jnp.zeros(dwq.shape, F32)
        dwk[...] = jnp.zeros(dwk.shape, F32)
        dwv[...] = jnp.zeros(dwv.shape, F32)

    @pl.when(seen_by(sc, count, device))
    def seen():
        dwk[...] += dot(nt_ref[0], dk_ref[0])
        dwv[...] += dot(nt_ref[0], dv_ref[0])

    def queries(n):
        empty = jnp.zeros((half, width), BF16)
        both = [dq_ref[n], empty] if n == 0 else [empty, dq_ref[n]]
        dwq[...] += dot(nt_ref[0], jnp.concatenate(both, axis=0))

    pl.when(device == sc[1])(functools.partial(queries, 0))
    pl.when(device == sc[2])(functools.partial(queries, 1))

    @pl.when(device == count - 1)
    def finish():
        per = width // wt_count

        def pad(value, lanes):
            empty = jnp.zeros((value.shape[0], lanes - value.shape[1]), F32)
            return jnp.concatenate([value, empty], axis=1)

        heads = rw_ref.shape[0]
        each = heads // wt_count
        square = jnp.concatenate([rw_ref[...], jnp.zeros((128 - heads, 128), F32)], axis=0).T
        below = keep_ref.shape[1] - 3 * per - TAIL_ROWS
        assert TAIL_ROWS >= 4 + 2 * each

        def tail(t):
            rows = [
                pad(gain_two_ref[:, t * per : (t + 1) * per], width),
                pad(sq_ref[0:3, :], width),
                pad(rl_ref[t * each : (t + 1) * each, :], width),
                pad(square[t * each : (t + 1) * each, :], width),
                jnp.zeros((TAIL_ROWS - 4 - 2 * each + below, width), F32),
            ]
            return jnp.concatenate(rows, axis=0).astype(BF16)

        for t in range(wt_count):
            cut = slice(t * per, (t + 1) * per)
            for n, total in enumerate((dwq, dwk, dwv)):
                put(keep_ref, send_ref, t ^ me_wt, slice(n * per, (n + 1) * per), total[cut, :].astype(BF16))
            put(keep_ref, send_ref, t ^ me_wt, slice(3 * per, keep_ref.shape[1]), tail(t))


def weight_grads(scalars, wt_count, total, dk, dv, dq, nt, rl, rw, gain_two, sq):
    count, rows, width = dk.shape
    place = lambda j, sc: (j, 0, 0)
    fixed = lambda j, sc: (0, 0)
    whole = lambda j, sc: (0, 0, 0)
    once = pl.Buffered(1)
    share = jax.ShapeDtypeStruct((wt_count // 2, total, width), BF16)
    return pl.pallas_call(
        functools.partial(weight_kernel, count, wt_count),
        grid_spec=pltpu.PrefetchScalarGridSpec(
            num_scalar_prefetch=1,
            grid=(count,),
            in_specs=[
                pl.BlockSpec((1, rows, width), place),
                pl.BlockSpec((1, rows, width), place),
                pl.BlockSpec((2, rows // 2, width), whole, pipeline_mode=once),
                pl.BlockSpec((1, width, rows), place),
                pl.BlockSpec(rl.shape, fixed),
                pl.BlockSpec(rw.shape, fixed),
                pl.BlockSpec((1, width), fixed),
                pl.BlockSpec(sq.shape, fixed),
            ],
            out_specs=[
                pl.BlockSpec((wt_count // 2, total, width), whole),
                pl.BlockSpec((wt_count // 2, total, width), whole),
            ],
            scratch_shapes=[pltpu.VMEM((width, width), F32)] * 3,
        ),
        out_shape=[share, share],
        **params(4 * count * rows * width * width, 10 * count * rows * width),
    )(scalars, dk, dv, dq, nt, rl, rw, gain_two, sq)


def token_kernel(
    count, first, sc, dk_ref, dv_ref, dq_ref, x_ref, wq_ref, mat_ref, gain_ref, gm_ref, part_ref
):
    rows, width = x_ref.shape[1:]
    half = rows // 2
    device = sc[HEAD + 2 * count + first + pl.program_id(0)]
    valid = seen_by(sc, count, device)

    @pl.when(valid)
    def seen():
        grad = dot_nt(dk_ref[0], mat_ref[:, :width]) + dot_nt(dv_ref[0], mat_ref[:, width:])
        inverse, bare = norm_parts(x_ref[0].astype(F32))
        part_ref[0] = norm_back(inverse, bare, grad, gain_ref[...]).astype(BF16)

    @pl.when(jnp.logical_not(valid))
    def unseen():
        part_ref[0] = jnp.zeros(part_ref.shape[1:], BF16)

    def queries(n):
        mine = slice(n * half, (n + 1) * half)
        grad = dot_nt(dq_ref[n], wq_ref[...])
        inverse, bare = norm_parts(x_ref[0, mine, :].astype(F32))
        found = norm_back(inverse, bare, grad, gain_ref[...]) + gm_ref[n]
        part_ref[0, mine, :] = (part_ref[0, mine, :].astype(F32) + found).astype(BF16)

    pl.when(device == sc[1])(functools.partial(queries, 0))
    pl.when(device == sc[2])(functools.partial(queries, 1))


def token_parts(scalars, first, batch, dk, dv, dq, xg, wq, mat, gain, gm):
    count, rows, width = xg.shape
    place = lambda j, sc: (sc[HEAD + 2 * count + first + j], 0, 0)
    fixed = lambda j, sc: (0, 0)
    whole = lambda j, sc: (0, 0, 0)
    once = pl.Buffered(1)
    return pl.pallas_call(
        functools.partial(token_kernel, count, first),
        grid_spec=pltpu.PrefetchScalarGridSpec(
            num_scalar_prefetch=1,
            grid=(batch,),
            in_specs=[
                pl.BlockSpec((1, rows, width), place),
                pl.BlockSpec((1, rows, width), place),
                pl.BlockSpec((2, rows // 2, width), whole, pipeline_mode=once),
                pl.BlockSpec((1, rows, width), place),
                pl.BlockSpec((width, width), fixed, pipeline_mode=once),
                pl.BlockSpec((width, 2 * width), fixed, pipeline_mode=once),
                pl.BlockSpec((1, width), fixed),
                pl.BlockSpec((2, rows // 2, width), whole, pipeline_mode=once),
            ],
            out_specs=pl.BlockSpec((1, rows, width), lambda j, sc: (j, 0, 0)),
        ),
        out_shape=jax.ShapeDtypeStruct((batch, rows, width), BF16),
        **params(4 * batch * rows * width * width, 8 * batch * rows * width),
    )(scalars, dk, dv, dq, xg, wq, mat, gain, gm)


def finish_kernel(entries, heads, sc, *refs):
    count = len(refs) - 12
    pieces, (wq_ref, wk_ref, wv_ref), outs, whole = refs[:count], refs[count : count + 3], refs[-9:-1], refs[-1]
    dq_ref, dk_ref, dv_ref, gain_ref, two_ref, logit_ref, weight_ref, rms_ref = outs
    per = pieces[0].shape[0]
    for n, piece in enumerate(pieces):
        whole[pl.ds(pl.multiple_of(sc[n] * per, 8), per), :] = piece[...].astype(F32)
    rows = wq_ref.shape[0]
    gain = jnp.zeros((rows, 1), F32)
    for n, (out, w) in enumerate(((dq_ref, wq_ref), (dk_ref, wk_ref), (dv_ref, wv_ref))):
        found = whole[n * rows : (n + 1) * rows, :]
        out[...] = found
        gain += jnp.sum(found * w[...].astype(F32), axis=1, keepdims=True)
    gain_ref[...] = gain
    tail = whole[3 * rows : 3 * rows + TAIL_ROWS, :]
    each = logit_ref.shape[0]
    two_ref[...] = tail[0:1, :rows]
    rms_ref[...] = jnp.sqrt(tail[1:4, 0:1] * (1.0 / entries))
    logit_ref[...] = tail[4 : 4 + each, :heads]
    weight_ref[...] = tail[4 + each : 4 + 2 * each, :heads]


def finish_grads(places, pieces, wq, wk, wv, entries, heads, each):
    count = len(pieces)
    rows, width = wq.shape
    ins = [*pieces, wq, wk, wv]
    shapes = [(rows, width)] * 3 + [(rows, 1), (1, rows), (each, heads), (each, heads), (3, 1)]
    fixed = lambda i, sc: (0, 0)
    return pl.pallas_call(
        functools.partial(finish_kernel, entries, heads),
        grid_spec=pltpu.PrefetchScalarGridSpec(
            num_scalar_prefetch=1,
            grid=(1,),
            in_specs=[pl.BlockSpec(v.shape, fixed) for v in ins],
            out_specs=[pl.BlockSpec(v, fixed) for v in shapes],
            scratch_shapes=[pltpu.VMEM((count * pieces[0].shape[0], width), F32)],
        ),
        out_shape=[jax.ShapeDtypeStruct(v, F32) for v in shapes],
        **params(0, 12 * rows * width),
    )(places, *ins)


def unpack_kernel(sum_ref, out_ref, in_ref, o_ref):
    rows, width = out_ref.shape
    per = o_ref.shape[0]
    out_ref[...] = sum_ref[:rows, :].astype(F32)
    chunks = in_ref.shape[1] // width
    for n in range(chunks):
        in_ref[:, n * width : (n + 1) * width] = sum_ref[rows + n * per : rows + (n + 1) * per, :].astype(F32)
    o_ref[...] = sum_ref[rows + chunks * per :, :].astype(F32)


def unpack(total, shapes):
    return pl.pallas_call(
        unpack_kernel,
        out_shape=[jax.ShapeDtypeStruct(shape, F32) for shape in shapes],
        **params(0, 6 * total.size, 0),
    )(total)


def swaps(size, distance):
    return [(i, i ^ distance) for i in range(size)]


def ring_order(count):
    return [2 * p if p < count // 2 else 2 * (count - 1 - p) + 1 for p in range(count)]


def ring(count, step):
    order = ring_order(count)
    return [(order[p], order[(p + step) % count]) for p in range(count)]


def ring_places(count, me, offsets):
    place = jnp.where((me & 1) == 0, me >> 1, count - 1 - (me >> 1))
    p = (place + jnp.array(offsets, jnp.int32)) & (count - 1)
    return jnp.where(p < count // 2, 2 * p, 2 * (count - 1 - p) + 1)


def ring_both(up, down):
    count = lax.axis_size("ctx")
    return lax.ppermute(up, "ctx", ring(count, 1)), lax.ppermute(down, "ctx", ring(count, -1))


def tie(*values):
    return lax.optimization_barrier(values)


def gather_all(value, stages, work):
    count = lax.axis_size("ctx")
    size = lax.axis_size("wt")
    half = value.shape[0] // 2
    rounds = [[(0, value)]]
    up = down = value
    shares, crossed = [], []
    for k in range(1, count // 2 + 1):
        last = k == count // 2
        up, down = ring_both(up[:half], down[half:]) if last else ring_both(up, down)
        tied = []
        if 2 <= k <= len(stages) + 1:
            tied.append(lax.ppermute(stages[k - 2], "wt", swaps(size, 1)))
            tied.append(lax.ppermute(crossed[k - 2], "wt", swaps(size, 1)))
        if k <= len(stages):
            crossed.append(lax.ppermute(stages[k - 1], "wt", swaps(size, 2)))
            if not last:
                tied.append(crossed.pop())
        done = work(rounds, shares) if k >= 3 else []
        up, down, done, *tied = tie(up, down, done, *tied)
        if k >= 3:
            work(rounds, shares, done)
        if k <= len(stages) and not last:
            crossed.append(tied.pop())
        if tied:
            shares.append([stages[k - 2], tied[0], crossed[k - 2], tied[1]])
        rounds.append([(count // 2, jnp.concatenate([up, down], axis=0))] if last else [(-k, up), (k, down)])
    return rounds, shares, crossed


def add(*values):
    return sum(v.astype(F32) for v in values).astype(BF16)


def far_start(far):
    half = far.shape[0] // 2
    up, down = ring_both(far[:half], far[half:])
    return up, down


def far_end(up, down):
    empty = jnp.zeros(up.shape, BF16)
    return jnp.concatenate([up, empty], axis=0), jnp.concatenate([empty, down], axis=0)


class Turning:
    def __init__(self, blocks, me):
        self.count = blocks.shape[0]
        self.blocks, self.me = blocks, me
        self.step, self.last = 0, self.count // 2
        self.pieces = []
        self.done = False

    def at(self, offset):
        place = ring_places(self.count, self.me, [offset])[0]
        return lax.dynamic_index_in_dim(self.blocks, place, 0, keepdims=False)

    def start(self):
        step, last = self.step, self.last
        if step == 0:
            return far_start(self.at(last))
        if step < last:
            return ring_both(
                add(self.up, self.at(last - step)), add(self.down, self.at(step - last))
            )
        if step < 2 * last - 1:
            return ring_both(self.up, self.down)
        half = self.up.shape[0] // 2
        return ring_both(self.up[:half], self.down[half:])

    def finish(self, up, down):
        step, last = self.step, self.last
        if step == 0:
            up, down = far_end(up, down)
        elif step == last - 1:
            up = down = add(up, down, self.at(0))
            self.pieces.append((0, up))
        elif last <= step < 2 * last - 1:
            k = step - last + 1
            self.pieces += [(-k, up), (k, down)]
        elif step == 2 * last - 1:
            self.pieces.append((last, jnp.concatenate([up, down], axis=0)))
            self.done = True
        self.up, self.down = up, down
        self.step += 1

    def ordered(self):
        found = {offset % self.count: piece for offset, piece in self.pieces}
        return [found[n] for n in range(self.count)]


def shards(
    residual_in,
    cotangent,
    block_order,
    doc_starts,
    gain_attn,
    w_query,
    w_key,
    w_value,
    mix_logit,
    mix_weight,
    w_output,
    gain_ffn,
    w_in,
    w_out,
):
    rows, width = residual_in.shape[1:]
    half = rows // 2
    heads = mix_logit.shape[1]
    size = width // heads
    scale = size ** (-0.5)
    count = lax.axis_size("ctx")
    me = lax.axis_index("ctx").astype(jnp.int32)
    wt_count = lax.axis_size("wt")
    starts = doc_starts[0]

    per = gain_attn.shape[0]
    across = lambda v, n: jnp.pad(v, ((0, n - v.shape[0]), (0, 2 * width - v.shape[1])))
    gains = jnp.concatenate([gain_attn, gain_ffn])[None, :]
    mixes_at = 8
    small = jnp.concatenate(
        [across(gains, mixes_at), across(jnp.concatenate([mix_logit, mix_weight], axis=1), mixes_at)], axis=0
    )
    kv_own = jnp.concatenate([jnp.concatenate([w_key, w_value], axis=1), small], axis=0)
    x_own = residual_in[0]
    stages = [kv_own, jnp.concatenate([w_query, w_output], axis=1)]
    stages += [w_in[:, n : n + 2 * width] for n in range(0, w_in.shape[1], 2 * width)]
    order = block_order.astype(jnp.int32)
    devices = jnp.arange(count, dtype=jnp.int32)
    by_block = jnp.sum(jnp.where(order[None, :] == devices[:, None], devices[None, :], 0), axis=1)
    own = order[me]
    partner = by_block[count - 1 - own]
    offsets = [0] + [o for k in range(1, count // 2) for o in (-k, k)] + [count // 2]
    relative = ring_places(count, me, offsets).astype(jnp.int32)
    wt_me = lax.axis_index("wt").astype(jnp.int32)
    scalars = jnp.concatenate(
        [
            jnp.stack([own, me, partner, starts[1], starts[2], wt_me]),
            by_block,
            order,
            relative,
        ]
    ).astype(jnp.int32)

    state = {"first": 0, "found": None, "seen": 0}

    def read_small(shares):
        small = jnp.stack([share[per:, : 2 * per] for share in shares[0]]).astype(F32)
        small = jnp.concatenate(
            [lax.dynamic_slice_in_dim(small, wt_me ^ n, 1, 0) for n in range(wt_count)], axis=0
        )
        gain_one = small[:, 0, :per].reshape(1, width)
        gain_two = small[:, 0, per:].reshape(1, width)
        mixes = small[:, mixes_at : mixes_at + mix_logit.shape[0], : 2 * heads].reshape(heads, 2 * heads)
        logit_mix, weight_mix = mixes[:, :heads], mixes[:, heads:]
        return gain_one, gain_two, logit_mix, weight_mix

    def work(rounds, shares, done=None):
        if done is not None:
            if done:
                *state["found"], state["mat"] = done
            return []
        if not state["seen"]:
            state["small"] = read_small(shares)
            state["mat"] = shares[0]
        batch = [piece for pieces in rounds[state["seen"] : -1] for _, piece in pieces]
        state["seen"] = len(rounds) - 1
        return project_batch(batch)

    def project_batch(batch):
        results = project(
            scalars, count, state["first"], batch, state["small"][0], state["mat"], state["found"]
        )
        state["first"] += len(batch)
        return [*results, state["mat"]][:7]

    rounds, shares, crossed = gather_all(x_own, stages, work)
    gain_one, gain_two, logit_mix, weight_mix = state["small"]
    qo_shares = shares[1]

    mix_by_g = jnp.repeat(logit_mix.T, size, axis=1)
    weight_by_g = jnp.repeat(weight_mix, size, axis=1)
    mix_rows = mix_by_g * (scale * LOG2E)
    spread = jnp.repeat(weight_mix.T, half, axis=1)
    logit_spread = jnp.repeat(logit_mix, half, axis=1)

    batch = [piece for pieces in rounds[state["seen"] :] for _, piece in pieces]
    k, v, kt, vt, nt, xg, kv_mat = project_batch(batch)
    xg, *crossed[len(shares) :] = tie(xg, *crossed[len(shares) :])
    q, x_low, query_mat = queries(scalars, xg, gain_one, qo_shares)
    x_low = x_low.reshape(rows, width)
    for n in range(len(shares), len(stages)):
        near = lax.ppermute(stages[n], "wt", swaps(wt_count, 1))
        both = lax.ppermute(crossed[n], "wt", swaps(wt_count, 1))
        q, near, both = lax.optimization_barrier((q, near, both))
        shares.append([stages[n], near, crossed[n], both])
    w_out_after, _ = lax.optimization_barrier((w_out, rounds[-1][0][1]))
    outer_mat = lax.all_gather(w_out_after, "wt", axis=0, tiled=True)

    def exchange(second):
        every = lax.all_gather(second, "ctx", axis=0)
        return lax.dynamic_index_in_dim(every, partner, 0, keepdims=False)

    dy_second, _ = lax.optimization_barrier((cotangent[0, half:], rounds[-1][0][1]))
    dy_low = jnp.concatenate([cotangent[0, :half], exchange(dy_second)], axis=0)

    attended, t, lse = attend(scalars, q, k, vt, mix_rows, spread, heads)
    out_low, grad_middle, grad_att, keep, send, grad_gain_two, squares = ffn(
        scalars, wt_count, heads, attended.reshape(rows, width), x_low, dy_low, gain_two,
        qo_shares, shares[2:], outer_mat,
    )
    output_own = jnp.concatenate([out_low[:half], exchange(out_low[half:])], axis=0)
    grad_att = grad_att.reshape(2, half, width)
    grad_middle = grad_middle.reshape(2, half, width)

    got = lax.ppermute(send, "wt", swaps(wt_count, 1))
    r_weight, delta = deltas(grad_att, t, spread, heads)
    summed = add(keep, got).reshape(2, count, -1, width).transpose(1, 0, 2, 3).reshape(-1, width)
    summed, delta = tie(summed, delta)
    summed = lax.psum_scatter(summed, "ctx", scatter_dimension=0, tiled=True)

    dk, dv, dq, r_logit = back(
        scalars, 0, heads, q, grad_att, k, v, kt, lse, delta, mix_rows, weight_by_g,
        logit_spread, heads, scale,
    )

    def parts(first, batch, dk):
        return token_parts(
            scalars, first, batch, dk, dv, dq, xg, query_mat, kv_mat, gain_one, grad_middle
        )

    last = count // 2
    far = parts(count - 1, 1, dk)
    dk, far = tie(dk, far)
    up, down = far_start(far[0])
    total = -(-(3 * per + TAIL_ROWS) // (8 * count)) * 8 * count
    keep, send = weight_grads(
        scalars, wt_count, total, dk, dv, dq, nt, r_logit, r_weight, grad_gain_two, squares
    )
    up, down, keep, send, summed, dk = tie(up, down, keep, send, summed, dk)
    up, down = far_end(up, down)
    summed = summed.reshape(2, -1, width)
    near = lax.ppermute(send, "wt", swaps(wt_count, 1))
    ffn_far = lax.ppermute(summed[1], "wt", swaps(wt_count, 2))
    pair = parts(2 * (last - 1) - 1, 2, dk)
    near, ffn_far, pair = tie(near, ffn_far, pair)
    over = lax.ppermute(add(keep[1], near[1]), "wt", swaps(wt_count, 2))
    share = add(summed[0], ffn_far)

    turn = None
    for k in range(last - 1, 0, -1):
        up, down = ring_both(add(up, pair[1]), add(down, pair[0]))
        beside = [over, share] if turn is None else list(turn.start())
        after = parts(2 * (k - 1) - 1, 2, dk) if k > 1 else parts(0, 1, dk)
        up, down, pair, *beside = tie(up, down, after, *beside)
        if turn is None:
            over, share = beside
            ffn_sum = lax.all_gather(share, "ctx", axis=0, tiled=True)
            turn = Turning(add(keep[0], near[0], over).reshape(count, -1, width), me)
        else:
            turn.finish(*beside)
    input_grad = add(up, down, pair[0])
    while not turn.done:
        turn.finish(*tie(*turn.start()))

    places = ring_places(count, me, list(range(count))).astype(jnp.int32)
    entries = float(rows * width) * (count * wt_count)
    grad_q, grad_k, grad_v, gain_sum, gain_two_grad, logit_grad, weight_grad, rms = finish_grads(
        places, turn.ordered(), w_query, w_key, w_value, entries, heads, heads // wt_count
    )
    grad_out, grad_in, grad_o = unpack(ffn_sum, (w_out.shape, w_in.shape, w_output.shape))
    return (
        output_own[None],
        input_grad[None],
        rms.reshape(3),
        gain_sum.reshape(per) / gain_attn.astype(F32),
        grad_q,
        grad_k,
        grad_v,
        logit_grad,
        weight_grad,
        grad_o,
        gain_two_grad.reshape(per),
        grad_in,
        grad_out,
    )


def solution(mesh):
    tokens = P("wt", "ctx", None)
    matrix = P("wt", None)
    vector = P("wt")
    return jax.shard_map(
        shards,
        mesh=mesh,
        in_specs=(tokens, tokens, P(), matrix, vector)
        + (matrix,) * 6
        + (vector, matrix, matrix),
        out_specs=(tokens, tokens, P(), vector) + (matrix,) * 6 + (vector, matrix, matrix),
        check_vma=False,
    )
```

```python
import functools
import math

import jax
import jax.numpy as jnp
from jax import lax
from jax.experimental import pallas as pl
from jax.experimental.pallas import tpu as pltpu
from jax.sharding import PartitionSpec as P

NEG = -1e30
EPS = 1e-06
LOG2E = 1.4426950408889634
LN2 = 0.6931471805599453
F32 = jnp.float32
BF16 = jnp.bfloat16
NT = (((1,), (1,)), ((), ()))
VMEM_BYTES = 60 * 1024 * 1024


def dot(left, right):
    return jnp.dot(left, right, preferred_element_type=F32)


def dot_nt(left, right):
    return lax.dot_general(left, right, NT, preferred_element_type=F32)


def rms_norm(values, gain):
    return values * lax.rsqrt(jnp.mean(values * values, axis=-1, keepdims=True) + EPS) * gain


def gelu_tanh(values):
    return jax.nn.gelu(values, approximate=True)


def params(flops, moved, dims=1):
    return dict(
        compiler_params=pltpu.CompilerParams(
            dimension_semantics=("arbitrary",) * dims, vmem_limit_bytes=VMEM_BYTES
        ),
        cost_estimate=pl.CostEstimate(flops=flops, bytes_accessed=moved, transcendentals=0),
    )


HEAD = 6


def assemble(me, target, pieces, per, cols=slice(None)):
    for n, piece in enumerate(pieces):
        rows = pl.ds(pl.multiple_of((me ^ n) * per, per), per)
        target[rows, :] = piece[:per, cols]


def project_kernel(batch, shares, sc, *refs):
    pieces, (gain_ref, *weights) = refs[:batch], refs[batch : batch + 1 + max(1, len(shares))]
    outs = refs[-(7 if shares else 6) :]
    k_ref, v_ref, kt_ref, vt_ref, nt_ref, x_out = outs[:6]
    width = x_out.shape[2]
    mat = outs[6] if shares else weights[0]
    if shares:

        @pl.when(pl.program_id(0) == 0)
        def start():
            assemble(sc[5], mat, weights, width // len(weights))

    def one(x_ref):
        x_low = x_ref[...]
        x_out[0] = x_low
        normed = rms_norm(x_low.astype(F32), gain_ref[...]).astype(BF16)
        nt_ref[0] = normed.T
        k = dot(normed, mat[:, :width]).astype(BF16)
        k_ref[0] = k
        kt_ref[0] = k.T
        v = dot(normed, mat[:, width:]).astype(BF16)
        v_ref[0] = v
        vt_ref[0] = v.T

    for n in range(batch):
        pl.when(pl.program_id(0) == n)(functools.partial(one, pieces[n]))


def project(scalars, count, first, pieces, gain, mat, before):
    batch = len(pieces)
    rows, width = pieces[0].shape
    place = lambda j, sc: (sc[HEAD + 2 * count + first + j], 0, 0)
    fixed = lambda j, sc: (0, 0)
    tall = jax.ShapeDtypeStruct((count, rows, width), BF16)
    wide = jax.ShapeDtypeStruct((count, width, rows), BF16)
    once = pl.Buffered(1)
    before = () if before is None else tuple(before)
    shares = tuple(mat) if isinstance(mat, (list, tuple)) else ()
    weights = shares or (mat,)
    out_specs = [
        pl.BlockSpec((1, rows, width), place),
        pl.BlockSpec((1, rows, width), place),
        pl.BlockSpec((1, width, rows), place),
        pl.BlockSpec((1, width, rows), place),
        pl.BlockSpec((1, width, rows), place),
        pl.BlockSpec((1, rows, width), place),
    ]
    out_shape = [tall, tall, wide, wide, wide, tall]
    if shares:
        out_specs.append(pl.BlockSpec((width, 2 * width), fixed, pipeline_mode=once))
        out_shape.append(jax.ShapeDtypeStruct((width, 2 * width), BF16))
    return pl.pallas_call(
        functools.partial(project_kernel, batch, shares),
        grid_spec=pltpu.PrefetchScalarGridSpec(
            num_scalar_prefetch=1,
            grid=(batch,),
            in_specs=[pl.BlockSpec((rows, width), fixed, pipeline_mode=once)] * batch
            + [pl.BlockSpec((1, width), fixed)]
            + [pl.BlockSpec(w.shape, fixed, pipeline_mode=once) for w in weights]
            + [pl.BlockSpec(memory_space=pl.ANY)] * len(before),
            out_specs=out_specs,
        ),
        out_shape=out_shape,
        input_output_aliases={batch + 2 + len(weights) + n: n for n in range(len(before))},
        **params(4 * batch * rows * width * width, 14 * batch * rows * width),
    )(scalars, *pieces, gain, *weights, *before)


def query_kernel(sc, x_ref, gain_ref, *refs):
    shares, (q_ref, x_out, mat) = refs[:-3], refs[-3:]

    @pl.when(pl.program_id(0) == 0)
    def start():
        assemble(sc[5], mat, shares, mat.shape[0] // len(shares), slice(0, mat.shape[1]))

    x_out[0] = x_ref[0]
    normed = rms_norm(x_ref[0].astype(F32), gain_ref[...]).astype(BF16)
    q_ref[0] = dot(normed, mat[...]).astype(BF16)


def queries(scalars, xg, gain, shares):
    count, rows, width = xg.shape
    half = rows // 2
    fixed = lambda n, sc: (0, 0)
    once = pl.Buffered(1)
    part = jax.ShapeDtypeStruct((2, half, width), BF16)
    return pl.pallas_call(
        query_kernel,
        grid_spec=pltpu.PrefetchScalarGridSpec(
            num_scalar_prefetch=1,
            grid=(2,),
            in_specs=[
                pl.BlockSpec((1, half, width), lambda n, sc: (sc[1 + n], n, 0)),
                pl.BlockSpec((1, width), fixed),
            ]
            + [pl.BlockSpec(w.shape, fixed, pipeline_mode=once) for w in shares],
            out_specs=[
                pl.BlockSpec((1, half, width), lambda n, sc: (n, 0, 0)),
                pl.BlockSpec((1, half, width), lambda n, sc: (n, 0, 0)),
                pl.BlockSpec((width, width), fixed, pipeline_mode=once),
            ],
        ),
        out_shape=[part, part, jax.ShapeDtypeStruct((width, width), BF16)],
        **params(2 * rows * width * width, 4 * width * width),
    )(scalars, xg, gain, *shares)


def doc_of(sc, place):
    return (place >= sc[3]).astype(jnp.int32) + (place >= sc[4]).astype(jnp.int32)


def set_bias(bias_s, sc, key_place, query_place):
    rows, twice = bias_s.shape
    half = twice // 2
    key_end, query_end = key_place + rows - 1, query_place + half - 1
    clear = (
        (key_end <= query_place)
        & (doc_of(sc, key_place) == doc_of(sc, query_end))
        & (doc_of(sc, key_end) == doc_of(sc, query_place))
        & (doc_of(sc, key_end) == doc_of(sc, query_end))
    )

    @pl.when(clear)
    def seen():
        bias_s[...] = jnp.zeros(bias_s.shape, F32)

    @pl.when(jnp.logical_not(clear))
    def mixed():
        key_pos = key_place + lax.broadcasted_iota(jnp.int32, (rows, 1), 0)
        lane = lax.broadcasted_iota(jnp.int32, (1, twice), 1)
        query_pos = query_place + jnp.where(lane >= half, lane - half, lane)
        visible = (key_pos <= query_pos) & (doc_of(sc, key_pos) == doc_of(sc, query_pos))
        bias_s[...] = jnp.where(visible, 0.0, NEG)


def fold(target, lead, source, mix_ref, heads, half):
    values = source.astype(F32)
    for g in range(heads):
        piece = (values * mix_ref[g : g + 1, :]).astype(BF16)
        if lead is None:
            target[g * half : (g + 1) * half, :] = piece
        else:
            target[lead, g * half : (g + 1) * half, :] = piece


def attend_kernel(
    count, heads, group, sc, q_ref, k_ref, vt_ref, mix_ref, spread_ref,
    att_ref, t_ref, lse_ref, folded, total, top, norm, bias_s, mixed_s, ahead,
):
    half, width = q_ref.shape[1], q_ref.shape[2]
    rows = k_ref.shape[1]
    step = pl.program_id(0)
    own = sc[0]
    first_half = step <= own
    tile = jnp.where(first_half, step, step - own - 1)
    query_place = jnp.where(first_half, own * rows, (count - 1 - own) * rows + half)

    @pl.when((step == 0) | (step == own + 1))
    def start():
        fold(folded, None, q_ref[0], mix_ref, heads, half)
        top[...] = jnp.full(top.shape, NEG, F32)
        norm[...] = jnp.zeros(norm.shape, F32)
        total[...] = jnp.zeros(total.shape, F32)

    set_bias(bias_s, sc, tile * rows, query_place)
    span = group * half
    chunks = [slice(c * span, (c + 1) * span) for c in range(heads // group)]
    ahead[0] = dot_nt(k_ref[0], folded[chunks[0], :])
    for c, cols in enumerate(chunks):
        if c + 1 < len(chunks):
            ahead[(c + 1) % 2] = dot_nt(k_ref[0], folded[chunks[c + 1], :])
        logits = ahead[c % 2] + jnp.concatenate([bias_s[...]] * (group // 2), axis=1)
        before = top[:, cols]
        after = jnp.maximum(before, jnp.max(logits, axis=0, keepdims=True))
        shrink = jnp.exp2(before - after)
        weights = jnp.exp2(logits - after)
        top[:, cols] = after
        norm[:, cols] = norm[:, cols] * shrink + jnp.sum(weights, axis=0, keepdims=True)
        total[:, cols] = total[:, cols] * shrink + dot(vt_ref[0], weights.astype(BF16))

    @pl.when((step == own) | (step == count))
    def finish():
        lse_ref[0] = top[...] + jnp.log2(norm[...])
        norm[...] = 1.0 / norm[...]
        mix_all(
            total, spread_ref, mixed_s, half,
            lambda h, rows, cols: scale_out(total, norm, t_ref, rows, cols),
        )
        att_ref[0] = (mixed_s[:, :half] + mixed_s[:, half:]).T.astype(BF16)


def scale_out(total, norm, t_ref, rows, cols):
    scaled = total[rows, cols] * norm[:, cols]
    t_ref[0, rows, cols] = scaled.astype(BF16)
    return scaled


def mix_all(total, spread_ref, mixed_s, half, find):
    heads = spread_ref.shape[0]
    size = mixed_s.shape[0] // heads
    for h in range(heads):
        rows = slice(h * size, (h + 1) * size)
        found = jnp.zeros((size, 2 * half), F32)
        for p in range(spread_ref.shape[1] // (2 * half)):
            cols = slice(2 * p * half, (2 * p + 2) * half)
            found += find(h, rows, cols) * spread_ref[h : h + 1, cols]
        mixed_s[rows, :] = found


def attend(scalars, q, k, vt, mix_rows, spread, heads):
    count, rows, width = k.shape
    half = q.shape[1]
    span = heads * half
    which = lambda s, sc: (jnp.where(s <= sc[0], 0, 1), 0, 0)
    tile = lambda s, sc: (sc[HEAD + jnp.where(s <= sc[0], s, s - sc[0] - 1)], 0, 0)
    fixed = lambda s, sc: (0, 0)
    group = math.gcd(heads, 4)
    return pl.pallas_call(
        functools.partial(attend_kernel, count, heads, group),
        grid_spec=pltpu.PrefetchScalarGridSpec(
            num_scalar_prefetch=1,
            grid=(count + 1,),
            in_specs=[
                pl.BlockSpec((1, half, width), which),
                pl.BlockSpec((1, rows, width), tile),
                pl.BlockSpec((1, width, rows), tile),
                pl.BlockSpec((heads, width), fixed),
                pl.BlockSpec((heads, span), fixed),
            ],
            out_specs=[
                pl.BlockSpec((1, half, width), which),
                pl.BlockSpec((1, width, span), which),
                pl.BlockSpec((1, 1, span), which),
            ],
            scratch_shapes=[
                pltpu.VMEM((span, width), BF16),
                pltpu.VMEM((width, span), F32),
                pltpu.VMEM((1, span), F32),
                pltpu.VMEM((1, span), F32),
                pltpu.VMEM((rows, 2 * half), F32),
                pltpu.VMEM((width, 2 * half), F32),
                pltpu.VMEM((2, rows, group * half), F32),
            ],
        ),
        out_shape=[
            jax.ShapeDtypeStruct((2, half, width), BF16),
            jax.ShapeDtypeStruct((2, width, span), BF16),
            jax.ShapeDtypeStruct((2, 1, span), F32),
        ],
        **params(4 * (count + 1) * rows * span * width, 6 * count * rows * width),
    )(scalars, q, k, vt, mix_rows, spread)


def pair_rows(left, right, heads):
    product = left * right
    size = product.shape[0] // heads
    return jnp.concatenate(
        [
            jnp.sum(product[h * size : (h + 1) * size, :], axis=0, keepdims=True)
            for h in range(heads)
        ],
        axis=0,
    )


def lanes_of(found, first, half, lanes=128):
    place = lax.broadcasted_iota(jnp.int32, (found.shape[0], lanes), 1)
    total = jnp.zeros((found.shape[0], lanes), F32)
    for n in range(found.shape[1] // half):
        piece = jnp.sum(found[:, n * half : (n + 1) * half], axis=1, keepdims=True)
        total = jnp.where(place == first + n, piece, total)
    return total


def delta_kernel(heads, grad_ref, t_ref, spread_ref, r_ref, delta_ref):
    half = grad_ref.shape[1]
    grad_t = grad_ref[0].astype(F32).T
    twice = jnp.concatenate([grad_t, grad_t], axis=1)
    sums = jnp.zeros(r_ref.shape, F32)
    for p in range(heads // 2):
        cols = slice(2 * p * half, (2 * p + 2) * half)
        found = pair_rows(twice, t_ref[0, :, cols].astype(F32), heads)
        sums += lanes_of(found, 2 * p, half)
        delta_ref[0, :, cols] = jnp.sum(found * spread_ref[:, cols], axis=0, keepdims=True)

    @pl.when(pl.program_id(0) == 0)
    def first():
        r_ref[...] = sums

    @pl.when(pl.program_id(0) == 1)
    def second():
        r_ref[...] += sums


def deltas(grad_att, t, spread, heads):
    _, half, width = grad_att.shape
    span = heads * half
    return pl.pallas_call(
        functools.partial(delta_kernel, heads),
        grid=(2,),
        in_specs=[
            pl.BlockSpec((1, half, width), lambda s: (s, 0, 0)),
            pl.BlockSpec((1, width, span), lambda s: (s, 0, 0)),
            pl.BlockSpec((heads, span), lambda s: (0, 0)),
        ],
        out_specs=[
            pl.BlockSpec((heads, 128), lambda s: (0, 0)),
            pl.BlockSpec((1, 1, span), lambda s: (s, 0, 0)),
        ],
        out_shape=[
            jax.ShapeDtypeStruct((heads, 128), F32),
            jax.ShapeDtypeStruct((2, 1, span), F32),
        ],
        **params(4 * width * span, 4 * width * span),
    )(grad_att, t, spread)


def back_place(step, own, count):
    low = jnp.minimum(own, count - 1 - own)
    both = step < 2 * (low + 1)
    tile = jnp.where(both, step // 2, step - low - 1)
    part = jnp.where(both, step % 2, jnp.where(own > count - 1 - own, 0, 1))
    return low, both, tile, part


def back_kernel(
    count, heads, base, group, scale, sc, q_ref, ga_ref, k_ref, v_ref, kt_ref, lse_ref, delta_ref,
    mix_ref, weight_ref, spread_ref, dk_ref, dv_ref, dq_ref, r_ref,
    fq, fa, total, dk_s, dv_s, bias_s, mixed_s, twice_s, rows_s, ahead_l, ahead_p,
):
    half, width = q_ref.shape[1], q_ref.shape[2]
    rows = k_ref.shape[1]
    step = pl.program_id(0)
    own = sc[0]
    low, both, tile, part = back_place(step, own, count)
    query_place = jnp.where(part == 0, own * rows, (count - 1 - own) * rows + half)

    @pl.when(step == 0)
    def start():
        for n in range(2):
            q = q_ref[n].astype(F32)
            ga = ga_ref[n].astype(F32)
            for g in range(group):
                cols = slice(g * half, (g + 1) * half)
                fq[n, cols, :] = (q * mix_ref[base + g : base + g + 1, :]).astype(BF16)
                fa[n, cols, :] = (ga * weight_ref[base + g : base + g + 1, :]).astype(BF16)
        total[...] = jnp.zeros(total.shape, F32)

    @pl.when(jnp.logical_not(both) | (part == 0))
    def clear():
        dk_s[...] = jnp.zeros(dk_s.shape, F32)
        dv_s[...] = jnp.zeros(dv_s.shape, F32)

    set_bias(bias_s, sc, tile * rows, query_place)
    chunk = math.gcd(group, 4)
    chunks = [slice(c * chunk * half, (c + 1) * chunk * half) for c in range(group // chunk)]

    def look(c):
        ahead_l[c % 2] = dot_nt(k_ref[0], fq[part, chunks[c], :])
        ahead_p[c % 2] = dot_nt(v_ref[0], fa[part, chunks[c], :])

    look(0)
    for c, cols in enumerate(chunks):
        if c + 1 < len(chunks):
            look(c + 1)
        logits = ahead_l[c % 2] + jnp.concatenate([bias_s[...]] * (chunk // 2), axis=1)
        prob = jnp.exp2(logits - lse_ref[part, :, cols])
        grad_logits = (prob * (ahead_p[c % 2] - delta_ref[part, :, cols])).astype(BF16)
        dv_s[...] += dot(prob.astype(BF16), fa[part, cols, :])
        dk_s[...] += dot(grad_logits, fq[part, cols, :])
        total[part, :, cols] += dot(kt_ref[0], grad_logits)

    @pl.when(jnp.logical_not(both) | (part == 1))
    def leave():
        dk_ref[0] = (dk_s[...] * LN2).astype(BF16)
        dv_ref[0] = dv_s[...].astype(BF16)

    @pl.when(step == count)
    def finish():
        sums = jnp.zeros(r_ref.shape, F32)
        size = width // heads
        for n in range(2):
            q_t = q_ref[n].astype(F32).T
            twice_s[...] = jnp.concatenate([q_t, q_t], axis=1)

            def find(h, rows, cols):
                piece = total[n, rows, cols]
                rows_s[h : h + 1, cols] = jnp.sum(piece * twice_s[rows, :], axis=0, keepdims=True)
                return piece

            mix_all(total, spread_ref, mixed_s, half, find)
            sums += lanes_of(rows_s[...], 0, half)
            dq_ref[n] = ((mixed_s[:, :half] + mixed_s[:, half:]).T * scale).astype(BF16)
        r_ref[...] = sums * scale


def back(
    scalars, base, group, q, grad_att, k, v, kt, lse, delta, mix_rows, weight_rows, spread, heads, scale
):
    count, rows, width = k.shape
    half = q.shape[1]
    span = group * half
    tile = lambda s, sc: (sc[HEAD + back_place(s, sc[0], count)[2]], 0, 0)
    whole = lambda s, sc: (0, 0, 0)
    cut = lambda s, sc: (0, 0, base // group)
    fixed = lambda s, sc: (0, 0)
    once = pl.Buffered(1)
    return pl.pallas_call(
        functools.partial(back_kernel, count, heads, base, group, scale),
        grid_spec=pltpu.PrefetchScalarGridSpec(
            num_scalar_prefetch=1,
            grid=(count + 1,),
            in_specs=[
                pl.BlockSpec((2, half, width), whole, pipeline_mode=once),
                pl.BlockSpec((2, half, width), whole, pipeline_mode=once),
                pl.BlockSpec((1, rows, width), tile),
                pl.BlockSpec((1, rows, width), tile),
                pl.BlockSpec((1, width, rows), tile),
                pl.BlockSpec((2, 1, span), cut, pipeline_mode=once),
                pl.BlockSpec((2, 1, span), cut, pipeline_mode=once),
                pl.BlockSpec((heads, width), fixed),
                pl.BlockSpec((heads, width), fixed),
                pl.BlockSpec((heads, span), fixed),
            ],
            out_specs=[
                pl.BlockSpec((1, rows, width), tile),
                pl.BlockSpec((1, rows, width), tile),
                pl.BlockSpec((2, half, width), whole),
                pl.BlockSpec((heads, 128), fixed),
            ],
            scratch_shapes=[
                pltpu.VMEM((2, span, width), BF16),
                pltpu.VMEM((2, span, width), BF16),
                pltpu.VMEM((2, width, span), F32),
                pltpu.VMEM((rows, width), F32),
                pltpu.VMEM((rows, width), F32),
                pltpu.VMEM((rows, 2 * half), F32),
                pltpu.VMEM((width, 2 * half), F32),
                pltpu.VMEM((width, 2 * half), F32),
                pltpu.VMEM((heads, span), F32),
                pltpu.VMEM((2, rows, math.gcd(group, 4) * half), F32),
                pltpu.VMEM((2, rows, math.gcd(group, 4) * half), F32),
            ],
        ),
        out_shape=[
            jax.ShapeDtypeStruct((count, rows, width), BF16),
            jax.ShapeDtypeStruct((count, rows, width), BF16),
            jax.ShapeDtypeStruct((2, half, width), BF16),
            jax.ShapeDtypeStruct((heads, 128), F32),
        ],
        **params(10 * (count + 1) * rows * span * width, 10 * count * rows * width),
    )(scalars, q, grad_att, k, v, kt, lse, delta, mix_rows, weight_rows, spread)


def put(keep_ref, send_ref, place, rows, value):
    @pl.when(place % 2 == 0)
    def kept():
        keep_ref[place // 2, rows, :] = value

    @pl.when(place % 2 == 1)
    def sent():
        send_ref[place // 2, rows, :] = value


def norm_parts(x):
    inverse = lax.rsqrt(jnp.mean(x * x, axis=-1, keepdims=True) + EPS)
    return inverse, x * inverse


def norm_back(inverse, bare, grad, gain):
    gained = grad * gain
    return inverse * (gained - bare * jnp.mean(gained * bare, axis=-1, keepdims=True))


def ffn_kernel(wt_count, sc, att_ref, x_ref, dy_ref, gain_ref, *refs):
    n = wt_count
    halves = (len(refs) - 15) // n - 2
    groups = [refs[i * n : (i + 1) * n] for i in range(halves + 2)]
    wo_shares, win_shares, wout_shares = groups[0], groups[1:-1], groups[-1]
    (
        out_ref, gm_ref, gatt_ref, keep_ref, send_ref, gain_out, sq_ref,
        middle_s, low_s, low_t, feed_s, grad_s, wo_ref, win_ref, wout_ref,
    ) = refs[(halves + 2) * n :]
    j = pl.program_id(0)
    last = pl.num_programs(0) - 1
    me = sc[5]
    width = x_ref.shape[1]
    per = width // wt_count
    for i in range(halves):
        for side in range(2):
            pl.when(j == 2 * i + side)(
                functools.partial(
                    assemble, me, win_ref, win_shares[i], per, slice(side * width, (side + 1) * width)
                )
            )

    def take(share):
        wout_ref[...] = share[...]

    for i, share in enumerate(wout_shares):
        pl.when((j ^ me) == i)(functools.partial(take, share))

    @pl.when(j == 0)
    def start():
        assemble(me, wo_ref, wo_shares, per, slice(width, 2 * width))
        branch = dot(att_ref[...], wo_ref[...])
        middle = x_ref[...].astype(F32) + branch
        middle_s[...] = middle
        _, bare = norm_parts(middle)
        low = (bare * gain_ref[...]).astype(BF16)
        low_s[...] = low
        low_t[...] = low.T
        feed_s[...] = jnp.zeros(feed_s.shape, F32)
        grad_s[...] = jnp.zeros(grad_s.shape, F32)
        sq_ref[...] = jnp.zeros(sq_ref.shape, F32)
        sq_ref[1:2, :] = jnp.broadcast_to(jnp.sum(branch * branch).reshape(1, 1), (1, 128))

    dy = dy_ref[...]
    hidden = dot(low_s[...], win_ref[...])
    grad_active = dot_nt(dy, wout_ref[...])
    square = hidden * hidden
    inner = jnp.tanh(hidden * (0.7978845608028654 + 0.7978845608028654 * 0.044715 * square))
    half_one = 0.5 + 0.5 * inner
    active = (hidden * half_one).astype(BF16)
    slope = half_one + (0.5 * hidden) * (1.0 - inner * inner) * (
        0.7978845608028654 + 3.0 * 0.7978845608028654 * 0.044715 * square
    )
    grad_hidden = (grad_active * slope).astype(BF16)
    feed_s[...] += dot(active, wout_ref[...])
    grad_s[...] += dot_nt(grad_hidden, win_ref[...])
    grad_out = dot(active.T, dy).astype(BF16)
    grad_in = dot(low_t[...], grad_hidden).astype(BF16)
    put(keep_ref, send_ref, j ^ me, slice(0, width), grad_out)
    for t in range(wt_count):
        rows = pl.ds(pl.multiple_of(width + j * per, per), per)
        put(keep_ref, send_ref, t ^ me, rows, grad_in[t * per : (t + 1) * per, :])

    @pl.when(j == last)
    def finish():
        middle = middle_s[...]
        feed = feed_s[...]
        output = middle + feed
        out_ref[...] = output.astype(BF16)
        sq_ref[0:1, :] = jnp.broadcast_to(jnp.sum(output * output).reshape(1, 1), (1, 128))
        sq_ref[2:3, :] = jnp.broadcast_to(jnp.sum(feed * feed).reshape(1, 1), (1, 128))
        inverse, bare = norm_parts(middle)
        grad = grad_s[...]
        gain_out[...] = jnp.sum(grad * bare, axis=0, keepdims=True)
        grad_middle = dy.astype(F32) + norm_back(inverse, bare, grad, gain_ref[...])
        gm_ref[...] = grad_middle
        low = grad_middle.astype(BF16)
        gatt_ref[...] = dot_nt(low, wo_ref[...]).astype(BF16)
        grad_o = dot(att_ref[...].T, low).astype(BF16)
        for t in range(wt_count):
            put(
                keep_ref, send_ref, t ^ me,
                slice(keep_ref.shape[1] - per, keep_ref.shape[1]),
                grad_o[t * per : (t + 1) * per, :],
            )


def ffn(scalars, wt_count, sq_rows, att, x, dy, gain, wo, wins, wout):
    rows, width = x.shape
    chunks = 2 * len(wins)
    per = width // wt_count
    total = width + per * chunks + per
    fixed = lambda j, sc: (0, 0)
    whole = lambda j, sc: (0, 0, 0)
    once = pl.Buffered(1)
    kernel = functools.partial(ffn_kernel, wt_count)
    shares = [*wo, *(share for win in wins for share in win), *wout]
    return pl.pallas_call(
        kernel,
        grid_spec=pltpu.PrefetchScalarGridSpec(
            num_scalar_prefetch=1,
            grid=(chunks,),
            in_specs=[
                pl.BlockSpec((rows, width), fixed, pipeline_mode=once),
                pl.BlockSpec((rows, width), fixed, pipeline_mode=once),
                pl.BlockSpec((rows, width), fixed, pipeline_mode=once),
                pl.BlockSpec((1, width), fixed),
            ]
            + [pl.BlockSpec(w.shape, fixed, pipeline_mode=once) for w in shares],
            out_specs=[
                pl.BlockSpec((rows, width), fixed),
                pl.BlockSpec((rows, width), fixed),
                pl.BlockSpec((rows, width), fixed),
                pl.BlockSpec((wt_count // 2, total, width), whole),
                pl.BlockSpec((wt_count // 2, total, width), whole),
                pl.BlockSpec((1, width), fixed),
                pl.BlockSpec((sq_rows, 128), fixed),
            ],
            scratch_shapes=[
                pltpu.VMEM((rows, width), F32),
                pltpu.VMEM((rows, width), BF16),
                pltpu.VMEM((width, rows), BF16),
                pltpu.VMEM((rows, width), F32),
                pltpu.VMEM((rows, width), F32),
                pltpu.VMEM((width, width), BF16),
                pltpu.VMEM((width, width), BF16),
                pltpu.VMEM((width, width), BF16),
            ],
        ),
        out_shape=[
            jax.ShapeDtypeStruct((rows, width), BF16),
            jax.ShapeDtypeStruct((rows, width), F32),
            jax.ShapeDtypeStruct((rows, width), BF16),
            jax.ShapeDtypeStruct((wt_count // 2, total, width), BF16),
            jax.ShapeDtypeStruct((wt_count // 2, total, width), BF16),
            jax.ShapeDtypeStruct((1, width), F32),
            jax.ShapeDtypeStruct((sq_rows, 128), F32),
        ],
        **params(10 * chunks * rows * width * width + 6 * rows * width * width, 24 * width * width),
    )(scalars, att, x, dy, gain, *shares)


TAIL_ROWS = 16


def seen_by(sc, count, device):
    return sc[HEAD + count + device] <= jnp.maximum(sc[0], count - 1 - sc[0])


def weight_kernel(
    count, wt_count, sc, dk_ref, dv_ref, dq_ref, nt_ref, rl_ref, rw_ref, gain_two_ref, sq_ref,
    keep_ref, send_ref, dwq, dwk, dwv,
):
    width, rows = nt_ref.shape[1:]
    half = rows // 2
    device = pl.program_id(0)
    me_wt = sc[5]

    @pl.when(device == 0)
    def start():
        dwq[...] = jnp.zeros(dwq.shape, F32)
        dwk[...] = jnp.zeros(dwk.shape, F32)
        dwv[...] = jnp.zeros(dwv.shape, F32)

    @pl.when(seen_by(sc, count, device))
    def seen():
        dwk[...] += dot(nt_ref[0], dk_ref[0])
        dwv[...] += dot(nt_ref[0], dv_ref[0])

    def queries(n):
        empty = jnp.zeros((half, width), BF16)
        both = [dq_ref[n], empty] if n == 0 else [empty, dq_ref[n]]
        dwq[...] += dot(nt_ref[0], jnp.concatenate(both, axis=0))

    pl.when(device == sc[1])(functools.partial(queries, 0))
    pl.when(device == sc[2])(functools.partial(queries, 1))

    @pl.when(device == count - 1)
    def finish():
        per = width // wt_count

        def pad(value, lanes):
            empty = jnp.zeros((value.shape[0], lanes - value.shape[1]), F32)
            return jnp.concatenate([value, empty], axis=1)

        heads = rw_ref.shape[0]
        each = heads // wt_count
        square = jnp.concatenate([rw_ref[...], jnp.zeros((128 - heads, 128), F32)], axis=0).T
        below = keep_ref.shape[1] - 3 * per - TAIL_ROWS
        assert TAIL_ROWS >= 4 + 2 * each

        def tail(t):
            rows = [
                pad(gain_two_ref[:, t * per : (t + 1) * per], width),
                pad(sq_ref[0:3, :], width),
                pad(rl_ref[t * each : (t + 1) * each, :], width),
                pad(square[t * each : (t + 1) * each, :], width),
                jnp.zeros((TAIL_ROWS - 4 - 2 * each + below, width), F32),
            ]
            return jnp.concatenate(rows, axis=0).astype(BF16)

        for t in range(wt_count):
            cut = slice(t * per, (t + 1) * per)
            for n, total in enumerate((dwq, dwk, dwv)):
                put(keep_ref, send_ref, t ^ me_wt, slice(n * per, (n + 1) * per), total[cut, :].astype(BF16))
            put(keep_ref, send_ref, t ^ me_wt, slice(3 * per, keep_ref.shape[1]), tail(t))


def weight_grads(scalars, wt_count, total, dk, dv, dq, nt, rl, rw, gain_two, sq):
    count, rows, width = dk.shape
    place = lambda j, sc: (j, 0, 0)
    fixed = lambda j, sc: (0, 0)
    whole = lambda j, sc: (0, 0, 0)
    once = pl.Buffered(1)
    share = jax.ShapeDtypeStruct((wt_count // 2, total, width), BF16)
    return pl.pallas_call(
        functools.partial(weight_kernel, count, wt_count),
        grid_spec=pltpu.PrefetchScalarGridSpec(
            num_scalar_prefetch=1,
            grid=(count,),
            in_specs=[
                pl.BlockSpec((1, rows, width), place),
                pl.BlockSpec((1, rows, width), place),
                pl.BlockSpec((2, rows // 2, width), whole, pipeline_mode=once),
                pl.BlockSpec((1, width, rows), place),
                pl.BlockSpec(rl.shape, fixed),
                pl.BlockSpec(rw.shape, fixed),
                pl.BlockSpec((1, width), fixed),
                pl.BlockSpec(sq.shape, fixed),
            ],
            out_specs=[
                pl.BlockSpec((wt_count // 2, total, width), whole),
                pl.BlockSpec((wt_count // 2, total, width), whole),
            ],
            scratch_shapes=[pltpu.VMEM((width, width), F32)] * 3,
        ),
        out_shape=[share, share],
        **params(4 * count * rows * width * width, 10 * count * rows * width),
    )(scalars, dk, dv, dq, nt, rl, rw, gain_two, sq)


def token_kernel(
    count, first, sc, dk_ref, dv_ref, dq_ref, x_ref, wq_ref, mat_ref, gain_ref, gm_ref, part_ref
):
    rows, width = x_ref.shape[1:]
    half = rows // 2
    device = sc[HEAD + 2 * count + first + pl.program_id(0)]
    valid = seen_by(sc, count, device)

    @pl.when(valid)
    def seen():
        grad = dot_nt(dk_ref[0], mat_ref[:, :width]) + dot_nt(dv_ref[0], mat_ref[:, width:])
        inverse, bare = norm_parts(x_ref[0].astype(F32))
        part_ref[0] = norm_back(inverse, bare, grad, gain_ref[...]).astype(BF16)

    @pl.when(jnp.logical_not(valid))
    def unseen():
        part_ref[0] = jnp.zeros(part_ref.shape[1:], BF16)

    def queries(n):
        mine = slice(n * half, (n + 1) * half)
        grad = dot_nt(dq_ref[n], wq_ref[...])
        inverse, bare = norm_parts(x_ref[0, mine, :].astype(F32))
        found = norm_back(inverse, bare, grad, gain_ref[...]) + gm_ref[n]
        part_ref[0, mine, :] = (part_ref[0, mine, :].astype(F32) + found).astype(BF16)

    pl.when(device == sc[1])(functools.partial(queries, 0))
    pl.when(device == sc[2])(functools.partial(queries, 1))


def token_parts(scalars, first, batch, dk, dv, dq, xg, wq, mat, gain, gm):
    count, rows, width = xg.shape
    place = lambda j, sc: (sc[HEAD + 2 * count + first + j], 0, 0)
    fixed = lambda j, sc: (0, 0)
    whole = lambda j, sc: (0, 0, 0)
    once = pl.Buffered(1)
    return pl.pallas_call(
        functools.partial(token_kernel, count, first),
        grid_spec=pltpu.PrefetchScalarGridSpec(
            num_scalar_prefetch=1,
            grid=(batch,),
            in_specs=[
                pl.BlockSpec((1, rows, width), place),
                pl.BlockSpec((1, rows, width), place),
                pl.BlockSpec((2, rows // 2, width), whole, pipeline_mode=once),
                pl.BlockSpec((1, rows, width), place),
                pl.BlockSpec((width, width), fixed, pipeline_mode=once),
                pl.BlockSpec((width, 2 * width), fixed, pipeline_mode=once),
                pl.BlockSpec((1, width), fixed),
                pl.BlockSpec((2, rows // 2, width), whole, pipeline_mode=once),
            ],
            out_specs=pl.BlockSpec((1, rows, width), lambda j, sc: (j, 0, 0)),
        ),
        out_shape=jax.ShapeDtypeStruct((batch, rows, width), BF16),
        **params(4 * batch * rows * width * width, 8 * batch * rows * width),
    )(scalars, dk, dv, dq, xg, wq, mat, gain, gm)


def finish_kernel(entries, heads, sc, *refs):
    count = len(refs) - 13
    pieces, (wq_ref, wk_ref, wv_ref, own_ref), outs, whole = refs[:count], refs[count : count + 4], refs[-9:-1], refs[-1]
    dq_ref, dk_ref, dv_ref, gain_ref, two_ref, logit_ref, weight_ref, rms_ref = outs
    gather_rows(sc, pieces, whole)
    rows = wq_ref.shape[0]
    gain = jnp.zeros((rows, 1), F32)
    for n, (out, w) in enumerate(((dq_ref, wq_ref), (dk_ref, wk_ref), (dv_ref, wv_ref))):
        found = whole[n * rows : (n + 1) * rows, :]
        out[...] = found
        gain += jnp.sum(found * w[...].astype(F32), axis=1, keepdims=True)
    gain_ref[...] = jnp.broadcast_to(gain, (rows, 128)).T[0:1, :] / own_ref[...].astype(F32)
    tail = whole[3 * rows : 3 * rows + TAIL_ROWS, :]
    each = logit_ref.shape[0]
    two_ref[...] = tail[0:1, :rows]
    rms_ref[...] = jnp.sqrt(tail[1:4, 0:1] * (1.0 / entries))
    logit_ref[...] = tail[4 : 4 + each, :heads]
    weight_ref[...] = tail[4 + each : 4 + 2 * each, :heads]


def finish_grads(places, pieces, wq, wk, wv, gain, entries, heads, each):
    count = len(pieces)
    rows, width = wq.shape
    ins = [*pieces, wq, wk, wv, gain]
    shapes = [(rows, width)] * 3 + [(1, rows), (1, rows), (each, heads), (each, heads), (3, 1)]
    fixed = lambda i, sc: (0, 0)
    return pl.pallas_call(
        functools.partial(finish_kernel, entries, heads),
        grid_spec=pltpu.PrefetchScalarGridSpec(
            num_scalar_prefetch=1,
            grid=(1,),
            in_specs=[pl.BlockSpec(v.shape, fixed) for v in ins],
            out_specs=[pl.BlockSpec(v, fixed) for v in shapes],
            scratch_shapes=[pltpu.VMEM((count * pieces[0].shape[0], width), F32)],
        ),
        out_shape=[jax.ShapeDtypeStruct(v, F32) for v in shapes],
        **params(0, 12 * rows * width),
    )(places, *ins)


def gather_rows(sc, pieces, whole):
    per = pieces[0].shape[0]
    for n, piece in enumerate(pieces):
        whole[pl.ds(pl.multiple_of(sc[n] * per, 8), per), :] = piece[...].astype(F32)


def unpack_kernel(sc, *refs):
    pieces, (out_ref, in_ref, o_ref, whole) = refs[:-4], refs[-4:]
    gather_rows(sc, pieces, whole)
    rows, width = out_ref.shape
    per = o_ref.shape[0]
    out_ref[...] = whole[:rows, :]
    chunks = in_ref.shape[1] // width
    for n in range(chunks):
        in_ref[:, n * width : (n + 1) * width] = whole[rows + n * per : rows + (n + 1) * per, :]
    o_ref[...] = whole[rows + chunks * per :, :]


def unpack(places, pieces, shapes):
    total = len(pieces) * pieces[0].shape[0]
    width = pieces[0].shape[1]
    fixed = lambda i, sc: (0, 0)
    return pl.pallas_call(
        unpack_kernel,
        grid_spec=pltpu.PrefetchScalarGridSpec(
            num_scalar_prefetch=1,
            grid=(1,),
            in_specs=[pl.BlockSpec(v.shape, fixed) for v in pieces],
            out_specs=[pl.BlockSpec(v, fixed) for v in shapes],
            scratch_shapes=[pltpu.VMEM((total, width), F32)],
        ),
        out_shape=[jax.ShapeDtypeStruct(shape, F32) for shape in shapes],
        **params(0, 6 * total * width),
    )(places, *pieces)


def swaps(size, distance):
    return [(i, i ^ distance) for i in range(size)]


def ring_order(count):
    return [2 * p if p < count // 2 else 2 * (count - 1 - p) + 1 for p in range(count)]


def ring(count, step):
    order = ring_order(count)
    return [(order[p], order[(p + step) % count]) for p in range(count)]


def ring_places(count, me, offsets):
    place = jnp.where((me & 1) == 0, me >> 1, count - 1 - (me >> 1))
    p = (place + jnp.array(offsets, jnp.int32)) & (count - 1)
    return jnp.where(p < count // 2, 2 * p, 2 * (count - 1 - p) + 1)


def ring_both(up, down):
    count = lax.axis_size("ctx")
    return lax.ppermute(up, "ctx", ring(count, 1)), lax.ppermute(down, "ctx", ring(count, -1))


def tie(*values):
    return lax.optimization_barrier(values)


def gather_all(value, stages, work):
    count = lax.axis_size("ctx")
    size = lax.axis_size("wt")
    half = value.shape[0] // 2
    rounds = [[(0, value)]]
    up = down = value
    shares, crossed = [], []
    for k in range(1, count // 2 + 1):
        last = k == count // 2
        up, down = ring_both(up[:half], down[half:]) if last else ring_both(up, down)
        tied = []
        if 2 <= k <= len(stages) + 1:
            tied.append(lax.ppermute(stages[k - 2], "wt", swaps(size, 1)))
            tied.append(lax.ppermute(crossed[k - 2], "wt", swaps(size, 1)))
        if k <= len(stages):
            crossed.append(lax.ppermute(stages[k - 1], "wt", swaps(size, 2)))
            if not last:
                tied.append(crossed.pop())
        done = work(rounds, shares) if k >= 3 else []
        up, down, done, *tied = tie(up, down, done, *tied)
        if k >= 3:
            work(rounds, shares, done)
        if k <= len(stages) and not last:
            crossed.append(tied.pop())
        if tied:
            shares.append([stages[k - 2], tied[0], crossed[k - 2], tied[1]])
        rounds.append([(count // 2, jnp.concatenate([up, down], axis=0))] if last else [(-k, up), (k, down)])
    return rounds, shares, crossed


def add(*values):
    return sum(v.astype(F32) for v in values).astype(BF16)


def far_start(far):
    half = far.shape[0] // 2
    up, down = ring_both(far[:half], far[half:])
    return up, down


def far_end(up, down):
    empty = jnp.zeros(up.shape, BF16)
    return jnp.concatenate([up, empty], axis=0), jnp.concatenate([empty, down], axis=0)


class Spreading:
    def __init__(self, piece, count):
        self.count, self.last = count, count // 2
        self.up = self.down = piece
        self.pieces = {0: piece}
        self.step = 0

    @property
    def done(self):
        return self.step == self.last

    def start(self):
        if self.step < self.last - 1:
            return ring_both(self.up, self.down)
        half = self.up.shape[0] // 2
        return ring_both(self.up[:half], self.down[half:])

    def finish(self, up, down):
        self.step += 1
        if self.done:
            self.pieces[self.last] = jnp.concatenate([up, down], axis=0)
        else:
            self.pieces[self.count - self.step], self.pieces[self.step] = up, down
        self.up, self.down = up, down

    def ordered(self):
        return [self.pieces[n] for n in range(self.count)]


class Turning:
    def __init__(self, blocks, me):
        self.count, self.last = blocks.shape[0], blocks.shape[0] // 2
        self.blocks, self.me = blocks, me
        self.step = 0
        self.spread = None

    @property
    def done(self):
        return self.spread is not None and self.spread.done

    def at(self, offset):
        place = ring_places(self.count, self.me, [offset])[0]
        return lax.dynamic_index_in_dim(self.blocks, place, 0, keepdims=False)

    def start(self):
        step, last = self.step, self.last
        if self.spread is not None:
            return self.spread.start()
        if step == 0:
            return far_start(self.at(last))
        return ring_both(add(self.up, self.at(last - step)), add(self.down, self.at(step - last)))

    def finish(self, up, down):
        if self.spread is not None:
            return self.spread.finish(up, down)
        if self.step == 0:
            up, down = far_end(up, down)
        elif self.step == self.last - 1:
            self.spread = Spreading(add(up, down, self.at(0)), self.count)
        self.up, self.down = up, down
        self.step += 1


def shards(
    residual_in,
    cotangent,
    block_order,
    doc_starts,
    gain_attn,
    w_query,
    w_key,
    w_value,
    mix_logit,
    mix_weight,
    w_output,
    gain_ffn,
    w_in,
    w_out,
):
    rows, width = residual_in.shape[1:]
    half = rows // 2
    heads = mix_logit.shape[1]
    size = width // heads
    scale = size ** (-0.5)
    count = lax.axis_size("ctx")
    me = lax.axis_index("ctx").astype(jnp.int32)
    wt_count = lax.axis_size("wt")
    starts = doc_starts[0]

    per = gain_attn.shape[0]
    across = lambda v, n: jnp.pad(v, ((0, n - v.shape[0]), (0, 2 * width - v.shape[1])))
    gains = jnp.concatenate([gain_attn, gain_ffn])[None, :]
    mixes_at = 8
    small = jnp.concatenate(
        [across(gains, mixes_at), across(jnp.concatenate([mix_logit, mix_weight], axis=1), mixes_at)], axis=0
    )
    kv_own = jnp.concatenate([jnp.concatenate([w_key, w_value], axis=1), small], axis=0)
    x_own = residual_in[0]
    stages = [kv_own, jnp.concatenate([w_query, w_output], axis=1)]
    stages += [w_in[:, n : n + 2 * width] for n in range(0, w_in.shape[1], 2 * width)]
    order = block_order.astype(jnp.int32)
    devices = jnp.arange(count, dtype=jnp.int32)
    by_block = jnp.sum(jnp.where(order[None, :] == devices[:, None], devices[None, :], 0), axis=1)
    own = order[me]
    partner = by_block[count - 1 - own]
    offsets = [0] + [o for k in range(1, count // 2) for o in (-k, k)] + [count // 2]
    relative = ring_places(count, me, offsets).astype(jnp.int32)
    wt_me = lax.axis_index("wt").astype(jnp.int32)
    scalars = jnp.concatenate(
        [
            jnp.stack([own, me, partner, starts[1], starts[2], wt_me]),
            by_block,
            order,
            relative,
        ]
    ).astype(jnp.int32)

    state = {"first": 0, "found": None, "seen": 0}

    def read_small(shares):
        small = jnp.stack([share[per:, : 2 * per] for share in shares[0]]).astype(F32)
        small = jnp.concatenate(
            [lax.dynamic_slice_in_dim(small, wt_me ^ n, 1, 0) for n in range(wt_count)], axis=0
        )
        gain_one = small[:, 0, :per].reshape(1, width)
        gain_two = small[:, 0, per:].reshape(1, width)
        mixes = small[:, mixes_at : mixes_at + mix_logit.shape[0], : 2 * heads].reshape(heads, 2 * heads)
        logit_mix, weight_mix = mixes[:, :heads], mixes[:, heads:]
        return gain_one, gain_two, logit_mix, weight_mix

    def work(rounds, shares, done=None):
        if done is not None:
            if done:
                *state["found"], state["mat"] = done
            return []
        if not state["seen"]:
            state["small"] = read_small(shares)
            state["mat"] = shares[0]
        batch = [piece for pieces in rounds[state["seen"] : -1] for _, piece in pieces]
        state["seen"] = len(rounds) - 1
        return project_batch(batch)

    def project_batch(batch):
        results = project(
            scalars, count, state["first"], batch, state["small"][0], state["mat"], state["found"]
        )
        state["first"] += len(batch)
        return [*results, state["mat"]][:7]

    rounds, shares, crossed = gather_all(x_own, stages, work)
    gain_one, gain_two, logit_mix, weight_mix = state["small"]
    qo_shares = shares[1]

    mix_by_g = jnp.repeat(logit_mix.T, size, axis=1)
    weight_by_g = jnp.repeat(weight_mix, size, axis=1)
    mix_rows = mix_by_g * (scale * LOG2E)
    spread = jnp.repeat(weight_mix.T, half, axis=1)
    logit_spread = jnp.repeat(logit_mix, half, axis=1)

    batch = [piece for pieces in rounds[state["seen"] :] for _, piece in pieces]
    k, v, kt, vt, nt, xg, kv_mat = project_batch(batch)
    xg, *crossed[len(shares) :] = tie(xg, *crossed[len(shares) :])
    q, x_low, query_mat = queries(scalars, xg, gain_one, qo_shares)
    x_low = x_low.reshape(rows, width)
    for n in range(len(shares), len(stages)):
        near = lax.ppermute(stages[n], "wt", swaps(wt_count, 1))
        both = lax.ppermute(crossed[n], "wt", swaps(wt_count, 1))
        q, near, both = lax.optimization_barrier((q, near, both))
        shares.append([stages[n], near, crossed[n], both])
    w_out, q = tie(w_out, q)
    far_out = lax.ppermute(w_out, "wt", swaps(wt_count, 2))
    near_out = lax.ppermute(w_out, "wt", swaps(wt_count, 1))

    def exchange(second):
        every = lax.all_gather(second, "ctx", axis=0)
        return lax.dynamic_index_in_dim(every, partner, 0, keepdims=False)

    dy_second, _ = lax.optimization_barrier((cotangent[0, half:], rounds[-1][0][1]))
    dy_low = jnp.concatenate([cotangent[0, :half], exchange(dy_second)], axis=0)

    attended, t, lse = attend(scalars, q, k, vt, mix_rows, spread, heads)
    far_out, attended = tie(far_out, attended)
    out_shares = [w_out, near_out, far_out, lax.ppermute(far_out, "wt", swaps(wt_count, 1))]
    out_low, grad_middle, grad_att, keep, send, grad_gain_two, squares = ffn(
        scalars, wt_count, heads, attended.reshape(rows, width), x_low, dy_low, gain_two,
        qo_shares, shares[2:], out_shares,
    )
    grad_att = grad_att.reshape(2, half, width)
    grad_middle = grad_middle.reshape(2, half, width)

    got = lax.ppermute(send, "wt", swaps(wt_count, 1))
    r_weight, delta = deltas(grad_att, t, spread, heads)
    summed = add(keep, got).reshape(2, count, -1, width).transpose(1, 0, 2, 3).reshape(-1, width)
    leaving = Spreading(out_low[half:], count)
    summed, delta, *moved = tie(summed, delta, *leaving.start())
    leaving.finish(*moved)
    summed = lax.psum_scatter(summed, "ctx", scatter_dimension=0, tiled=True)

    moved = leaving.start()
    dk, dv, dq, r_logit = back(
        scalars, 0, heads, q, grad_att, k, v, kt, lse, delta, mix_rows, weight_by_g,
        logit_spread, heads, scale,
    )

    def parts(first, batch, dk):
        return token_parts(
            scalars, first, batch, dk, dv, dq, xg, query_mat, kv_mat, gain_one, grad_middle
        )

    last = count // 2
    total = -(-(3 * per + TAIL_ROWS) // (8 * count)) * 8 * count
    dk, *moved = tie(dk, *moved)
    leaving.finish(*moved)
    moved = leaving.start()
    keep, send = weight_grads(
        scalars, wt_count, total, dk, dv, dq, nt, r_logit, r_weight, grad_gain_two, squares
    )
    send, dk, *moved = tie(send, dk, *moved)
    leaving.finish(*moved)
    near = lax.ppermute(send, "wt", swaps(wt_count, 1))
    far = parts(count - 1, 1, dk)
    near, far, summed, *moved = tie(near, far, summed, *leaving.start())
    leaving.finish(*moved)
    summed = summed.reshape(2, -1, width)
    ffn_far = lax.ppermute(summed[1], "wt", swaps(wt_count, 2))
    up, down = far_start(far[0])
    over = lax.ppermute(add(keep[1], near[1]), "wt", swaps(wt_count, 2))
    pair = parts(2 * (last - 1) - 1, 2, dk)
    up, down, pair, ffn_far = tie(up, down, pair, ffn_far)
    up, down = far_end(up, down)
    spread = Spreading(add(summed[0], ffn_far), count)

    turn = None
    for k in range(last - 1, 0, -1):
        up, down = ring_both(add(up, pair[1]), add(down, pair[0]))
        streams = [s for s in (spread, leaving) if not s.done]
        moved = [stream.start() for stream in streams]
        after = parts(2 * (k - 1) - 1, 2, dk) if k > 1 else parts(0, 1, dk)
        if turn is None:
            up, down, pair, moved, over = tie(up, down, after, moved, over)
            turn = Turning(add(keep[0], near[0], over).reshape(count, -1, width), me)
        else:
            if not turn.done:
                after, *both = tie(after, *turn.start())
                turn.finish(*both)
            both = [] if turn.done else turn.start()
            up, down, pair, moved, both = tie(up, down, after, moved, both)
            if both:
                turn.finish(*both)
        for stream, both in zip(streams, moved):
            stream.finish(*both)
    input_grad = add(up, down, pair[0])
    while not leaving.done:
        leaving.finish(*tie(*leaving.start()))
    order_places = jnp.where((partner & 1) == 0, partner >> 1, count - 1 - (partner >> 1))
    own_place = jnp.where((me & 1) == 0, me >> 1, count - 1 - (me >> 1))
    offset = (order_places - own_place) & (count - 1)
    second = leaving.pieces[1]
    for n in range(2, count):
        second = jnp.where(offset == n, leaving.pieces[n], second)
    output_own = jnp.concatenate([out_low[:half], second], axis=0)
    places = ring_places(count, me, list(range(count))).astype(jnp.int32)
    ffn_grads = None
    while not turn.done:
        moving = [] if spread.done else list(spread.start())
        one, two, *moving = tie(*turn.start(), *moving)
        turn.finish(one, two)
        if moving:
            spread.finish(*moving)
        elif ffn_grads is None:
            ffn_grads = unpack(places, spread.ordered(), (w_out.shape, w_in.shape, w_output.shape))
            turn_start = list(turn.start())
            one, two, *ffn_grads = tie(*turn_start, *ffn_grads)
            turn.finish(one, two)
    grad_out, grad_in, grad_o = ffn_grads
    entries = float(rows * width) * (count * wt_count)
    grad_q, grad_k, grad_v, gain_grad, gain_two_grad, logit_grad, weight_grad, rms = finish_grads(
        places, turn.spread.ordered(), w_query, w_key, w_value, gain_attn[None, :], entries, heads, heads // wt_count
    )
    return (
        output_own[None],
        input_grad[None],
        rms.reshape(3),
        gain_grad.reshape(per),
        grad_q,
        grad_k,
        grad_v,
        logit_grad,
        weight_grad,
        grad_o,
        gain_two_grad.reshape(per),
        grad_in,
        grad_out,
    )


def solution(mesh):
    tokens = P("wt", "ctx", None)
    matrix = P("wt", None)
    vector = P("wt")
    return jax.shard_map(
        shards,
        mesh=mesh,
        in_specs=(tokens, tokens, P(), matrix, vector)
        + (matrix,) * 6
        + (vector, matrix, matrix),
        out_specs=(tokens, tokens, P(), vector) + (matrix,) * 6 + (vector, matrix, matrix),
        check_vma=False,
    )
```

```python
import functools
import math

import jax
import jax.numpy as jnp
from jax import lax
from jax.experimental import pallas as pl
from jax.experimental.pallas import tpu as pltpu
from jax.sharding import PartitionSpec as P

NEG = -1e30
EPS = 1e-06
LOG2E = 1.4426950408889634
LN2 = 0.6931471805599453
F32 = jnp.float32
BF16 = jnp.bfloat16
NT = (((1,), (1,)), ((), ()))
VMEM_BYTES = 60 * 1024 * 1024


def dot(left, right):
    return jnp.dot(left, right, preferred_element_type=F32)


def dot_nt(left, right):
    return lax.dot_general(left, right, NT, preferred_element_type=F32)


def rms_norm(values, gain):
    return values * lax.rsqrt(jnp.mean(values * values, axis=-1, keepdims=True) + EPS) * gain


def gelu_tanh(values):
    return jax.nn.gelu(values, approximate=True)


def params(flops, moved, dims=1):
    return dict(
        compiler_params=pltpu.CompilerParams(
            dimension_semantics=("arbitrary",) * dims, vmem_limit_bytes=VMEM_BYTES
        ),
        cost_estimate=pl.CostEstimate(flops=flops, bytes_accessed=moved, transcendentals=0),
    )


HEAD = 6


def assemble(me, target, pieces, per, cols=slice(None)):
    for n, piece in enumerate(pieces):
        rows = pl.ds(pl.multiple_of((me ^ n) * per, per), per)
        target[rows, :] = piece[:per, cols]


def project_kernel(batch, shares, sc, *refs):
    pieces, (gain_ref, *weights) = refs[:batch], refs[batch : batch + 1 + max(1, len(shares))]
    outs = refs[-(4 if shares else 3) :]
    k_ref, v_ref, x_out = outs[:3]
    width = x_out.shape[2]
    mat = outs[3] if shares else weights[0]
    if shares:

        @pl.when(pl.program_id(0) == 0)
        def start():
            assemble(sc[5], mat, weights, width // len(weights))

    def one(x_ref):
        x_low = x_ref[...]
        x_out[0] = x_low
        normed = rms_norm(x_low.astype(F32), gain_ref[...]).astype(BF16)
        k_ref[0] = dot(normed, mat[:, :width]).astype(BF16)
        v_ref[0] = dot(normed, mat[:, width:]).astype(BF16)

    for n in range(batch):
        pl.when(pl.program_id(0) == n)(functools.partial(one, pieces[n]))


def project(scalars, count, first, pieces, gain, mat, before):
    batch = len(pieces)
    rows, width = pieces[0].shape
    place = lambda j, sc: (sc[HEAD + 2 * count + first + j], 0, 0)
    fixed = lambda j, sc: (0, 0)
    tall = jax.ShapeDtypeStruct((count, rows, width), BF16)
    once = pl.Buffered(1)
    before = () if before is None else tuple(before)
    shares = tuple(mat) if isinstance(mat, (list, tuple)) else ()
    weights = shares or (mat,)
    out_specs = [pl.BlockSpec((1, rows, width), place)] * 3
    out_shape = [tall] * 3
    if shares:
        out_specs.append(pl.BlockSpec((width, 2 * width), fixed, pipeline_mode=once))
        out_shape.append(jax.ShapeDtypeStruct((width, 2 * width), BF16))
    return pl.pallas_call(
        functools.partial(project_kernel, batch, shares),
        grid_spec=pltpu.PrefetchScalarGridSpec(
            num_scalar_prefetch=1,
            grid=(batch,),
            in_specs=[pl.BlockSpec((rows, width), fixed, pipeline_mode=once)] * batch
            + [pl.BlockSpec((1, width), fixed)]
            + [pl.BlockSpec(w.shape, fixed, pipeline_mode=once) for w in weights]
            + [pl.BlockSpec(memory_space=pl.ANY)] * len(before),
            out_specs=out_specs,
        ),
        out_shape=out_shape,
        input_output_aliases={batch + 2 + len(weights) + n: n for n in range(len(before))},
        **params(4 * batch * rows * width * width, 8 * batch * rows * width),
    )(scalars, *pieces, gain, *weights, *before)


def query_kernel(sc, x_ref, gain_ref, *refs):
    shares, (q_ref, x_out, mat) = refs[:-3], refs[-3:]

    @pl.when(pl.program_id(0) == 0)
    def start():
        assemble(sc[5], mat, shares, mat.shape[0] // len(shares), slice(0, mat.shape[1]))

    x_out[0] = x_ref[0]
    normed = rms_norm(x_ref[0].astype(F32), gain_ref[...]).astype(BF16)
    q_ref[0] = dot(normed, mat[...]).astype(BF16)


def queries(scalars, xg, gain, shares):
    count, rows, width = xg.shape
    half = rows // 2
    fixed = lambda n, sc: (0, 0)
    once = pl.Buffered(1)
    part = jax.ShapeDtypeStruct((2, half, width), BF16)
    return pl.pallas_call(
        query_kernel,
        grid_spec=pltpu.PrefetchScalarGridSpec(
            num_scalar_prefetch=1,
            grid=(2,),
            in_specs=[
                pl.BlockSpec((1, half, width), lambda n, sc: (sc[1 + n], n, 0)),
                pl.BlockSpec((1, width), fixed),
            ]
            + [pl.BlockSpec(w.shape, fixed, pipeline_mode=once) for w in shares],
            out_specs=[
                pl.BlockSpec((1, half, width), lambda n, sc: (n, 0, 0)),
                pl.BlockSpec((1, half, width), lambda n, sc: (n, 0, 0)),
                pl.BlockSpec((width, width), fixed, pipeline_mode=once),
            ],
        ),
        out_shape=[part, part, jax.ShapeDtypeStruct((width, width), BF16)],
        **params(2 * rows * width * width, 4 * width * width),
    )(scalars, xg, gain, *shares)


def doc_of(sc, place):
    return (place >= sc[3]).astype(jnp.int32) + (place >= sc[4]).astype(jnp.int32)


def set_bias(bias_s, sc, key_place, query_place):
    rows, twice = bias_s.shape
    half = twice // 2
    key_end, query_end = key_place + rows - 1, query_place + half - 1
    clear = (
        (key_end <= query_place)
        & (doc_of(sc, key_place) == doc_of(sc, query_end))
        & (doc_of(sc, key_end) == doc_of(sc, query_place))
        & (doc_of(sc, key_end) == doc_of(sc, query_end))
    )

    @pl.when(clear)
    def seen():
        bias_s[...] = jnp.zeros(bias_s.shape, F32)

    @pl.when(jnp.logical_not(clear))
    def mixed():
        key_pos = key_place + lax.broadcasted_iota(jnp.int32, (rows, 1), 0)
        lane = lax.broadcasted_iota(jnp.int32, (1, twice), 1)
        query_pos = query_place + jnp.where(lane >= half, lane - half, lane)
        visible = (key_pos <= query_pos) & (doc_of(sc, key_pos) == doc_of(sc, query_pos))
        bias_s[...] = jnp.where(visible, 0.0, NEG)


def fold(target, lead, source, mix_ref, heads, half):
    values = source.astype(F32)
    for g in range(heads):
        piece = (values * mix_ref[g : g + 1, :]).astype(BF16)
        if lead is None:
            target[g * half : (g + 1) * half, :] = piece
        else:
            target[lead, g * half : (g + 1) * half, :] = piece


def attend_kernel(
    count, heads, group, sc, q_ref, k_ref, v_ref, mix_ref, spread_ref,
    att_ref, t_ref, lse_ref, folded, total, top, norm, bias_s, mixed_s, ahead, vt_s,
):
    half, width = q_ref.shape[1], q_ref.shape[2]
    rows = k_ref.shape[1]
    step = pl.program_id(0)
    own = sc[0]
    first_half = step <= own
    tile = jnp.where(first_half, step, step - own - 1)
    query_place = jnp.where(first_half, own * rows, (count - 1 - own) * rows + half)

    @pl.when((step == 0) | (step == own + 1))
    def start():
        fold(folded, None, q_ref[0], mix_ref, heads, half)
        top[...] = jnp.full(top.shape, NEG, F32)
        norm[...] = jnp.zeros(norm.shape, F32)
        total[...] = jnp.zeros(total.shape, F32)

    set_bias(bias_s, sc, tile * rows, query_place)
    span = group * half
    chunks = [slice(c * span, (c + 1) * span) for c in range(heads // group)]
    vt_s[...] = v_ref[0].T
    ahead[0] = dot_nt(k_ref[0], folded[chunks[0], :])
    for c, cols in enumerate(chunks):
        if c + 1 < len(chunks):
            ahead[(c + 1) % 2] = dot_nt(k_ref[0], folded[chunks[c + 1], :])
        logits = ahead[c % 2] + jnp.concatenate([bias_s[...]] * (group // 2), axis=1)
        before = top[:, cols]
        after = jnp.maximum(before, jnp.max(logits, axis=0, keepdims=True))
        shrink = jnp.exp2(before - after)
        weights = jnp.exp2(logits - after)
        top[:, cols] = after
        norm[:, cols] = norm[:, cols] * shrink + jnp.sum(weights, axis=0, keepdims=True)
        total[:, cols] = total[:, cols] * shrink + dot(vt_s[...], weights.astype(BF16))

    @pl.when((step == own) | (step == count))
    def finish():
        lse_ref[0] = top[...] + jnp.log2(norm[...])
        norm[...] = 1.0 / norm[...]
        mix_all(
            total, spread_ref, mixed_s, half,
            lambda h, rows, cols: scale_out(total, norm, t_ref, rows, cols),
        )
        att_ref[0] = (mixed_s[:, :half] + mixed_s[:, half:]).T.astype(BF16)


def scale_out(total, norm, t_ref, rows, cols):
    scaled = total[rows, cols] * norm[:, cols]
    t_ref[0, rows, cols] = scaled.astype(BF16)
    return scaled


def mix_all(total, spread_ref, mixed_s, half, find):
    heads = spread_ref.shape[0]
    size = mixed_s.shape[0] // heads
    for h in range(heads):
        rows = slice(h * size, (h + 1) * size)
        found = jnp.zeros((size, 2 * half), F32)
        for p in range(spread_ref.shape[1] // (2 * half)):
            cols = slice(2 * p * half, (2 * p + 2) * half)
            found += find(h, rows, cols) * spread_ref[h : h + 1, cols]
        mixed_s[rows, :] = found


def attend(scalars, q, k, v, mix_rows, spread, heads):
    count, rows, width = k.shape
    half = q.shape[1]
    span = heads * half
    which = lambda s, sc: (jnp.where(s <= sc[0], 0, 1), 0, 0)
    tile = lambda s, sc: (sc[HEAD + jnp.where(s <= sc[0], s, s - sc[0] - 1)], 0, 0)
    fixed = lambda s, sc: (0, 0)
    group = math.gcd(heads, 4)
    return pl.pallas_call(
        functools.partial(attend_kernel, count, heads, group),
        grid_spec=pltpu.PrefetchScalarGridSpec(
            num_scalar_prefetch=1,
            grid=(count + 1,),
            in_specs=[
                pl.BlockSpec((1, half, width), which),
                pl.BlockSpec((1, rows, width), tile),
                pl.BlockSpec((1, rows, width), tile),
                pl.BlockSpec((heads, width), fixed),
                pl.BlockSpec((heads, span), fixed),
            ],
            out_specs=[
                pl.BlockSpec((1, half, width), which),
                pl.BlockSpec((1, width, span), which),
                pl.BlockSpec((1, 1, span), which),
            ],
            scratch_shapes=[
                pltpu.VMEM((span, width), BF16),
                pltpu.VMEM((width, span), F32),
                pltpu.VMEM((1, span), F32),
                pltpu.VMEM((1, span), F32),
                pltpu.VMEM((rows, 2 * half), F32),
                pltpu.VMEM((width, 2 * half), F32),
                pltpu.VMEM((2, rows, group * half), F32),
                pltpu.VMEM((width, rows), BF16),
            ],
        ),
        out_shape=[
            jax.ShapeDtypeStruct((2, half, width), BF16),
            jax.ShapeDtypeStruct((2, width, span), BF16),
            jax.ShapeDtypeStruct((2, 1, span), F32),
        ],
        **params(4 * (count + 1) * rows * span * width, 6 * count * rows * width),
    )(scalars, q, k, v, mix_rows, spread)


def pair_rows(left, right, heads):
    product = left * right
    size = product.shape[0] // heads
    return jnp.concatenate(
        [
            jnp.sum(product[h * size : (h + 1) * size, :], axis=0, keepdims=True)
            for h in range(heads)
        ],
        axis=0,
    )


def lanes_of(found, first, half, lanes=128):
    place = lax.broadcasted_iota(jnp.int32, (found.shape[0], lanes), 1)
    total = jnp.zeros((found.shape[0], lanes), F32)
    for n in range(found.shape[1] // half):
        piece = jnp.sum(found[:, n * half : (n + 1) * half], axis=1, keepdims=True)
        total = jnp.where(place == first + n, piece, total)
    return total


def delta_kernel(heads, grad_ref, t_ref, spread_ref, r_ref, delta_ref):
    half = grad_ref.shape[1]
    grad_t = grad_ref[0].astype(F32).T
    twice = jnp.concatenate([grad_t, grad_t], axis=1)
    sums = jnp.zeros(r_ref.shape, F32)
    for p in range(heads // 2):
        cols = slice(2 * p * half, (2 * p + 2) * half)
        found = pair_rows(twice, t_ref[0, :, cols].astype(F32), heads)
        sums += lanes_of(found, 2 * p, half)
        delta_ref[0, :, cols] = jnp.sum(found * spread_ref[:, cols], axis=0, keepdims=True)

    @pl.when(pl.program_id(0) == 0)
    def first():
        r_ref[...] = sums

    @pl.when(pl.program_id(0) == 1)
    def second():
        r_ref[...] += sums


def deltas(grad_att, t, spread, heads):
    _, half, width = grad_att.shape
    span = heads * half
    return pl.pallas_call(
        functools.partial(delta_kernel, heads),
        grid=(2,),
        in_specs=[
            pl.BlockSpec((1, half, width), lambda s: (s, 0, 0)),
            pl.BlockSpec((1, width, span), lambda s: (s, 0, 0)),
            pl.BlockSpec((heads, span), lambda s: (0, 0)),
        ],
        out_specs=[
            pl.BlockSpec((heads, 128), lambda s: (0, 0)),
            pl.BlockSpec((1, 1, span), lambda s: (s, 0, 0)),
        ],
        out_shape=[
            jax.ShapeDtypeStruct((heads, 128), F32),
            jax.ShapeDtypeStruct((2, 1, span), F32),
        ],
        **params(4 * width * span, 4 * width * span),
    )(grad_att, t, spread)


def back_place(step, own, count):
    low = jnp.minimum(own, count - 1 - own)
    both = step < 2 * (low + 1)
    tile = jnp.where(both, step // 2, step - low - 1)
    part = jnp.where(both, step % 2, jnp.where(own > count - 1 - own, 0, 1))
    return low, both, tile, part


def back_kernel(
    count, heads, base, group, scale, sc, q_ref, ga_ref, k_ref, v_ref, lse_ref, delta_ref,
    mix_ref, weight_ref, spread_ref, dk_ref, dv_ref, dq_ref, r_ref,
    fq, fa, total, dk_s, dv_s, bias_s, kt_s, mixed_s, twice_s, rows_s, ahead_l, ahead_p,
):
    half, width = q_ref.shape[1], q_ref.shape[2]
    rows = k_ref.shape[1]
    step = pl.program_id(0)
    own = sc[0]
    low, both, tile, part = back_place(step, own, count)
    query_place = jnp.where(part == 0, own * rows, (count - 1 - own) * rows + half)

    @pl.when(step == 0)
    def start():
        for n in range(2):
            q = q_ref[n].astype(F32)
            ga = ga_ref[n].astype(F32)
            for g in range(group):
                cols = slice(g * half, (g + 1) * half)
                fq[n, cols, :] = (q * mix_ref[base + g : base + g + 1, :]).astype(BF16)
                fa[n, cols, :] = (ga * weight_ref[base + g : base + g + 1, :]).astype(BF16)
        total[...] = jnp.zeros(total.shape, F32)

    @pl.when(jnp.logical_not(both) | (part == 0))
    def clear():
        dk_s[...] = jnp.zeros(dk_s.shape, F32)
        dv_s[...] = jnp.zeros(dv_s.shape, F32)

    set_bias(bias_s, sc, tile * rows, query_place)
    chunk = math.gcd(group, 4)
    chunks = [slice(c * chunk * half, (c + 1) * chunk * half) for c in range(group // chunk)]

    def look(c):
        ahead_l[c % 2] = dot_nt(k_ref[0], fq[part, chunks[c], :])
        ahead_p[c % 2] = dot_nt(v_ref[0], fa[part, chunks[c], :])

    kt_s[...] = k_ref[0].T
    look(0)
    for c, cols in enumerate(chunks):
        if c + 1 < len(chunks):
            look(c + 1)
        logits = ahead_l[c % 2] + jnp.concatenate([bias_s[...]] * (chunk // 2), axis=1)
        prob = jnp.exp2(logits - lse_ref[part, :, cols])
        grad_logits = (prob * (ahead_p[c % 2] - delta_ref[part, :, cols])).astype(BF16)
        dv_s[...] += dot(prob.astype(BF16), fa[part, cols, :])
        dk_s[...] += dot(grad_logits, fq[part, cols, :])
        total[part, :, cols] += dot(kt_s[...], grad_logits)

    @pl.when(jnp.logical_not(both) | (part == 1))
    def leave():
        dk_ref[0] = (dk_s[...] * LN2).astype(BF16)
        dv_ref[0] = dv_s[...].astype(BF16)

    @pl.when(step == count)
    def finish():
        sums = jnp.zeros(r_ref.shape, F32)
        size = width // heads
        for n in range(2):
            q_t = q_ref[n].astype(F32).T
            twice_s[...] = jnp.concatenate([q_t, q_t], axis=1)

            def find(h, rows, cols):
                piece = total[n, rows, cols]
                rows_s[h : h + 1, cols] = jnp.sum(piece * twice_s[rows, :], axis=0, keepdims=True)
                return piece

            mix_all(total, spread_ref, mixed_s, half, find)
            sums += lanes_of(rows_s[...], 0, half)
            dq_ref[n] = ((mixed_s[:, :half] + mixed_s[:, half:]).T * scale).astype(BF16)
        r_ref[...] = sums * scale


def back(
    scalars, base, group, q, grad_att, k, v, lse, delta, mix_rows, weight_rows, spread, heads, scale
):
    count, rows, width = k.shape
    half = q.shape[1]
    span = group * half
    tile = lambda s, sc: (sc[HEAD + back_place(s, sc[0], count)[2]], 0, 0)
    whole = lambda s, sc: (0, 0, 0)
    cut = lambda s, sc: (0, 0, base // group)
    fixed = lambda s, sc: (0, 0)
    once = pl.Buffered(1)
    return pl.pallas_call(
        functools.partial(back_kernel, count, heads, base, group, scale),
        grid_spec=pltpu.PrefetchScalarGridSpec(
            num_scalar_prefetch=1,
            grid=(count + 1,),
            in_specs=[
                pl.BlockSpec((2, half, width), whole, pipeline_mode=once),
                pl.BlockSpec((2, half, width), whole, pipeline_mode=once),
                pl.BlockSpec((1, rows, width), tile),
                pl.BlockSpec((1, rows, width), tile),
                pl.BlockSpec((2, 1, span), cut, pipeline_mode=once),
                pl.BlockSpec((2, 1, span), cut, pipeline_mode=once),
                pl.BlockSpec((heads, width), fixed),
                pl.BlockSpec((heads, width), fixed),
                pl.BlockSpec((heads, span), fixed),
            ],
            out_specs=[
                pl.BlockSpec((1, rows, width), tile),
                pl.BlockSpec((1, rows, width), tile),
                pl.BlockSpec((2, half, width), whole),
                pl.BlockSpec((heads, 128), fixed),
            ],
            scratch_shapes=[
                pltpu.VMEM((2, span, width), BF16),
                pltpu.VMEM((2, span, width), BF16),
                pltpu.VMEM((2, width, span), F32),
                pltpu.VMEM((rows, width), F32),
                pltpu.VMEM((rows, width), F32),
                pltpu.VMEM((rows, 2 * half), F32),
                pltpu.VMEM((width, rows), BF16),
                pltpu.VMEM((width, 2 * half), F32),
                pltpu.VMEM((width, 2 * half), F32),
                pltpu.VMEM((heads, span), F32),
                pltpu.VMEM((2, rows, math.gcd(group, 4) * half), F32),
                pltpu.VMEM((2, rows, math.gcd(group, 4) * half), F32),
            ],
        ),
        out_shape=[
            jax.ShapeDtypeStruct((count, rows, width), BF16),
            jax.ShapeDtypeStruct((count, rows, width), BF16),
            jax.ShapeDtypeStruct((2, half, width), BF16),
            jax.ShapeDtypeStruct((heads, 128), F32),
        ],
        **params(10 * (count + 1) * rows * span * width, 10 * count * rows * width),
    )(scalars, q, grad_att, k, v, lse, delta, mix_rows, weight_rows, spread)


def put(keep_ref, send_ref, place, rows, value):
    @pl.when(place % 2 == 0)
    def kept():
        keep_ref[place // 2, rows, :] = value

    @pl.when(place % 2 == 1)
    def sent():
        send_ref[place // 2, rows, :] = value


def norm_parts(x):
    inverse = lax.rsqrt(jnp.mean(x * x, axis=-1, keepdims=True) + EPS)
    return inverse, x * inverse


def norm_back(inverse, bare, grad, gain):
    gained = grad * gain
    return inverse * (gained - bare * jnp.mean(gained * bare, axis=-1, keepdims=True))


def ffn_kernel(wt_count, sc, att_ref, x_ref, dy_ref, gain_ref, *refs):
    n = wt_count
    halves = (len(refs) - 21) // n - 2
    chunks = 2 * halves
    groups = [refs[i * n : (i + 1) * n] for i in range(halves + 2)]
    wo_shares, win_shares, wout_shares = groups[0], groups[1:-1], groups[-1]
    (
        out_ref, gm_ref, gatt_ref, keep_ref, send_ref, gain_out, sq_ref,
        middle_s, low_s, low_t, feed_s, grad_s, wo_ref, win_buf, wout_buf, leave_out, leave_in, leave_o,
        wo_sem, in_sem, out_sem,
    ) = refs[(halves + 2) * n :]
    j = pl.program_id(0)
    me = sc[5]
    width = x_ref.shape[1]
    per = width // n
    slot = j % 2

    def share_rows(i):
        return pl.ds(pl.multiple_of((me ^ i) * per, per), per)

    def wo_copies():
        return [
            pltpu.make_async_copy(
                wo_shares[i].at[:, pl.ds(width, width)], wo_ref.at[share_rows(i), :], wo_sem.at[i]
            )
            for i in range(n)
        ]

    def in_copies(c):
        return [
            pltpu.make_async_copy(
                win_shares[c // 2][i].at[:, pl.ds(c % 2 * width, width)],
                win_buf.at[c % 2, share_rows(i), :],
                in_sem.at[c % 2, i],
            )
            for i in range(n)
        ]

    def outer_copy(c, i):
        return pltpu.make_async_copy(wout_shares[i], wout_buf.at[c % 2], in_sem.at[c % 2, n])

    def fetch(c):
        for copy in in_copies(c):
            copy.start()
        for i in range(n):
            pl.when((c ^ me) == i)(outer_copy(c, i).start)

    def arrive(c):
        for copy in in_copies(c):
            copy.wait()
        outer_copy(c, 0).wait()

    def leaving(source, place, first, sem):
        target = (keep_ref, send_ref)[place % 2]
        rows = pl.ds(first, source.shape[0])
        return pltpu.make_async_copy(source, target.at[rows, pl.ds(place // 2 * width, width)], sem)

    def depart(source, target, first, sem):
        for place in range(n):
            pl.when((target ^ me) == place)(leaving(source, place, first, sem).start)

    def outgoing(c):
        yield leave_out.at[c % 2], c, 0, out_sem.at[c % 2, n]
        for t in range(n):
            yield leave_in.at[c % 2, pl.ds(t * per, per), :], t, width + c * per, out_sem.at[c % 2, t]

    def gone(c):
        for source, _, first, sem in outgoing(c):
            leaving(source, 0, first, sem).wait()

    @pl.when(j == 0)
    def start():
        for copy in wo_copies():
            copy.start()
        fetch(0)
        for copy in wo_copies():
            copy.wait()

    for c in range(chunks):

        @pl.when(j == c)
        def move():
            if c + 1 < chunks:
                fetch(c + 1)
            if c >= 2:
                gone(c - 2)
            arrive(c)

    @pl.when(j == 0)
    def first():
        branch = dot(att_ref[...], wo_ref[...])
        middle = x_ref[...].astype(F32) + branch
        middle_s[...] = middle
        _, bare = norm_parts(middle)
        low = (bare * gain_ref[...]).astype(BF16)
        low_s[...] = low
        low_t[...] = low.T
        feed_s[...] = jnp.zeros(feed_s.shape, F32)
        grad_s[...] = jnp.zeros(grad_s.shape, F32)
        sq_ref[...] = jnp.zeros(sq_ref.shape, F32)
        sq_ref[1:2, :] = jnp.broadcast_to(jnp.sum(branch * branch).reshape(1, 1), (1, 128))

    dy = dy_ref[...]
    win, wout = win_buf[slot], wout_buf[slot]
    hidden = dot(low_s[...], win)
    grad_active = dot_nt(dy, wout)
    square = hidden * hidden
    inner = jnp.tanh(hidden * (0.7978845608028654 + 0.7978845608028654 * 0.044715 * square))
    half_one = 0.5 + 0.5 * inner
    active = (hidden * half_one).astype(BF16)
    slope = half_one + (0.5 * hidden) * (1.0 - inner * inner) * (
        0.7978845608028654 + 3.0 * 0.7978845608028654 * 0.044715 * square
    )
    grad_hidden = (grad_active * slope).astype(BF16)
    feed_s[...] += dot(active, wout)
    grad_s[...] += dot_nt(grad_hidden, win)
    leave_out[slot] = dot(active.T, dy).astype(BF16)
    leave_in[slot] = dot(low_t[...], grad_hidden).astype(BF16)

    for c in range(chunks):

        @pl.when(j == c)
        def part():
            for copy in outgoing(c):
                depart(*copy)

    @pl.when(j == chunks - 1)
    def finish():
        middle = middle_s[...]
        feed = feed_s[...]
        output = middle + feed
        out_ref[...] = output.astype(BF16)
        sq_ref[0:1, :] = jnp.broadcast_to(jnp.sum(output * output).reshape(1, 1), (1, 128))
        sq_ref[2:3, :] = jnp.broadcast_to(jnp.sum(feed * feed).reshape(1, 1), (1, 128))
        inverse, bare = norm_parts(middle)
        grad = grad_s[...]
        gain_out[...] = jnp.sum(grad * bare, axis=0, keepdims=True)
        grad_middle = dy.astype(F32) + norm_back(inverse, bare, grad, gain_ref[...])
        gm_ref[...] = grad_middle
        low = grad_middle.astype(BF16)
        leave_o[...] = dot(att_ref[...].T, low).astype(BF16)
        rows = width + per * chunks
        for t in range(n):
            depart(leave_o.at[pl.ds(t * per, per), :], t, rows, wo_sem.at[t])
        gatt_ref[...] = dot_nt(low, wo_ref[...]).astype(BF16)
        for c in range(max(chunks - 2, 0), chunks):
            gone(c)
        for t in range(n):
            leaving(leave_o.at[pl.ds(t * per, per), :], 0, rows, wo_sem.at[t]).wait()


def ffn(scalars, wt_count, sq_rows, att, x, dy, gain, wo, wins, wout):
    rows, width = x.shape
    chunks = 2 * len(wins)
    per = width // wt_count
    total = width + per * chunks + per
    fixed = lambda j, sc: (0, 0)
    once = pl.Buffered(1)
    shares = [*wo, *(share for win in wins for share in win), *wout]
    anywhere = pl.BlockSpec(memory_space=pl.ANY)
    square = pltpu.VMEM((width, width), BF16)
    squares = pltpu.VMEM((2, width, width), BF16)
    return pl.pallas_call(
        functools.partial(ffn_kernel, wt_count),
        grid_spec=pltpu.PrefetchScalarGridSpec(
            num_scalar_prefetch=1,
            grid=(chunks,),
            in_specs=[
                pl.BlockSpec((rows, width), fixed, pipeline_mode=once),
                pl.BlockSpec((rows, width), fixed, pipeline_mode=once),
                pl.BlockSpec((rows, width), fixed, pipeline_mode=once),
                pl.BlockSpec((1, width), fixed),
            ]
            + [anywhere] * len(shares),
            out_specs=[
                pl.BlockSpec((rows, width), fixed),
                pl.BlockSpec((rows, width), fixed),
                pl.BlockSpec((rows, width), fixed),
                anywhere,
                anywhere,
                pl.BlockSpec((1, width), fixed),
                pl.BlockSpec((sq_rows, 128), fixed),
            ],
            scratch_shapes=[
                pltpu.VMEM((rows, width), F32),
                pltpu.VMEM((rows, width), BF16),
                pltpu.VMEM((width, rows), BF16),
                pltpu.VMEM((rows, width), F32),
                pltpu.VMEM((rows, width), F32),
                square,
                squares,
                squares,
                squares,
                squares,
                square,
                pltpu.SemaphoreType.DMA((wt_count,)),
                pltpu.SemaphoreType.DMA((2, wt_count + 1)),
                pltpu.SemaphoreType.DMA((2, wt_count + 1)),
            ],
        ),
        out_shape=[
            jax.ShapeDtypeStruct((rows, width), BF16),
            jax.ShapeDtypeStruct((rows, width), F32),
            jax.ShapeDtypeStruct((rows, width), BF16),
            jax.ShapeDtypeStruct((total, wt_count // 2 * width), BF16),
            jax.ShapeDtypeStruct((total, wt_count // 2 * width), BF16),
            jax.ShapeDtypeStruct((1, width), F32),
            jax.ShapeDtypeStruct((sq_rows, 128), F32),
        ],
        **params(10 * chunks * rows * width * width + 6 * rows * width * width, 24 * width * width),
    )(scalars, att, x, dy, gain, *shares)


TAIL_ROWS = 16


def seen_by(sc, count, device):
    return sc[HEAD + count + device] <= jnp.maximum(sc[0], count - 1 - sc[0])


def weight_kernel(
    count, wt_count, sc, dk_ref, dv_ref, dq_ref, x_ref, gain_ref, rl_ref, rw_ref, gain_two_ref, sq_ref,
    keep_ref, send_ref, dwq, dwk, dwv, normed_t,
):
    rows, width = x_ref.shape[1:]
    half = rows // 2
    device = pl.program_id(0)
    me_wt = sc[5]

    @pl.when(device == 0)
    def start():
        dwq[...] = jnp.zeros(dwq.shape, F32)
        dwk[...] = jnp.zeros(dwk.shape, F32)
        dwv[...] = jnp.zeros(dwv.shape, F32)

    @pl.when(seen_by(sc, count, device))
    def seen():
        normed_t[...] = rms_norm(x_ref[0].astype(F32), gain_ref[...]).astype(BF16).T
        dwk[...] += dot(normed_t[...], dk_ref[0])
        dwv[...] += dot(normed_t[...], dv_ref[0])

    def queries(n):
        empty = jnp.zeros((half, width), BF16)
        both = [dq_ref[n], empty] if n == 0 else [empty, dq_ref[n]]
        dwq[...] += dot(normed_t[...], jnp.concatenate(both, axis=0))

    pl.when(device == sc[1])(functools.partial(queries, 0))
    pl.when(device == sc[2])(functools.partial(queries, 1))

    @pl.when(device == count - 1)
    def finish():
        per = width // wt_count

        def pad(value, lanes):
            empty = jnp.zeros((value.shape[0], lanes - value.shape[1]), F32)
            return jnp.concatenate([value, empty], axis=1)

        heads = rw_ref.shape[0]
        each = heads // wt_count
        square = jnp.concatenate([rw_ref[...], jnp.zeros((128 - heads, 128), F32)], axis=0).T
        below = keep_ref.shape[1] - 3 * per - TAIL_ROWS
        assert TAIL_ROWS >= 4 + 2 * each

        def tail(t):
            rows = [
                pad(gain_two_ref[:, t * per : (t + 1) * per], width),
                pad(sq_ref[0:3, :], width),
                pad(rl_ref[t * each : (t + 1) * each, :], width),
                pad(square[t * each : (t + 1) * each, :], width),
                jnp.zeros((TAIL_ROWS - 4 - 2 * each + below, width), F32),
            ]
            return jnp.concatenate(rows, axis=0).astype(BF16)

        for t in range(wt_count):
            cut = slice(t * per, (t + 1) * per)
            for n, total in enumerate((dwq, dwk, dwv)):
                put(keep_ref, send_ref, t ^ me_wt, slice(n * per, (n + 1) * per), total[cut, :].astype(BF16))
            put(keep_ref, send_ref, t ^ me_wt, slice(3 * per, keep_ref.shape[1]), tail(t))


def weight_grads(scalars, wt_count, total, dk, dv, dq, xg, gain, rl, rw, gain_two, sq):
    count, rows, width = dk.shape
    place = lambda j, sc: (j, 0, 0)
    fixed = lambda j, sc: (0, 0)
    whole = lambda j, sc: (0, 0, 0)
    once = pl.Buffered(1)
    share = jax.ShapeDtypeStruct((wt_count // 2, total, width), BF16)
    return pl.pallas_call(
        functools.partial(weight_kernel, count, wt_count),
        grid_spec=pltpu.PrefetchScalarGridSpec(
            num_scalar_prefetch=1,
            grid=(count,),
            in_specs=[
                pl.BlockSpec((1, rows, width), place),
                pl.BlockSpec((1, rows, width), place),
                pl.BlockSpec((2, rows // 2, width), whole, pipeline_mode=once),
                pl.BlockSpec((1, rows, width), place),
                pl.BlockSpec((1, width), fixed),
                pl.BlockSpec(rl.shape, fixed),
                pl.BlockSpec(rw.shape, fixed),
                pl.BlockSpec((1, width), fixed),
                pl.BlockSpec(sq.shape, fixed),
            ],
            out_specs=[
                pl.BlockSpec((wt_count // 2, total, width), whole),
                pl.BlockSpec((wt_count // 2, total, width), whole),
            ],
            scratch_shapes=[pltpu.VMEM((width, width), F32)] * 3 + [pltpu.VMEM((width, rows), BF16)],
        ),
        out_shape=[share, share],
        **params(4 * count * rows * width * width, 10 * count * rows * width),
    )(scalars, dk, dv, dq, xg, gain, rl, rw, gain_two, sq)


def token_kernel(
    count, first, sc, dk_ref, dv_ref, dq_ref, x_ref, wq_ref, mat_ref, gain_ref, gm_ref, part_ref
):
    rows, width = x_ref.shape[1:]
    half = rows // 2
    device = sc[HEAD + 2 * count + first + pl.program_id(0)]
    valid = seen_by(sc, count, device)

    @pl.when(valid)
    def seen():
        grad = dot_nt(dk_ref[0], mat_ref[:, :width]) + dot_nt(dv_ref[0], mat_ref[:, width:])
        inverse, bare = norm_parts(x_ref[0].astype(F32))
        part_ref[0] = norm_back(inverse, bare, grad, gain_ref[...]).astype(BF16)

    @pl.when(jnp.logical_not(valid))
    def unseen():
        part_ref[0] = jnp.zeros(part_ref.shape[1:], BF16)

    def queries(n):
        mine = slice(n * half, (n + 1) * half)
        grad = dot_nt(dq_ref[n], wq_ref[...])
        inverse, bare = norm_parts(x_ref[0, mine, :].astype(F32))
        found = norm_back(inverse, bare, grad, gain_ref[...]) + gm_ref[n]
        part_ref[0, mine, :] = (part_ref[0, mine, :].astype(F32) + found).astype(BF16)

    pl.when(device == sc[1])(functools.partial(queries, 0))
    pl.when(device == sc[2])(functools.partial(queries, 1))


def token_parts(scalars, first, batch, dk, dv, dq, xg, wq, mat, gain, gm):
    count, rows, width = xg.shape
    place = lambda j, sc: (sc[HEAD + 2 * count + first + j], 0, 0)
    fixed = lambda j, sc: (0, 0)
    whole = lambda j, sc: (0, 0, 0)
    once = pl.Buffered(1)
    return pl.pallas_call(
        functools.partial(token_kernel, count, first),
        grid_spec=pltpu.PrefetchScalarGridSpec(
            num_scalar_prefetch=1,
            grid=(batch,),
            in_specs=[
                pl.BlockSpec((1, rows, width), place),
                pl.BlockSpec((1, rows, width), place),
                pl.BlockSpec((2, rows // 2, width), whole, pipeline_mode=once),
                pl.BlockSpec((1, rows, width), place),
                pl.BlockSpec((width, width), fixed, pipeline_mode=once),
                pl.BlockSpec((width, 2 * width), fixed, pipeline_mode=once),
                pl.BlockSpec((1, width), fixed),
                pl.BlockSpec((2, rows // 2, width), whole, pipeline_mode=once),
            ],
            out_specs=pl.BlockSpec((1, rows, width), lambda j, sc: (j, 0, 0)),
        ),
        out_shape=jax.ShapeDtypeStruct((batch, rows, width), BF16),
        **params(4 * batch * rows * width * width, 8 * batch * rows * width),
    )(scalars, dk, dv, dq, xg, wq, mat, gain, gm)


def finish_kernel(entries, heads, sc, *refs):
    count = len(refs) - 13
    pieces, (wq_ref, wk_ref, wv_ref, own_ref), outs, whole = refs[:count], refs[count : count + 4], refs[-9:-1], refs[-1]
    dq_ref, dk_ref, dv_ref, gain_ref, two_ref, logit_ref, weight_ref, rms_ref = outs
    gather_rows(sc, pieces, whole)
    rows = wq_ref.shape[0]
    gain = jnp.zeros((rows, 1), F32)
    for n, (out, w) in enumerate(((dq_ref, wq_ref), (dk_ref, wk_ref), (dv_ref, wv_ref))):
        found = whole[n * rows : (n + 1) * rows, :]
        out[...] = found
        gain += jnp.sum(found * w[...].astype(F32), axis=1, keepdims=True)
    gain_ref[...] = jnp.broadcast_to(gain, (rows, 128)).T[0:1, :] / own_ref[...].astype(F32)
    tail = whole[3 * rows : 3 * rows + TAIL_ROWS, :]
    each = logit_ref.shape[0]
    two_ref[...] = tail[0:1, :rows]
    rms_ref[...] = jnp.sqrt(tail[1:4, 0:1] * (1.0 / entries))
    logit_ref[...] = tail[4 : 4 + each, :heads]
    weight_ref[...] = tail[4 + each : 4 + 2 * each, :heads]


def finish_grads(places, pieces, wq, wk, wv, gain, entries, heads, each):
    count = len(pieces)
    rows, width = wq.shape
    ins = [*pieces, wq, wk, wv, gain]
    shapes = [(rows, width)] * 3 + [(1, rows), (1, rows), (each, heads), (each, heads), (3, 1)]
    fixed = lambda i, sc: (0, 0)
    return pl.pallas_call(
        functools.partial(finish_kernel, entries, heads),
        grid_spec=pltpu.PrefetchScalarGridSpec(
            num_scalar_prefetch=1,
            grid=(1,),
            in_specs=[pl.BlockSpec(v.shape, fixed) for v in ins],
            out_specs=[pl.BlockSpec(v, fixed) for v in shapes],
            scratch_shapes=[pltpu.VMEM((count * pieces[0].shape[0], width), F32)],
        ),
        out_shape=[jax.ShapeDtypeStruct(v, F32) for v in shapes],
        **params(0, 12 * rows * width),
    )(places, *ins)


def gather_rows(sc, pieces, whole):
    per = pieces[0].shape[0]
    for n, piece in enumerate(pieces):
        whole[pl.ds(pl.multiple_of(sc[n] * per, 8), per), :] = piece[...].astype(F32)


def unpack_kernel(sc, *refs):
    pieces, (out_ref, in_ref, o_ref, whole) = refs[:-4], refs[-4:]
    gather_rows(sc, pieces, whole)
    rows, width = out_ref.shape
    per = o_ref.shape[0]
    out_ref[...] = whole[:rows, :]
    chunks = in_ref.shape[1] // width
    for n in range(chunks):
        in_ref[:, n * width : (n + 1) * width] = whole[rows + n * per : rows + (n + 1) * per, :]
    o_ref[...] = whole[rows + chunks * per :, :]


def unpack(places, pieces, shapes):
    total = len(pieces) * pieces[0].shape[0]
    width = pieces[0].shape[1]
    fixed = lambda i, sc: (0, 0)
    return pl.pallas_call(
        unpack_kernel,
        grid_spec=pltpu.PrefetchScalarGridSpec(
            num_scalar_prefetch=1,
            grid=(1,),
            in_specs=[pl.BlockSpec(v.shape, fixed) for v in pieces],
            out_specs=[pl.BlockSpec(v, fixed) for v in shapes],
            scratch_shapes=[pltpu.VMEM((total, width), F32)],
        ),
        out_shape=[jax.ShapeDtypeStruct(shape, F32) for shape in shapes],
        **params(0, 6 * total * width),
    )(places, *pieces)


def swaps(size, distance):
    return [(i, i ^ distance) for i in range(size)]


def ring_order(count):
    return [2 * p if p < count // 2 else 2 * (count - 1 - p) + 1 for p in range(count)]


def ring(count, step):
    order = ring_order(count)
    return [(order[p], order[(p + step) % count]) for p in range(count)]


def ring_places(count, me, offsets):
    place = jnp.where((me & 1) == 0, me >> 1, count - 1 - (me >> 1))
    p = (place + jnp.array(offsets, jnp.int32)) & (count - 1)
    return jnp.where(p < count // 2, 2 * p, 2 * (count - 1 - p) + 1)


def ring_both(up, down):
    count = lax.axis_size("ctx")
    return lax.ppermute(up, "ctx", ring(count, 1)), lax.ppermute(down, "ctx", ring(count, -1))


def tie(*values):
    return lax.optimization_barrier(values)


def gather_all(value, stages, work):
    count = lax.axis_size("ctx")
    size = lax.axis_size("wt")
    half = value.shape[0] // 2
    rounds = [[(0, value)]]
    up = down = value
    shares, crossed = [], []
    for k in range(1, count // 2 + 1):
        last = k == count // 2
        up, down = ring_both(up[:half], down[half:]) if last else ring_both(up, down)
        tied = []
        if 2 <= k <= len(stages) + 1:
            tied.append(lax.ppermute(stages[k - 2], "wt", swaps(size, 1)))
            tied.append(lax.ppermute(crossed[k - 2], "wt", swaps(size, 1)))
        if k <= len(stages):
            crossed.append(lax.ppermute(stages[k - 1], "wt", swaps(size, 2)))
            if not last:
                tied.append(crossed.pop())
        done = work(rounds, shares) if k >= 3 else []
        up, down, done, *tied = tie(up, down, done, *tied)
        if k >= 3:
            work(rounds, shares, done)
        if k <= len(stages) and not last:
            crossed.append(tied.pop())
        if tied:
            shares.append([stages[k - 2], tied[0], crossed[k - 2], tied[1]])
        rounds.append([(count // 2, jnp.concatenate([up, down], axis=0))] if last else [(-k, up), (k, down)])
    return rounds, shares, crossed


def add(*values):
    return sum(v.astype(F32) for v in values).astype(BF16)


def far_start(far):
    half = far.shape[0] // 2
    up, down = ring_both(far[:half], far[half:])
    return up, down


def far_end(up, down):
    empty = jnp.zeros(up.shape, BF16)
    return jnp.concatenate([up, empty], axis=0), jnp.concatenate([empty, down], axis=0)


class Spreading:
    def __init__(self, piece, count):
        self.count, self.last = count, count // 2
        self.up = self.down = piece
        self.pieces = {0: piece}
        self.step = 0

    @property
    def done(self):
        return self.step == self.last

    def start(self):
        if self.step < self.last - 1:
            return ring_both(self.up, self.down)
        half = self.up.shape[0] // 2
        return ring_both(self.up[:half], self.down[half:])

    def finish(self, up, down):
        self.step += 1
        if self.done:
            self.pieces[self.last] = jnp.concatenate([up, down], axis=0)
        else:
            self.pieces[self.count - self.step], self.pieces[self.step] = up, down
        self.up, self.down = up, down

    def ordered(self):
        return [self.pieces[n] for n in range(self.count)]


class Turning:
    def __init__(self, blocks, me):
        self.count, self.last = blocks.shape[0], blocks.shape[0] // 2
        self.blocks, self.me = blocks, me
        self.step = 0
        self.spread = None

    @property
    def done(self):
        return self.spread is not None and self.spread.done

    def at(self, offset):
        place = ring_places(self.count, self.me, [offset])[0]
        return lax.dynamic_index_in_dim(self.blocks, place, 0, keepdims=False)

    def start(self):
        step, last = self.step, self.last
        if self.spread is not None:
            return self.spread.start()
        if step == 0:
            return far_start(self.at(last))
        return ring_both(add(self.up, self.at(last - step)), add(self.down, self.at(step - last)))

    def finish(self, up, down):
        if self.spread is not None:
            return self.spread.finish(up, down)
        if self.step == 0:
            up, down = far_end(up, down)
        elif self.step == self.last - 1:
            self.spread = Spreading(add(up, down, self.at(0)), self.count)
        self.up, self.down = up, down
        self.step += 1


def shards(
    residual_in,
    cotangent,
    block_order,
    doc_starts,
    gain_attn,
    w_query,
    w_key,
    w_value,
    mix_logit,
    mix_weight,
    w_output,
    gain_ffn,
    w_in,
    w_out,
):
    rows, width = residual_in.shape[1:]
    half = rows // 2
    heads = mix_logit.shape[1]
    size = width // heads
    scale = size ** (-0.5)
    count = lax.axis_size("ctx")
    me = lax.axis_index("ctx").astype(jnp.int32)
    wt_count = lax.axis_size("wt")
    starts = doc_starts[0]

    per = gain_attn.shape[0]
    across = lambda v, n: jnp.pad(v, ((0, n - v.shape[0]), (0, 2 * width - v.shape[1])))
    gains = jnp.concatenate([gain_attn, gain_ffn])[None, :]
    mixes_at = 8
    small = jnp.concatenate(
        [across(gains, mixes_at), across(jnp.concatenate([mix_logit, mix_weight], axis=1), mixes_at)], axis=0
    )
    kv_own = jnp.concatenate([jnp.concatenate([w_key, w_value], axis=1), small], axis=0)
    x_own = residual_in[0]
    stages = [kv_own, jnp.concatenate([w_query, w_output], axis=1)]
    stages += [w_in[:, n : n + 2 * width] for n in range(0, w_in.shape[1], 2 * width)]
    order = block_order.astype(jnp.int32)
    devices = jnp.arange(count, dtype=jnp.int32)
    by_block = jnp.sum(jnp.where(order[None, :] == devices[:, None], devices[None, :], 0), axis=1)
    own = order[me]
    partner = by_block[count - 1 - own]
    offsets = [0] + [o for k in range(1, count // 2) for o in (-k, k)] + [count // 2]
    relative = ring_places(count, me, offsets).astype(jnp.int32)
    wt_me = lax.axis_index("wt").astype(jnp.int32)
    scalars = jnp.concatenate(
        [
            jnp.stack([own, me, partner, starts[1], starts[2], wt_me]),
            by_block,
            order,
            relative,
        ]
    ).astype(jnp.int32)

    state = {"first": 0, "found": None, "seen": 0}

    def read_small(shares):
        small = jnp.stack([share[per:, : 2 * per] for share in shares[0]]).astype(F32)
        small = jnp.concatenate(
            [lax.dynamic_slice_in_dim(small, wt_me ^ n, 1, 0) for n in range(wt_count)], axis=0
        )
        gain_one = small[:, 0, :per].reshape(1, width)
        gain_two = small[:, 0, per:].reshape(1, width)
        mixes = small[:, mixes_at : mixes_at + mix_logit.shape[0], : 2 * heads].reshape(heads, 2 * heads)
        logit_mix, weight_mix = mixes[:, :heads], mixes[:, heads:]
        return gain_one, gain_two, logit_mix, weight_mix

    def work(rounds, shares, done=None):
        if done is not None:
            if done:
                *state["found"], state["mat"] = done
            return []
        if not state["seen"]:
            state["small"] = read_small(shares)
            state["mat"] = shares[0]
        batch = [piece for pieces in rounds[state["seen"] : -1] for _, piece in pieces]
        state["seen"] = len(rounds) - 1
        return project_batch(batch)

    def project_batch(batch):
        results = project(
            scalars, count, state["first"], batch, state["small"][0], state["mat"], state["found"]
        )
        state["first"] += len(batch)
        return [*results, state["mat"]][:4]

    rounds, shares, crossed = gather_all(x_own, stages, work)
    gain_one, gain_two, logit_mix, weight_mix = state["small"]
    qo_shares = shares[1]

    mix_by_g = jnp.repeat(logit_mix.T, size, axis=1)
    weight_by_g = jnp.repeat(weight_mix, size, axis=1)
    mix_rows = mix_by_g * (scale * LOG2E)
    spread = jnp.repeat(weight_mix.T, half, axis=1)
    logit_spread = jnp.repeat(logit_mix, half, axis=1)

    batch = [piece for pieces in rounds[state["seen"] :] for _, piece in pieces]
    k, v, xg, kv_mat = project_batch(batch)
    xg, *crossed[len(shares) :] = tie(xg, *crossed[len(shares) :])
    q, x_low, query_mat = queries(scalars, xg, gain_one, qo_shares)
    x_low = x_low.reshape(rows, width)
    for n in range(len(shares), len(stages)):
        near = lax.ppermute(stages[n], "wt", swaps(wt_count, 1))
        both = lax.ppermute(crossed[n], "wt", swaps(wt_count, 1))
        q, near, both = lax.optimization_barrier((q, near, both))
        shares.append([stages[n], near, crossed[n], both])
    w_out, q = tie(w_out, q)
    far_out = lax.ppermute(w_out, "wt", swaps(wt_count, 2))
    near_out = lax.ppermute(w_out, "wt", swaps(wt_count, 1))

    def exchange(second):
        every = lax.all_gather(second, "ctx", axis=0)
        return lax.dynamic_index_in_dim(every, partner, 0, keepdims=False)

    dy_second, _ = lax.optimization_barrier((cotangent[0, half:], rounds[-1][0][1]))
    dy_low = jnp.concatenate([cotangent[0, :half], exchange(dy_second)], axis=0)

    attended, t, lse = attend(scalars, q, k, v, mix_rows, spread, heads)
    far_out, attended = tie(far_out, attended)
    out_shares = [w_out, near_out, far_out, lax.ppermute(far_out, "wt", swaps(wt_count, 1))]
    out_low, grad_middle, grad_att, keep, send, grad_gain_two, squares = ffn(
        scalars, wt_count, heads, attended.reshape(rows, width), x_low, dy_low, gain_two,
        qo_shares, shares[2:], out_shares,
    )
    grad_att = grad_att.reshape(2, half, width)
    grad_middle = grad_middle.reshape(2, half, width)

    got = lax.ppermute(send, "wt", swaps(wt_count, 1))
    r_weight, delta = deltas(grad_att, t, spread, heads)
    summed = add(keep, got)
    leaving = Spreading(out_low[half:], count)
    summed, delta, *moved = tie(summed, delta, *leaving.start())
    leaving.finish(*moved)
    summed = lax.psum_scatter(summed, "ctx", scatter_dimension=0, tiled=True)

    moved = leaving.start()
    dk, dv, dq, r_logit = back(
        scalars, 0, heads, q, grad_att, k, v, lse, delta, mix_rows, weight_by_g,
        logit_spread, heads, scale,
    )

    def parts(first, batch, dk):
        return token_parts(
            scalars, first, batch, dk, dv, dq, xg, query_mat, kv_mat, gain_one, grad_middle
        )

    last = count // 2
    total = -(-(3 * per + TAIL_ROWS) // (8 * count)) * 8 * count
    dk, *moved = tie(dk, *moved)
    leaving.finish(*moved)
    moved = leaving.start()
    keep, send = weight_grads(
        scalars, wt_count, total, dk, dv, dq, xg, gain_one, r_logit, r_weight, grad_gain_two, squares
    )
    send, dk, *moved = tie(send, dk, *moved)
    leaving.finish(*moved)
    near = lax.ppermute(send, "wt", swaps(wt_count, 1))
    far = parts(count - 1, 1, dk)
    near, far, summed, *moved = tie(near, far, summed, *leaving.start())
    leaving.finish(*moved)
    ffn_far = lax.ppermute(summed[:, width:], "wt", swaps(wt_count, 2))
    up, down = far_start(far[0])
    over = lax.ppermute(add(keep[1], near[1]), "wt", swaps(wt_count, 2))
    pair = parts(2 * (last - 1) - 1, 2, dk)
    up, down, pair, ffn_far = tie(up, down, pair, ffn_far)
    up, down = far_end(up, down)
    spread = Spreading(add(summed[:, :width], ffn_far), count)

    turn = None
    for k in range(last - 1, 0, -1):
        up, down = ring_both(add(up, pair[1]), add(down, pair[0]))
        streams = [s for s in (spread, leaving) if not s.done]
        moved = [stream.start() for stream in streams]
        after = parts(2 * (k - 1) - 1, 2, dk) if k > 1 else parts(0, 1, dk)
        if turn is None:
            up, down, pair, moved, over = tie(up, down, after, moved, over)
            turn = Turning(add(keep[0], near[0], over).reshape(count, -1, width), me)
        else:
            if not turn.done:
                after, *both = tie(after, *turn.start())
                turn.finish(*both)
            both = [] if turn.done else turn.start()
            up, down, pair, moved, both = tie(up, down, after, moved, both)
            if both:
                turn.finish(*both)
        for stream, both in zip(streams, moved):
            stream.finish(*both)
    input_grad = add(up, down, pair[0])
    while not leaving.done:
        leaving.finish(*tie(*leaving.start()))
    order_places = jnp.where((partner & 1) == 0, partner >> 1, count - 1 - (partner >> 1))
    own_place = jnp.where((me & 1) == 0, me >> 1, count - 1 - (me >> 1))
    offset = (order_places - own_place) & (count - 1)
    second = leaving.pieces[1]
    for n in range(2, count):
        second = jnp.where(offset == n, leaving.pieces[n], second)
    output_own = jnp.concatenate([out_low[:half], second], axis=0)
    places = ring_places(count, me, list(range(count))).astype(jnp.int32)
    ffn_grads = None
    while not turn.done:
        moving = [] if spread.done else list(spread.start())
        one, two, *moving = tie(*turn.start(), *moving)
        turn.finish(one, two)
        if moving:
            spread.finish(*moving)
        elif ffn_grads is None:
            ffn_grads = unpack(places, spread.ordered(), (w_out.shape, w_in.shape, w_output.shape))
            turn_start = list(turn.start())
            one, two, *ffn_grads = tie(*turn_start, *ffn_grads)
            turn.finish(one, two)
    grad_out, grad_in, grad_o = ffn_grads
    entries = float(rows * width) * (count * wt_count)
    grad_q, grad_k, grad_v, gain_grad, gain_two_grad, logit_grad, weight_grad, rms = finish_grads(
        places, turn.spread.ordered(), w_query, w_key, w_value, gain_attn[None, :], entries, heads, heads // wt_count
    )
    return (
        output_own[None],
        input_grad[None],
        rms.reshape(3),
        gain_grad.reshape(per),
        grad_q,
        grad_k,
        grad_v,
        logit_grad,
        weight_grad,
        grad_o,
        gain_two_grad.reshape(per),
        grad_in,
        grad_out,
    )


def solution(mesh):
    tokens = P("wt", "ctx", None)
    matrix = P("wt", None)
    vector = P("wt")
    return jax.shard_map(
        shards,
        mesh=mesh,
        in_specs=(tokens, tokens, P(), matrix, vector)
        + (matrix,) * 6
        + (vector, matrix, matrix),
        out_specs=(tokens, tokens, P(), vector) + (matrix,) * 6 + (vector, matrix, matrix),
        check_vma=False,
    )
```

```python
import functools
import math

import jax
import jax.numpy as jnp
from jax import lax
from jax.experimental import pallas as pl
from jax.experimental.pallas import tpu as pltpu
from jax.sharding import PartitionSpec as P

NEG = -1e30
EPS = 1e-06
LOG2E = 1.4426950408889634
LN2 = 0.6931471805599453
F32 = jnp.float32
BF16 = jnp.bfloat16
NT = (((1,), (1,)), ((), ()))
VMEM_BYTES = 60 * 1024 * 1024


def dot(left, right):
    return jnp.dot(left, right, preferred_element_type=F32)


def dot_nt(left, right):
    return lax.dot_general(left, right, NT, preferred_element_type=F32)


def rms_norm(values, gain):
    return values * lax.rsqrt(jnp.mean(values * values, axis=-1, keepdims=True) + EPS) * gain


def gelu_tanh(values):
    return jax.nn.gelu(values, approximate=True)


def params(flops, moved, dims=1):
    return dict(
        compiler_params=pltpu.CompilerParams(
            dimension_semantics=("arbitrary",) * dims, vmem_limit_bytes=VMEM_BYTES
        ),
        cost_estimate=pl.CostEstimate(flops=flops, bytes_accessed=moved, transcendentals=0),
    )


HEAD = 6


def assemble(me, target, pieces, per, cols=slice(None)):
    for n, piece in enumerate(pieces):
        rows = pl.ds(pl.multiple_of((me ^ n) * per, per), per)
        target[rows, :] = piece[:per, cols]


def project_kernel(batch, shares, sc, *refs):
    pieces, (gain_ref, *weights) = refs[:batch], refs[batch : batch + 1 + max(1, len(shares))]
    outs = refs[-(4 if shares else 3) :]
    k_ref, v_ref, x_out = outs[:3]
    width = x_out.shape[2]
    mat = outs[3] if shares else weights[0]
    if shares:

        @pl.when(pl.program_id(0) == 0)
        def start():
            assemble(sc[5], mat, weights, width // len(weights))

    def one(x_ref):
        x_low = x_ref[...]
        x_out[0] = x_low
        normed = rms_norm(x_low.astype(F32), gain_ref[...]).astype(BF16)
        k_ref[0] = dot(normed, mat[:, :width]).astype(BF16)
        v_ref[0] = dot(normed, mat[:, width:]).astype(BF16)

    for n in range(batch):
        pl.when(pl.program_id(0) == n)(functools.partial(one, pieces[n]))


def project(scalars, count, first, pieces, gain, mat, before):
    batch = len(pieces)
    rows, width = pieces[0].shape
    place = lambda j, sc: (sc[HEAD + 2 * count + first + j], 0, 0)
    fixed = lambda j, sc: (0, 0)
    tall = jax.ShapeDtypeStruct((count, rows, width), BF16)
    once = pl.Buffered(1)
    before = () if before is None else tuple(before)
    shares = tuple(mat) if isinstance(mat, (list, tuple)) else ()
    weights = shares or (mat,)
    out_specs = [pl.BlockSpec((1, rows, width), place)] * 3
    out_shape = [tall] * 3
    if shares:
        out_specs.append(pl.BlockSpec((width, 2 * width), fixed, pipeline_mode=once))
        out_shape.append(jax.ShapeDtypeStruct((width, 2 * width), BF16))
    return pl.pallas_call(
        functools.partial(project_kernel, batch, shares),
        grid_spec=pltpu.PrefetchScalarGridSpec(
            num_scalar_prefetch=1,
            grid=(batch,),
            in_specs=[pl.BlockSpec((rows, width), fixed, pipeline_mode=once)] * batch
            + [pl.BlockSpec((1, width), fixed)]
            + [pl.BlockSpec(w.shape, fixed, pipeline_mode=once) for w in weights]
            + [pl.BlockSpec(memory_space=pl.ANY)] * len(before),
            out_specs=out_specs,
        ),
        out_shape=out_shape,
        input_output_aliases={batch + 2 + len(weights) + n: n for n in range(len(before))},
        **params(4 * batch * rows * width * width, 8 * batch * rows * width),
    )(scalars, *pieces, gain, *weights, *before)


def query_kernel(sc, x_ref, gain_ref, *refs):
    shares, (q_ref, x_out, mat) = refs[:-3], refs[-3:]

    @pl.when(pl.program_id(0) == 0)
    def start():
        assemble(sc[5], mat, shares, mat.shape[0] // len(shares), slice(0, mat.shape[1]))

    x_out[0] = x_ref[0]
    normed = rms_norm(x_ref[0].astype(F32), gain_ref[...]).astype(BF16)
    q_ref[0] = dot(normed, mat[...]).astype(BF16)


def queries(scalars, xg, gain, shares):
    count, rows, width = xg.shape
    half = rows // 2
    fixed = lambda n, sc: (0, 0)
    once = pl.Buffered(1)
    part = jax.ShapeDtypeStruct((2, half, width), BF16)
    return pl.pallas_call(
        query_kernel,
        grid_spec=pltpu.PrefetchScalarGridSpec(
            num_scalar_prefetch=1,
            grid=(2,),
            in_specs=[
                pl.BlockSpec((1, half, width), lambda n, sc: (sc[1 + n], n, 0)),
                pl.BlockSpec((1, width), fixed),
            ]
            + [pl.BlockSpec(w.shape, fixed, pipeline_mode=once) for w in shares],
            out_specs=[
                pl.BlockSpec((1, half, width), lambda n, sc: (n, 0, 0)),
                pl.BlockSpec((1, half, width), lambda n, sc: (n, 0, 0)),
                pl.BlockSpec((width, width), fixed, pipeline_mode=once),
            ],
        ),
        out_shape=[part, part, jax.ShapeDtypeStruct((width, width), BF16)],
        **params(2 * rows * width * width, 4 * width * width),
    )(scalars, xg, gain, *shares)


def doc_of(sc, place):
    return (place >= sc[3]).astype(jnp.int32) + (place >= sc[4]).astype(jnp.int32)


def set_bias(bias_s, sc, key_place, query_place):
    rows, twice = bias_s.shape
    half = twice // 2
    key_end, query_end = key_place + rows - 1, query_place + half - 1
    clear = (
        (key_end <= query_place)
        & (doc_of(sc, key_place) == doc_of(sc, query_end))
        & (doc_of(sc, key_end) == doc_of(sc, query_place))
        & (doc_of(sc, key_end) == doc_of(sc, query_end))
    )

    @pl.when(clear)
    def seen():
        bias_s[...] = jnp.zeros(bias_s.shape, F32)

    @pl.when(jnp.logical_not(clear))
    def mixed():
        key_pos = key_place + lax.broadcasted_iota(jnp.int32, (rows, 1), 0)
        lane = lax.broadcasted_iota(jnp.int32, (1, twice), 1)
        query_pos = query_place + jnp.where(lane >= half, lane - half, lane)
        visible = (key_pos <= query_pos) & (doc_of(sc, key_pos) == doc_of(sc, query_pos))
        bias_s[...] = jnp.where(visible, 0.0, NEG)


def fold(target, lead, source, mix_ref, heads, half):
    values = source.astype(F32)
    for g in range(heads):
        piece = (values * mix_ref[g : g + 1, :]).astype(BF16)
        if lead is None:
            target[g * half : (g + 1) * half, :] = piece
        else:
            target[lead, g * half : (g + 1) * half, :] = piece


def attend_kernel(
    count, heads, group, sc, q_ref, k_ref, v_ref, mix_ref, spread_ref,
    att_ref, t_ref, lse_ref, folded, total, top, norm, bias_s, mixed_s, ahead, vt_s,
):
    half, width = q_ref.shape[1], q_ref.shape[2]
    rows = k_ref.shape[1]
    step = pl.program_id(0)
    own = sc[0]
    first_half = step <= own
    tile = jnp.where(first_half, step, step - own - 1)
    query_place = jnp.where(first_half, own * rows, (count - 1 - own) * rows + half)

    @pl.when((step == 0) | (step == own + 1))
    def start():
        fold(folded, None, q_ref[0], mix_ref, heads, half)
        top[...] = jnp.full(top.shape, NEG, F32)
        norm[...] = jnp.zeros(norm.shape, F32)
        total[...] = jnp.zeros(total.shape, F32)

    set_bias(bias_s, sc, tile * rows, query_place)
    span = group * half
    chunks = [slice(c * span, (c + 1) * span) for c in range(heads // group)]
    vt_s[...] = v_ref[0].T
    ahead[0] = dot_nt(k_ref[0], folded[chunks[0], :])
    for c, cols in enumerate(chunks):
        if c + 1 < len(chunks):
            ahead[(c + 1) % 2] = dot_nt(k_ref[0], folded[chunks[c + 1], :])
        logits = ahead[c % 2] + jnp.concatenate([bias_s[...]] * (group // 2), axis=1)
        before = top[:, cols]
        after = jnp.maximum(before, jnp.max(logits, axis=0, keepdims=True))
        shrink = jnp.exp2(before - after)
        weights = jnp.exp2(logits - after)
        top[:, cols] = after
        norm[:, cols] = norm[:, cols] * shrink + jnp.sum(weights, axis=0, keepdims=True)
        total[:, cols] = total[:, cols] * shrink + dot(vt_s[...], weights.astype(BF16))

    @pl.when((step == own) | (step == count))
    def finish():
        lse_ref[0] = top[...] + jnp.log2(norm[...])
        norm[...] = 1.0 / norm[...]
        mix_all(
            total, spread_ref, mixed_s, half,
            lambda h, rows, cols: scale_out(total, norm, t_ref, rows, cols),
        )
        att_ref[0] = (mixed_s[:, :half] + mixed_s[:, half:]).T.astype(BF16)


def scale_out(total, norm, t_ref, rows, cols):
    scaled = total[rows, cols] * norm[:, cols]
    t_ref[0, rows, cols] = scaled.astype(BF16)
    return scaled


def mix_all(total, spread_ref, mixed_s, half, find):
    heads = spread_ref.shape[0]
    size = mixed_s.shape[0] // heads
    for h in range(heads):
        rows = slice(h * size, (h + 1) * size)
        found = jnp.zeros((size, 2 * half), F32)
        for p in range(spread_ref.shape[1] // (2 * half)):
            cols = slice(2 * p * half, (2 * p + 2) * half)
            found += find(h, rows, cols) * spread_ref[h : h + 1, cols]
        mixed_s[rows, :] = found


def attend(scalars, q, k, v, mix_rows, spread, heads):
    count, rows, width = k.shape
    half = q.shape[1]
    span = heads * half
    which = lambda s, sc: (jnp.where(s <= sc[0], 0, 1), 0, 0)
    tile = lambda s, sc: (sc[HEAD + jnp.where(s <= sc[0], s, s - sc[0] - 1)], 0, 0)
    fixed = lambda s, sc: (0, 0)
    group = math.gcd(heads, 4)
    return pl.pallas_call(
        functools.partial(attend_kernel, count, heads, group),
        grid_spec=pltpu.PrefetchScalarGridSpec(
            num_scalar_prefetch=1,
            grid=(count + 1,),
            in_specs=[
                pl.BlockSpec((1, half, width), which),
                pl.BlockSpec((1, rows, width), tile),
                pl.BlockSpec((1, rows, width), tile),
                pl.BlockSpec((heads, width), fixed),
                pl.BlockSpec((heads, span), fixed),
            ],
            out_specs=[
                pl.BlockSpec((1, half, width), which),
                pl.BlockSpec((1, width, span), which),
                pl.BlockSpec((1, 1, span), which),
            ],
            scratch_shapes=[
                pltpu.VMEM((span, width), BF16),
                pltpu.VMEM((width, span), F32),
                pltpu.VMEM((1, span), F32),
                pltpu.VMEM((1, span), F32),
                pltpu.VMEM((rows, 2 * half), F32),
                pltpu.VMEM((width, 2 * half), F32),
                pltpu.VMEM((2, rows, group * half), F32),
                pltpu.VMEM((width, rows), BF16),
            ],
        ),
        out_shape=[
            jax.ShapeDtypeStruct((2, half, width), BF16),
            jax.ShapeDtypeStruct((2, width, span), BF16),
            jax.ShapeDtypeStruct((2, 1, span), F32),
        ],
        **params(4 * (count + 1) * rows * span * width, 6 * count * rows * width),
    )(scalars, q, k, v, mix_rows, spread)


def pair_rows(left, right, heads):
    product = left * right
    size = product.shape[0] // heads
    return jnp.concatenate(
        [
            jnp.sum(product[h * size : (h + 1) * size, :], axis=0, keepdims=True)
            for h in range(heads)
        ],
        axis=0,
    )


def lanes_of(found, first, half, lanes=128):
    place = lax.broadcasted_iota(jnp.int32, (found.shape[0], lanes), 1)
    total = jnp.zeros((found.shape[0], lanes), F32)
    for n in range(found.shape[1] // half):
        piece = jnp.sum(found[:, n * half : (n + 1) * half], axis=1, keepdims=True)
        total = jnp.where(place == first + n, piece, total)
    return total


def delta_kernel(heads, grad_ref, t_ref, spread_ref, r_ref, delta_ref):
    half = grad_ref.shape[1]
    grad_t = grad_ref[0].astype(F32).T
    twice = jnp.concatenate([grad_t, grad_t], axis=1)
    sums = jnp.zeros(r_ref.shape, F32)
    for p in range(heads // 2):
        cols = slice(2 * p * half, (2 * p + 2) * half)
        found = pair_rows(twice, t_ref[0, :, cols].astype(F32), heads)
        sums += lanes_of(found, 2 * p, half)
        delta_ref[0, :, cols] = jnp.sum(found * spread_ref[:, cols], axis=0, keepdims=True)

    @pl.when(pl.program_id(0) == 0)
    def first():
        r_ref[...] = sums

    @pl.when(pl.program_id(0) == 1)
    def second():
        r_ref[...] += sums


def deltas(grad_att, t, spread, heads):
    _, half, width = grad_att.shape
    span = heads * half
    return pl.pallas_call(
        functools.partial(delta_kernel, heads),
        grid=(2,),
        in_specs=[
            pl.BlockSpec((1, half, width), lambda s: (s, 0, 0)),
            pl.BlockSpec((1, width, span), lambda s: (s, 0, 0)),
            pl.BlockSpec((heads, span), lambda s: (0, 0)),
        ],
        out_specs=[
            pl.BlockSpec((heads, 128), lambda s: (0, 0)),
            pl.BlockSpec((1, 1, span), lambda s: (s, 0, 0)),
        ],
        out_shape=[
            jax.ShapeDtypeStruct((heads, 128), F32),
            jax.ShapeDtypeStruct((2, 1, span), F32),
        ],
        **params(4 * width * span, 4 * width * span),
    )(grad_att, t, spread)


def back_place(step, own, count):
    low = jnp.minimum(own, count - 1 - own)
    both = step < 2 * (low + 1)
    tile = jnp.where(both, step // 2, step - low - 1)
    part = jnp.where(both, step % 2, jnp.where(own > count - 1 - own, 0, 1))
    return low, both, tile, part


def back_kernel(
    count, heads, base, group, scale, sc, q_ref, ga_ref, k_ref, v_ref, lse_ref, delta_ref,
    mix_ref, weight_ref, spread_ref, dk_ref, dv_ref, dq_ref, r_ref,
    fq, fa, total, dk_s, dv_s, bias_s, kt_s, mixed_s, twice_s, rows_s, ahead_l, ahead_p,
):
    half, width = q_ref.shape[1], q_ref.shape[2]
    rows = k_ref.shape[1]
    step = pl.program_id(0)
    own = sc[0]
    low, both, tile, part = back_place(step, own, count)
    query_place = jnp.where(part == 0, own * rows, (count - 1 - own) * rows + half)

    @pl.when(step == 0)
    def start():
        for n in range(2):
            q = q_ref[n].astype(F32)
            ga = ga_ref[n].astype(F32)
            for g in range(group):
                cols = slice(g * half, (g + 1) * half)
                fq[n, cols, :] = (q * mix_ref[base + g : base + g + 1, :]).astype(BF16)
                fa[n, cols, :] = (ga * weight_ref[base + g : base + g + 1, :]).astype(BF16)
        total[...] = jnp.zeros(total.shape, F32)

    @pl.when(jnp.logical_not(both) | (part == 0))
    def clear():
        dk_s[...] = jnp.zeros(dk_s.shape, F32)
        dv_s[...] = jnp.zeros(dv_s.shape, F32)

    set_bias(bias_s, sc, tile * rows, query_place)
    chunk = math.gcd(group, 4)
    chunks = [slice(c * chunk * half, (c + 1) * chunk * half) for c in range(group // chunk)]

    def look(c):
        ahead_l[c % 2] = dot_nt(k_ref[0], fq[part, chunks[c], :])
        ahead_p[c % 2] = dot_nt(v_ref[0], fa[part, chunks[c], :])

    kt_s[...] = k_ref[0].T
    look(0)
    for c, cols in enumerate(chunks):
        if c + 1 < len(chunks):
            look(c + 1)
        logits = ahead_l[c % 2] + jnp.concatenate([bias_s[...]] * (chunk // 2), axis=1)
        prob = jnp.exp2(logits - lse_ref[part, :, cols])
        grad_logits = (prob * (ahead_p[c % 2] - delta_ref[part, :, cols])).astype(BF16)
        dv_s[...] += dot(prob.astype(BF16), fa[part, cols, :])
        dk_s[...] += dot(grad_logits, fq[part, cols, :])
        total[part, :, cols] += dot(kt_s[...], grad_logits)

    @pl.when(jnp.logical_not(both) | (part == 1))
    def leave():
        dk_ref[0] = (dk_s[...] * LN2).astype(BF16)
        dv_ref[0] = dv_s[...].astype(BF16)

    @pl.when(step == count)
    def finish():
        sums = jnp.zeros(r_ref.shape, F32)
        size = width // heads
        for n in range(2):
            q_t = q_ref[n].astype(F32).T
            twice_s[...] = jnp.concatenate([q_t, q_t], axis=1)

            def find(h, rows, cols):
                piece = total[n, rows, cols]
                rows_s[h : h + 1, cols] = jnp.sum(piece * twice_s[rows, :], axis=0, keepdims=True)
                return piece

            mix_all(total, spread_ref, mixed_s, half, find)
            sums += lanes_of(rows_s[...], 0, half)
            dq_ref[n] = ((mixed_s[:, :half] + mixed_s[:, half:]).T * scale).astype(BF16)
        r_ref[...] = sums * scale


def back(
    scalars, base, group, q, grad_att, k, v, lse, delta, mix_rows, weight_rows, spread, heads, scale
):
    count, rows, width = k.shape
    half = q.shape[1]
    span = group * half
    tile = lambda s, sc: (sc[HEAD + back_place(s, sc[0], count)[2]], 0, 0)
    whole = lambda s, sc: (0, 0, 0)
    cut = lambda s, sc: (0, 0, base // group)
    fixed = lambda s, sc: (0, 0)
    once = pl.Buffered(1)
    return pl.pallas_call(
        functools.partial(back_kernel, count, heads, base, group, scale),
        grid_spec=pltpu.PrefetchScalarGridSpec(
            num_scalar_prefetch=1,
            grid=(count + 1,),
            in_specs=[
                pl.BlockSpec((2, half, width), whole, pipeline_mode=once),
                pl.BlockSpec((2, half, width), whole, pipeline_mode=once),
                pl.BlockSpec((1, rows, width), tile),
                pl.BlockSpec((1, rows, width), tile),
                pl.BlockSpec((2, 1, span), cut, pipeline_mode=once),
                pl.BlockSpec((2, 1, span), cut, pipeline_mode=once),
                pl.BlockSpec((heads, width), fixed),
                pl.BlockSpec((heads, width), fixed),
                pl.BlockSpec((heads, span), fixed),
            ],
            out_specs=[
                pl.BlockSpec((1, rows, width), tile),
                pl.BlockSpec((1, rows, width), tile),
                pl.BlockSpec((2, half, width), whole),
                pl.BlockSpec((heads, 128), fixed),
            ],
            scratch_shapes=[
                pltpu.VMEM((2, span, width), BF16),
                pltpu.VMEM((2, span, width), BF16),
                pltpu.VMEM((2, width, span), F32),
                pltpu.VMEM((rows, width), F32),
                pltpu.VMEM((rows, width), F32),
                pltpu.VMEM((rows, 2 * half), F32),
                pltpu.VMEM((width, rows), BF16),
                pltpu.VMEM((width, 2 * half), F32),
                pltpu.VMEM((width, 2 * half), F32),
                pltpu.VMEM((heads, span), F32),
                pltpu.VMEM((2, rows, math.gcd(group, 4) * half), F32),
                pltpu.VMEM((2, rows, math.gcd(group, 4) * half), F32),
            ],
        ),
        out_shape=[
            jax.ShapeDtypeStruct((count, rows, width), BF16),
            jax.ShapeDtypeStruct((count, rows, width), BF16),
            jax.ShapeDtypeStruct((2, half, width), BF16),
            jax.ShapeDtypeStruct((heads, 128), F32),
        ],
        **params(10 * (count + 1) * rows * span * width, 10 * count * rows * width),
    )(scalars, q, grad_att, k, v, lse, delta, mix_rows, weight_rows, spread)


def put(keep_ref, send_ref, place, rows, value):
    @pl.when(place % 2 == 0)
    def kept():
        keep_ref[place // 2, rows, :] = value

    @pl.when(place % 2 == 1)
    def sent():
        send_ref[place // 2, rows, :] = value


def norm_parts(x):
    inverse = lax.rsqrt(jnp.mean(x * x, axis=-1, keepdims=True) + EPS)
    return inverse, x * inverse


def norm_back(inverse, bare, grad, gain):
    gained = grad * gain
    return inverse * (gained - bare * jnp.mean(gained * bare, axis=-1, keepdims=True))


def ffn_kernel(wt_count, sc, att_ref, x_ref, dy_ref, gain_ref, *refs):
    n = wt_count
    halves = (len(refs) - 21) // n - 2
    chunks = 2 * halves
    groups = [refs[i * n : (i + 1) * n] for i in range(halves + 2)]
    wo_shares, win_shares, wout_shares = groups[0], groups[1:-1], groups[-1]
    (
        out_ref, gm_ref, gatt_ref, keep_ref, send_ref, gain_out, sq_ref,
        middle_s, low_s, low_t, feed_s, grad_s, wo_ref, win_buf, wout_buf, leave_out, leave_in, leave_o,
        wo_sem, in_sem, out_sem,
    ) = refs[(halves + 2) * n :]
    j = pl.program_id(0)
    me = sc[5]
    width = x_ref.shape[1]
    per = width // n
    slot = j % 2

    def share_rows(i):
        return pl.ds(pl.multiple_of((me ^ i) * per, per), per)

    def wo_copies():
        return [
            pltpu.make_async_copy(
                wo_shares[i].at[:, pl.ds(width, width)], wo_ref.at[share_rows(i), :], wo_sem.at[i]
            )
            for i in range(n)
        ]

    def in_copies(c):
        return [
            pltpu.make_async_copy(
                win_shares[c // 2][i].at[:, pl.ds(c % 2 * width, width)],
                win_buf.at[c % 2, share_rows(i), :],
                in_sem.at[c % 2, i],
            )
            for i in range(n)
        ]

    def outer_copy(c, i):
        return pltpu.make_async_copy(wout_shares[i], wout_buf.at[c % 2], in_sem.at[c % 2, n])

    def fetch(c):
        for copy in in_copies(c):
            copy.start()
        for i in range(n):
            pl.when((c ^ me) == i)(outer_copy(c, i).start)

    def arrive(c):
        for copy in in_copies(c):
            copy.wait()
        outer_copy(c, 0).wait()

    def leaving(source, place, first, sem):
        target = (keep_ref, send_ref)[place % 2]
        rows = pl.ds(first, source.shape[0])
        return pltpu.make_async_copy(source, target.at[rows, pl.ds(place // 2 * width, width)], sem)

    def depart(source, target, first, sem):
        for place in range(n):
            pl.when((target ^ me) == place)(leaving(source, place, first, sem).start)

    def outgoing(c):
        yield leave_out.at[c % 2], c, 0, out_sem.at[c % 2, n]
        for t in range(n):
            yield leave_in.at[c % 2, pl.ds(t * per, per), :], t, width + c * per, out_sem.at[c % 2, t]

    def gone(c):
        for source, _, first, sem in outgoing(c):
            leaving(source, 0, first, sem).wait()

    @pl.when(j == 0)
    def start():
        for copy in wo_copies():
            copy.start()
        fetch(0)
        for copy in wo_copies():
            copy.wait()

    for c in range(chunks):

        @pl.when(j == c)
        def move():
            if c + 1 < chunks:
                fetch(c + 1)
            if c >= 2:
                gone(c - 2)
            arrive(c)

    @pl.when(j == 0)
    def first():
        branch = dot(att_ref[...], wo_ref[...])
        middle = x_ref[...].astype(F32) + branch
        middle_s[...] = middle
        _, bare = norm_parts(middle)
        low = (bare * gain_ref[...]).astype(BF16)
        low_s[...] = low
        low_t[...] = low.T
        feed_s[...] = jnp.zeros(feed_s.shape, F32)
        grad_s[...] = jnp.zeros(grad_s.shape, F32)
        sq_ref[...] = jnp.zeros(sq_ref.shape, F32)
        sq_ref[1:2, :] = jnp.broadcast_to(jnp.sum(branch * branch).reshape(1, 1), (1, 128))

    dy = dy_ref[...]
    win, wout = win_buf[slot], wout_buf[slot]
    hidden = dot(low_s[...], win)
    grad_active = dot_nt(dy, wout)
    square = hidden * hidden
    inner = jnp.tanh(hidden * (0.7978845608028654 + 0.7978845608028654 * 0.044715 * square))
    half_one = 0.5 + 0.5 * inner
    active = (hidden * half_one).astype(BF16)
    slope = half_one + (0.5 * hidden) * (1.0 - inner * inner) * (
        0.7978845608028654 + 3.0 * 0.7978845608028654 * 0.044715 * square
    )
    grad_hidden = (grad_active * slope).astype(BF16)
    feed_s[...] += dot(active, wout)
    grad_s[...] += dot_nt(grad_hidden, win)
    leave_out[slot] = dot(active.T, dy).astype(BF16)
    leave_in[slot] = dot(low_t[...], grad_hidden).astype(BF16)

    for c in range(chunks):

        @pl.when(j == c)
        def part():
            for copy in outgoing(c):
                depart(*copy)

    @pl.when(j == chunks - 1)
    def finish():
        middle = middle_s[...]
        feed = feed_s[...]
        output = middle + feed
        out_ref[...] = output.astype(BF16)
        sq_ref[0:1, :] = jnp.broadcast_to(jnp.sum(output * output).reshape(1, 1), (1, 128))
        sq_ref[2:3, :] = jnp.broadcast_to(jnp.sum(feed * feed).reshape(1, 1), (1, 128))
        inverse, bare = norm_parts(middle)
        grad = grad_s[...]
        gain_out[...] = jnp.sum(grad * bare, axis=0, keepdims=True)
        grad_middle = dy.astype(F32) + norm_back(inverse, bare, grad, gain_ref[...])
        gm_ref[...] = grad_middle
        low = grad_middle.astype(BF16)
        leave_o[...] = dot(att_ref[...].T, low).astype(BF16)
        rows = width + per * chunks
        for t in range(n):
            depart(leave_o.at[pl.ds(t * per, per), :], t, rows, wo_sem.at[t])
        gatt_ref[...] = dot_nt(low, wo_ref[...]).astype(BF16)
        for c in range(max(chunks - 2, 0), chunks):
            gone(c)
        for t in range(n):
            leaving(leave_o.at[pl.ds(t * per, per), :], 0, rows, wo_sem.at[t]).wait()


def ffn(scalars, wt_count, sq_rows, att, x, dy, gain, wo, wins, wout):
    rows, width = x.shape
    chunks = 2 * len(wins)
    per = width // wt_count
    total = width + per * chunks + per
    fixed = lambda j, sc: (0, 0)
    once = pl.Buffered(1)
    shares = [*wo, *(share for win in wins for share in win), *wout]
    anywhere = pl.BlockSpec(memory_space=pl.ANY)
    square = pltpu.VMEM((width, width), BF16)
    squares = pltpu.VMEM((2, width, width), BF16)
    return pl.pallas_call(
        functools.partial(ffn_kernel, wt_count),
        grid_spec=pltpu.PrefetchScalarGridSpec(
            num_scalar_prefetch=1,
            grid=(chunks,),
            in_specs=[
                pl.BlockSpec((rows, width), fixed, pipeline_mode=once),
                pl.BlockSpec((rows, width), fixed, pipeline_mode=once),
                pl.BlockSpec((rows, width), fixed, pipeline_mode=once),
                pl.BlockSpec((1, width), fixed),
            ]
            + [anywhere] * len(shares),
            out_specs=[
                pl.BlockSpec((rows, width), fixed),
                pl.BlockSpec((rows, width), fixed),
                pl.BlockSpec((rows, width), fixed),
                anywhere,
                anywhere,
                pl.BlockSpec((1, width), fixed),
                pl.BlockSpec((sq_rows, 128), fixed),
            ],
            scratch_shapes=[
                pltpu.VMEM((rows, width), F32),
                pltpu.VMEM((rows, width), BF16),
                pltpu.VMEM((width, rows), BF16),
                pltpu.VMEM((rows, width), F32),
                pltpu.VMEM((rows, width), F32),
                square,
                squares,
                squares,
                squares,
                squares,
                square,
                pltpu.SemaphoreType.DMA((wt_count,)),
                pltpu.SemaphoreType.DMA((2, wt_count + 1)),
                pltpu.SemaphoreType.DMA((2, wt_count + 1)),
            ],
        ),
        out_shape=[
            jax.ShapeDtypeStruct((rows, width), BF16),
            jax.ShapeDtypeStruct((rows, width), F32),
            jax.ShapeDtypeStruct((rows, width), BF16),
            jax.ShapeDtypeStruct((total, wt_count // 2 * width), BF16),
            jax.ShapeDtypeStruct((total, wt_count // 2 * width), BF16),
            jax.ShapeDtypeStruct((1, width), F32),
            jax.ShapeDtypeStruct((sq_rows, 128), F32),
        ],
        **params(10 * chunks * rows * width * width + 6 * rows * width * width, 24 * width * width),
    )(scalars, att, x, dy, gain, *shares)


TAIL_ROWS = 16


def seen_by(sc, count, device):
    return sc[HEAD + count + device] <= jnp.maximum(sc[0], count - 1 - sc[0])


def weight_kernel(
    count, wt_count, sc, dk_ref, dv_ref, dq_ref, x_ref, gain_ref, rl_ref, rw_ref, gain_two_ref, sq_ref,
    keep_ref, send_ref, dwq, dwk, dwv, normed_t,
):
    rows, width = x_ref.shape[1:]
    half = rows // 2
    device = pl.program_id(0)
    me_wt = sc[5]

    @pl.when(device == 0)
    def start():
        dwq[...] = jnp.zeros(dwq.shape, F32)
        dwk[...] = jnp.zeros(dwk.shape, F32)
        dwv[...] = jnp.zeros(dwv.shape, F32)

    @pl.when(seen_by(sc, count, device))
    def seen():
        normed_t[...] = rms_norm(x_ref[0].astype(F32), gain_ref[...]).astype(BF16).T
        dwk[...] += dot(normed_t[...], dk_ref[0])
        dwv[...] += dot(normed_t[...], dv_ref[0])

    def queries(n):
        empty = jnp.zeros((half, width), BF16)
        both = [dq_ref[n], empty] if n == 0 else [empty, dq_ref[n]]
        dwq[...] += dot(normed_t[...], jnp.concatenate(both, axis=0))

    pl.when(device == sc[1])(functools.partial(queries, 0))
    pl.when(device == sc[2])(functools.partial(queries, 1))

    @pl.when(device == count - 1)
    def finish():
        per = width // wt_count

        def pad(value, lanes):
            empty = jnp.zeros((value.shape[0], lanes - value.shape[1]), F32)
            return jnp.concatenate([value, empty], axis=1)

        heads = rw_ref.shape[0]
        each = heads // wt_count
        square = jnp.concatenate([rw_ref[...], jnp.zeros((128 - heads, 128), F32)], axis=0).T
        below = keep_ref.shape[1] - 3 * per - TAIL_ROWS
        assert TAIL_ROWS >= 4 + 2 * each

        def tail(t):
            rows = [
                pad(gain_two_ref[:, t * per : (t + 1) * per], width),
                pad(sq_ref[0:3, :], width),
                pad(rl_ref[t * each : (t + 1) * each, :], width),
                pad(square[t * each : (t + 1) * each, :], width),
                jnp.zeros((TAIL_ROWS - 4 - 2 * each + below, width), F32),
            ]
            return jnp.concatenate(rows, axis=0).astype(BF16)

        for t in range(wt_count):
            cut = slice(t * per, (t + 1) * per)
            for n, total in enumerate((dwq, dwk, dwv)):
                put(keep_ref, send_ref, t ^ me_wt, slice(n * per, (n + 1) * per), total[cut, :].astype(BF16))
            put(keep_ref, send_ref, t ^ me_wt, slice(3 * per, keep_ref.shape[1]), tail(t))


def weight_grads(scalars, wt_count, total, dk, dv, dq, xg, gain, rl, rw, gain_two, sq):
    count, rows, width = dk.shape
    place = lambda j, sc: (j, 0, 0)
    fixed = lambda j, sc: (0, 0)
    whole = lambda j, sc: (0, 0, 0)
    once = pl.Buffered(1)
    share = jax.ShapeDtypeStruct((wt_count // 2, total, width), BF16)
    return pl.pallas_call(
        functools.partial(weight_kernel, count, wt_count),
        grid_spec=pltpu.PrefetchScalarGridSpec(
            num_scalar_prefetch=1,
            grid=(count,),
            in_specs=[
                pl.BlockSpec((1, rows, width), place),
                pl.BlockSpec((1, rows, width), place),
                pl.BlockSpec((2, rows // 2, width), whole, pipeline_mode=once),
                pl.BlockSpec((1, rows, width), place),
                pl.BlockSpec((1, width), fixed),
                pl.BlockSpec(rl.shape, fixed),
                pl.BlockSpec(rw.shape, fixed),
                pl.BlockSpec((1, width), fixed),
                pl.BlockSpec(sq.shape, fixed),
            ],
            out_specs=[
                pl.BlockSpec((wt_count // 2, total, width), whole),
                pl.BlockSpec((wt_count // 2, total, width), whole),
            ],
            scratch_shapes=[pltpu.VMEM((width, width), F32)] * 3 + [pltpu.VMEM((width, rows), BF16)],
        ),
        out_shape=[share, share],
        **params(4 * count * rows * width * width, 10 * count * rows * width),
    )(scalars, dk, dv, dq, xg, gain, rl, rw, gain_two, sq)


def token_kernel(
    count, first, sc, dk_ref, dv_ref, dq_ref, x_ref, wq_ref, mat_ref, gain_ref, gm_ref, part_ref
):
    rows, width = x_ref.shape[1:]
    half = rows // 2
    device = sc[HEAD + 2 * count + first + pl.program_id(0)]
    valid = seen_by(sc, count, device)

    @pl.when(valid)
    def seen():
        grad = dot_nt(dk_ref[0], mat_ref[:, :width]) + dot_nt(dv_ref[0], mat_ref[:, width:])
        inverse, bare = norm_parts(x_ref[0].astype(F32))
        part_ref[0] = norm_back(inverse, bare, grad, gain_ref[...]).astype(BF16)

    @pl.when(jnp.logical_not(valid))
    def unseen():
        part_ref[0] = jnp.zeros(part_ref.shape[1:], BF16)

    def queries(n):
        mine = slice(n * half, (n + 1) * half)
        grad = dot_nt(dq_ref[n], wq_ref[...])
        inverse, bare = norm_parts(x_ref[0, mine, :].astype(F32))
        found = norm_back(inverse, bare, grad, gain_ref[...]) + gm_ref[n]
        part_ref[0, mine, :] = (part_ref[0, mine, :].astype(F32) + found).astype(BF16)

    pl.when(device == sc[1])(functools.partial(queries, 0))
    pl.when(device == sc[2])(functools.partial(queries, 1))


def token_parts(scalars, first, batch, dk, dv, dq, xg, wq, mat, gain, gm):
    count, rows, width = xg.shape
    place = lambda j, sc: (sc[HEAD + 2 * count + first + j], 0, 0)
    fixed = lambda j, sc: (0, 0)
    whole = lambda j, sc: (0, 0, 0)
    once = pl.Buffered(1)
    return pl.pallas_call(
        functools.partial(token_kernel, count, first),
        grid_spec=pltpu.PrefetchScalarGridSpec(
            num_scalar_prefetch=1,
            grid=(batch,),
            in_specs=[
                pl.BlockSpec((1, rows, width), place),
                pl.BlockSpec((1, rows, width), place),
                pl.BlockSpec((2, rows // 2, width), whole, pipeline_mode=once),
                pl.BlockSpec((1, rows, width), place),
                pl.BlockSpec((width, width), fixed, pipeline_mode=once),
                pl.BlockSpec((width, 2 * width), fixed, pipeline_mode=once),
                pl.BlockSpec((1, width), fixed),
                pl.BlockSpec((2, rows // 2, width), whole, pipeline_mode=once),
            ],
            out_specs=pl.BlockSpec((1, rows, width), lambda j, sc: (j, 0, 0)),
        ),
        out_shape=jax.ShapeDtypeStruct((batch, rows, width), BF16),
        **params(4 * batch * rows * width * width, 8 * batch * rows * width),
    )(scalars, dk, dv, dq, xg, wq, mat, gain, gm)


def finish_kernel(entries, heads, sc, *refs):
    count = len(refs) - 13
    pieces, (wq_ref, wk_ref, wv_ref, own_ref), outs, whole = refs[:count], refs[count : count + 4], refs[-9:-1], refs[-1]
    dq_ref, dk_ref, dv_ref, gain_ref, two_ref, logit_ref, weight_ref, rms_ref = outs
    gather_rows(sc, pieces, whole)
    rows = wq_ref.shape[0]
    gain = jnp.zeros((rows, 1), F32)
    for n, (out, w) in enumerate(((dq_ref, wq_ref), (dk_ref, wk_ref), (dv_ref, wv_ref))):
        found = whole[n * rows : (n + 1) * rows, :]
        out[...] = found
        gain += jnp.sum(found * w[...].astype(F32), axis=1, keepdims=True)
    gain_ref[...] = jnp.broadcast_to(gain, (rows, 128)).T[0:1, :] / own_ref[...].astype(F32)
    tail = whole[3 * rows : 3 * rows + TAIL_ROWS, :]
    each = logit_ref.shape[0]
    two_ref[...] = tail[0:1, :rows]
    squares = jnp.concatenate([tail[n : n + 1, 0:1] for n in range(1, 4)], axis=1)
    rms_ref[...] = jnp.sqrt(squares * (1.0 / entries))
    logit_ref[...] = tail[4 : 4 + each, :heads]
    weight_ref[...] = tail[4 + each : 4 + 2 * each, :heads]


def finish_grads(places, pieces, wq, wk, wv, gain, entries, heads, each):
    count = len(pieces)
    rows, width = wq.shape
    ins = [*pieces, wq, wk, wv, gain]
    shapes = [(rows, width)] * 3 + [(1, rows), (1, rows), (each, heads), (each, heads), (1, 3)]
    fixed = lambda i, sc: (0, 0)
    return pl.pallas_call(
        functools.partial(finish_kernel, entries, heads),
        grid_spec=pltpu.PrefetchScalarGridSpec(
            num_scalar_prefetch=1,
            grid=(1,),
            in_specs=[pl.BlockSpec(v.shape, fixed) for v in ins],
            out_specs=[pl.BlockSpec(v, fixed) for v in shapes],
            scratch_shapes=[pltpu.VMEM((count * pieces[0].shape[0], width), F32)],
        ),
        out_shape=[jax.ShapeDtypeStruct(v, F32) for v in shapes],
        **params(0, 12 * rows * width),
    )(places, *ins)


def gather_rows(sc, pieces, whole):
    per = pieces[0].shape[0]
    for n, piece in enumerate(pieces):
        whole[pl.ds(pl.multiple_of(sc[n] * per, 8), per), :] = piece[...].astype(F32)


def unpack_kernel(sc, *refs):
    pieces, (out_ref, in_ref, o_ref, whole) = refs[:-4], refs[-4:]
    gather_rows(sc, pieces, whole)
    rows, width = out_ref.shape
    per = o_ref.shape[0]
    out_ref[...] = whole[:rows, :]
    chunks = in_ref.shape[1] // width
    for n in range(chunks):
        in_ref[:, n * width : (n + 1) * width] = whole[rows + n * per : rows + (n + 1) * per, :]
    o_ref[...] = whole[rows + chunks * per :, :]


def unpack(places, pieces, shapes):
    total = len(pieces) * pieces[0].shape[0]
    width = pieces[0].shape[1]
    fixed = lambda i, sc: (0, 0)
    return pl.pallas_call(
        unpack_kernel,
        grid_spec=pltpu.PrefetchScalarGridSpec(
            num_scalar_prefetch=1,
            grid=(1,),
            in_specs=[pl.BlockSpec(v.shape, fixed) for v in pieces],
            out_specs=[pl.BlockSpec(v, fixed) for v in shapes],
            scratch_shapes=[pltpu.VMEM((total, width), F32)],
        ),
        out_shape=[jax.ShapeDtypeStruct(shape, F32) for shape in shapes],
        **params(0, 6 * total * width),
    )(places, *pieces)


def swaps(size, distance):
    return [(i, i ^ distance) for i in range(size)]


def ring_order(count):
    return [2 * p if p < count // 2 else 2 * (count - 1 - p) + 1 for p in range(count)]


def ring(count, step):
    order = ring_order(count)
    return [(order[p], order[(p + step) % count]) for p in range(count)]


def ring_places(count, me, offsets):
    place = jnp.where((me & 1) == 0, me >> 1, count - 1 - (me >> 1))
    p = (place + jnp.array(offsets, jnp.int32)) & (count - 1)
    return jnp.where(p < count // 2, 2 * p, 2 * (count - 1 - p) + 1)


def ring_both(up, down):
    count = lax.axis_size("ctx")
    return lax.ppermute(up, "ctx", ring(count, 1)), lax.ppermute(down, "ctx", ring(count, -1))


def tie(*values):
    return lax.optimization_barrier(values)


def gather_all(value, stages, work):
    count = lax.axis_size("ctx")
    size = lax.axis_size("wt")
    half = value.shape[0] // 2
    rounds = [[(0, value)]]
    up = down = value
    shares, crossed = [], []
    for k in range(1, count // 2 + 1):
        last = k == count // 2
        up, down = ring_both(up[:half], down[half:]) if last else ring_both(up, down)
        tied = []
        if 2 <= k <= len(stages) + 1:
            tied.append(lax.ppermute(stages[k - 2], "wt", swaps(size, 1)))
            tied.append(lax.ppermute(crossed[k - 2], "wt", swaps(size, 1)))
        if k <= len(stages):
            crossed.append(lax.ppermute(stages[k - 1], "wt", swaps(size, 2)))
            if not last:
                tied.append(crossed.pop())
        done = work(rounds, shares) if k >= 3 else []
        up, down, done, *tied = tie(up, down, done, *tied)
        if k >= 3:
            work(rounds, shares, done)
        if k <= len(stages) and not last:
            crossed.append(tied.pop())
        if tied:
            shares.append([stages[k - 2], tied[0], crossed[k - 2], tied[1]])
        rounds.append([(count // 2, jnp.concatenate([up, down], axis=0))] if last else [(-k, up), (k, down)])
    return rounds, shares, crossed


def add(*values):
    return sum(v.astype(F32) for v in values).astype(BF16)


def far_start(far):
    half = far.shape[0] // 2
    up, down = ring_both(far[:half], far[half:])
    return up, down


def far_end(up, down):
    empty = jnp.zeros(up.shape, BF16)
    return jnp.concatenate([up, empty], axis=0), jnp.concatenate([empty, down], axis=0)


class Spreading:
    def __init__(self, piece, count):
        self.count, self.last = count, count // 2
        self.up = self.down = piece
        self.pieces = {0: piece}
        self.step = 0

    @property
    def done(self):
        return self.step == self.last

    def start(self):
        if self.step < self.last - 1:
            return ring_both(self.up, self.down)
        half = self.up.shape[0] // 2
        return ring_both(self.up[:half], self.down[half:])

    def finish(self, up, down):
        self.step += 1
        if self.done:
            self.pieces[self.last] = jnp.concatenate([up, down], axis=0)
        else:
            self.pieces[self.count - self.step], self.pieces[self.step] = up, down
        self.up, self.down = up, down

    def ordered(self):
        return [self.pieces[n] for n in range(self.count)]


class Turning:
    def __init__(self, blocks, me):
        self.count, self.last = blocks.shape[0], blocks.shape[0] // 2
        self.blocks, self.me = blocks, me
        self.step = 0
        self.spread = None

    @property
    def done(self):
        return self.spread is not None and self.spread.done

    def at(self, offset):
        place = ring_places(self.count, self.me, [offset])[0]
        return lax.dynamic_index_in_dim(self.blocks, place, 0, keepdims=False)

    def start(self):
        step, last = self.step, self.last
        if self.spread is not None:
            return self.spread.start()
        if step == 0:
            return far_start(self.at(last))
        return ring_both(add(self.up, self.at(last - step)), add(self.down, self.at(step - last)))

    def finish(self, up, down):
        if self.spread is not None:
            return self.spread.finish(up, down)
        if self.step == 0:
            up, down = far_end(up, down)
        elif self.step == self.last - 1:
            self.spread = Spreading(add(up, down, self.at(0)), self.count)
        self.up, self.down = up, down
        self.step += 1


def shards(
    residual_in,
    cotangent,
    block_order,
    doc_starts,
    gain_attn,
    w_query,
    w_key,
    w_value,
    mix_logit,
    mix_weight,
    w_output,
    gain_ffn,
    w_in,
    w_out,
):
    rows, width = residual_in.shape[1:]
    half = rows // 2
    heads = mix_logit.shape[1]
    size = width // heads
    scale = size ** (-0.5)
    count = lax.axis_size("ctx")
    me = lax.axis_index("ctx").astype(jnp.int32)
    wt_count = lax.axis_size("wt")
    starts = doc_starts[0]

    per = gain_attn.shape[0]
    across = lambda v, n: jnp.pad(v, ((0, n - v.shape[0]), (0, 2 * width - v.shape[1])))
    gains = jnp.concatenate([gain_attn, gain_ffn])[None, :]
    mixes_at = 8
    small = jnp.concatenate(
        [across(gains, mixes_at), across(jnp.concatenate([mix_logit, mix_weight], axis=1), mixes_at)], axis=0
    )
    kv_own = jnp.concatenate([jnp.concatenate([w_key, w_value], axis=1), small], axis=0)
    x_own = residual_in[0]
    stages = [kv_own, jnp.concatenate([w_query, w_output], axis=1)]
    stages += [w_in[:, n : n + 2 * width] for n in range(0, w_in.shape[1], 2 * width)]
    order = block_order.astype(jnp.int32)
    devices = jnp.arange(count, dtype=jnp.int32)
    by_block = jnp.sum(jnp.where(order[None, :] == devices[:, None], devices[None, :], 0), axis=1)
    own = order[me]
    partner = by_block[count - 1 - own]
    offsets = [0] + [o for k in range(1, count // 2) for o in (-k, k)] + [count // 2]
    relative = ring_places(count, me, offsets).astype(jnp.int32)
    wt_me = lax.axis_index("wt").astype(jnp.int32)
    scalars = jnp.concatenate(
        [
            jnp.stack([own, me, partner, starts[1], starts[2], wt_me]),
            by_block,
            order,
            relative,
        ]
    ).astype(jnp.int32)

    state = {"first": 0, "found": None, "seen": 0}

    def read_small(shares):
        small = jnp.stack([share[per:, : 2 * per] for share in shares[0]]).astype(F32)
        small = jnp.concatenate(
            [lax.dynamic_slice_in_dim(small, wt_me ^ n, 1, 0) for n in range(wt_count)], axis=0
        )
        gain_one = small[:, 0, :per].reshape(1, width)
        gain_two = small[:, 0, per:].reshape(1, width)
        mixes = small[:, mixes_at : mixes_at + mix_logit.shape[0], : 2 * heads].reshape(heads, 2 * heads)
        logit_mix, weight_mix = mixes[:, :heads], mixes[:, heads:]
        return gain_one, gain_two, logit_mix, weight_mix

    def work(rounds, shares, done=None):
        if done is not None:
            if done:
                *state["found"], state["mat"] = done
            return []
        if not state["seen"]:
            state["small"] = read_small(shares)
            state["mat"] = shares[0]
        batch = [piece for pieces in rounds[state["seen"] : -1] for _, piece in pieces]
        state["seen"] = len(rounds) - 1
        return project_batch(batch)

    def project_batch(batch):
        results = project(
            scalars, count, state["first"], batch, state["small"][0], state["mat"], state["found"]
        )
        state["first"] += len(batch)
        return [*results, state["mat"]][:4]

    rounds, shares, crossed = gather_all(x_own, stages, work)
    gain_one, gain_two, logit_mix, weight_mix = state["small"]
    qo_shares = shares[1]

    mix_by_g = jnp.repeat(logit_mix.T, size, axis=1)
    weight_by_g = jnp.repeat(weight_mix, size, axis=1)
    mix_rows = mix_by_g * (scale * LOG2E)
    spread = jnp.repeat(weight_mix.T, half, axis=1)
    logit_spread = jnp.repeat(logit_mix, half, axis=1)

    batch = [piece for pieces in rounds[state["seen"] :] for _, piece in pieces]
    k, v, xg, kv_mat = project_batch(batch)
    xg, *crossed[len(shares) :] = tie(xg, *crossed[len(shares) :])
    q, x_low, query_mat = queries(scalars, xg, gain_one, qo_shares)
    x_low = x_low.reshape(rows, width)
    for n in range(len(shares), len(stages)):
        near = lax.ppermute(stages[n], "wt", swaps(wt_count, 1))
        both = lax.ppermute(crossed[n], "wt", swaps(wt_count, 1))
        q, near, both = lax.optimization_barrier((q, near, both))
        shares.append([stages[n], near, crossed[n], both])
    w_out, q = tie(w_out, q)
    far_out = lax.ppermute(w_out, "wt", swaps(wt_count, 2))
    near_out = lax.ppermute(w_out, "wt", swaps(wt_count, 1))

    def exchange(second):
        every = lax.all_gather(second, "ctx", axis=0)
        return lax.dynamic_index_in_dim(every, partner, 0, keepdims=False)

    dy_second, _ = lax.optimization_barrier((cotangent[0, half:], rounds[-1][0][1]))
    dy_low = jnp.concatenate([cotangent[0, :half], exchange(dy_second)], axis=0)

    attended, t, lse = attend(scalars, q, k, v, mix_rows, spread, heads)
    far_out, attended = tie(far_out, attended)
    out_shares = [w_out, near_out, far_out, lax.ppermute(far_out, "wt", swaps(wt_count, 1))]
    out_low, grad_middle, grad_att, keep, send, grad_gain_two, squares = ffn(
        scalars, wt_count, heads, attended.reshape(rows, width), x_low, dy_low, gain_two,
        qo_shares, shares[2:], out_shares,
    )
    grad_att = grad_att.reshape(2, half, width)
    grad_middle = grad_middle.reshape(2, half, width)

    got = lax.ppermute(send, "wt", swaps(wt_count, 1))
    r_weight, delta = deltas(grad_att, t, spread, heads)
    summed = add(keep, got)
    leaving = Spreading(out_low[half:], count)
    summed, delta, *moved = tie(summed, delta, *leaving.start())
    leaving.finish(*moved)
    summed = lax.psum_scatter(summed, "ctx", scatter_dimension=0, tiled=True)

    moved = leaving.start()
    dk, dv, dq, r_logit = back(
        scalars, 0, heads, q, grad_att, k, v, lse, delta, mix_rows, weight_by_g,
        logit_spread, heads, scale,
    )

    def parts(first, batch, dk):
        return token_parts(
            scalars, first, batch, dk, dv, dq, xg, query_mat, kv_mat, gain_one, grad_middle
        )

    last = count // 2
    far = parts(count - 1, 1, dk)
    dk, far, *moved = tie(dk, far, *moved)
    leaving.finish(*moved)
    up, down = far_start(far[0])
    moved = leaving.start()
    total = -(-(3 * per + TAIL_ROWS) // (8 * count)) * 8 * count
    keep, send = weight_grads(
        scalars, wt_count, total, dk, dv, dq, xg, gain_one, r_logit, r_weight, grad_gain_two, squares
    )
    up, down, keep, send, summed, dk, *moved = tie(up, down, keep, send, summed, dk, *moved)
    leaving.finish(*moved)
    up, down = far_end(up, down)
    near = lax.ppermute(send, "wt", swaps(wt_count, 1))
    ffn_far = lax.ppermute(summed[:, width:], "wt", swaps(wt_count, 2))
    pair = parts(2 * (last - 1) - 1, 2, dk)
    near, ffn_far, pair, *moved = tie(near, ffn_far, pair, *leaving.start())
    leaving.finish(*moved)
    over = lax.ppermute(add(keep[1], near[1]), "wt", swaps(wt_count, 2))
    spread = Spreading(add(summed[:, :width], ffn_far), count)

    turn = None
    for k in range(last - 1, 0, -1):
        up, down, dk = tie(add(up, pair[1]), add(down, pair[0]), dk)
        up, down = ring_both(up, down)
        streams = [s for s in (spread, leaving) if not s.done]
        moved = [stream.start() for stream in streams]
        after = parts(2 * (k - 1) - 1, 2, dk) if k > 1 else parts(0, 1, dk)
        if turn is None:
            up, down, pair, moved, over = tie(up, down, after, moved, over)
            turn = Turning(add(keep[0], near[0], over).reshape(count, -1, width), me)
        else:
            for _ in range(2):
                if not turn.done:
                    after, *both = tie(after, *turn.start())
                    turn.finish(*both)
            both = [] if turn.done else turn.start()
            up, down, pair, moved, both = tie(up, down, after, moved, both)
            if both:
                turn.finish(*both)
        for stream, both in zip(streams, moved):
            stream.finish(*both)
    input_grad = add(up, down, pair[0])
    while not leaving.done:
        leaving.finish(*tie(*leaving.start()))
    order_places = jnp.where((partner & 1) == 0, partner >> 1, count - 1 - (partner >> 1))
    own_place = jnp.where((me & 1) == 0, me >> 1, count - 1 - (me >> 1))
    offset = (order_places - own_place) & (count - 1)
    second = leaving.pieces[1]
    for n in range(2, count):
        second = jnp.where(offset == n, leaving.pieces[n], second)
    output_own = jnp.concatenate([out_low[:half], second], axis=0)
    places = ring_places(count, me, list(range(count))).astype(jnp.int32)
    ffn_grads = []

    def unpacked():
        return unpack(places, spread.ordered(), (w_out.shape, w_in.shape, w_output.shape))

    while not turn.done:
        moving = [] if spread.done else list(spread.start())
        if spread.done and not ffn_grads:
            ffn_grads = unpacked()
            one, two, ffn_grads = tie(*turn.start(), ffn_grads)
        else:
            one, two, *moving = tie(*turn.start(), *moving)
        turn.finish(one, two)
        if moving:
            spread.finish(*moving)
    while not spread.done:
        spread.finish(*tie(*spread.start()))
    ffn_grads = ffn_grads or unpacked()
    grad_out, grad_in, grad_o = ffn_grads
    entries = float(rows * width) * (count * wt_count)
    grad_q, grad_k, grad_v, gain_grad, gain_two_grad, logit_grad, weight_grad, rms = finish_grads(
        places, turn.spread.ordered(), w_query, w_key, w_value, gain_attn[None, :], entries, heads, heads // wt_count
    )
    return (
        output_own[None],
        input_grad[None],
        rms.reshape(3),
        gain_grad.reshape(per),
        grad_q,
        grad_k,
        grad_v,
        logit_grad,
        weight_grad,
        grad_o,
        gain_two_grad.reshape(per),
        grad_in,
        grad_out,
    )


def solution(mesh):
    tokens = P("wt", "ctx", None)
    matrix = P("wt", None)
    vector = P("wt")
    return jax.shard_map(
        shards,
        mesh=mesh,
        in_specs=(tokens, tokens, P(), matrix, vector)
        + (matrix,) * 6
        + (vector, matrix, matrix),
        out_specs=(tokens, tokens, P(), vector) + (matrix,) * 6 + (vector, matrix, matrix),
        check_vma=False,
    )
```
